128 devices in a mesh: rep: 4 (over y), shard: 32 (over x, z, core).
Axes of the slice: x: 4, y: 4, z: 4, core: 2. Of those that a mesh axis runs over, the one named last changes fastest.
Arguments:
- embed_table: bfloat16 [262144, 128], P('shard'), may hold values from -6 to 6
- row_ids: int32 [128, 8192], P(('rep', 'shard')), may hold values from 0 to 1023
- row_owner: int32 [128, 8192, 1], P(('rep', 'shard')), may hold values from 0 to 31; in each aligned block of 8192 rows (0 to 8191, 8192 to 16383, ..., all dimensions but the last counted through in order) at most 512 rows name the same one
- lengths: int32 [128, 1024], P(('rep', 'shard')), may hold values from 1 to 200, 8192 in all within a row
- feature_slot: int32 [32, 8], replicated, may hold values from 0 to 7, each once within a row
- labels: int32 [16384], P(('rep', 'shard')), may hold values 0 or 1
- norm_gain: float32 [1024], replicated, may hold values from 0.1 to 1.9
- cross_weight: bfloat16 [3, 1024, 1024], replicated, may hold values from -0.1875 to 0.1875
- cross_bias: float32 [3, 1024], replicated, may hold values from -3 to 3
- deep_weight: bfloat16 [3, 1024, 1024], replicated, may hold values from -0.1875 to 0.1875
- deep_bias: float32 [3, 1024], replicated, may hold values from -3 to 3
- out_weight: float32 [1024], replicated, may hold values from -0.1875 to 0.1875
Outputs:
- row_grad: float32 [262144, 128], P('shard')
- first_grad: float32 [1024, 1024], replicated
- logits: float32 [16384], P(('rep', 'shard'))
The draws below stay inside these ranges and needn't reach their ends.
Inputs may be any that keep to these rules, and one draw needn't show every extreme that they name: `row_owner`: among one device's ids, at most 512 have the same owner, and in every draw some device sends exactly 512 to some owner. Each device's 1024 lengths sum to 8192; the largest is 200. `feature_slot`: each row holds each of 0 to 7 once.
All inputs are finite; a program needn't handle non-finite values. No bound on the sum of `labels` on one device may be relied on, other than what follows from the above.
Results may differ from the reference program's by a relative error of at most 0.035.
Values may be sent and summed in bfloat16 or wider, within the bound.
No kernel may reach another device: no remote copies, remote signals or barrier semaphores. Data moves between devices by JAX's collectives and lax.ppermute only.
A program may use at most 128 MiB of HBM per device.

```python
import math
import jax
import jax.numpy as jnp
import numpy as np
from jax import lax

EMB = 128
F = 8
CROSS = 3
DEEP = 3
MAXLEN = 200
ROWS_DEV = 8192
D = 1024
BAGS_DEV = 1024
IDS_DEV = 8192
CAP = 512
VOC = 1024
DEVS = 128
SAMPLES = 16384
TABLE_ROWS = 262144
N_SHARD = 32


def place_ends(drawn, stream_key, smallest, high):
    spot = [jax.random.randint(jax.random.fold_in(stream_key, axis), (), 0, length) for axis, length in enumerate(drawn.shape)]
    widest = drawn.shape.index(max(drawn.shape))
    beside = spot[:widest] + [(spot[widest] + 1) % drawn.shape[widest]] + spot[widest + 1:]
    return drawn.at[tuple(spot)].set(smallest).at[tuple(beside)].set(high)


def block_scale(stream_key, extent, cuts, least, top_value):
    loudness, own = 1.0, jax.random.fold_in(stream_key, 6)
    for dim, shards_of in cuts:
        heights = jnp.exp(jax.random.uniform(jax.random.fold_in(own, dim), (shards_of,), jnp.float32, least / len(cuts), top_value / len(cuts)))
        loudness = loudness * jnp.repeat(heights, extent[dim] // shards_of).reshape([-1 if axis == dim else 1 for axis in range(len(extent))])
    return loudness


def rank_table(number_of, lean):
    portions = [(1 << 20) // math.isqrt(grade ** lean) + 1 for grade in range(1, number_of + 1)]
    deviation = 1 + sum(portions) // (1 << 30)
    return np.cumsum(np.array([max(1, weight // deviation) for weight in portions]))


def ranked_ids(own_key, dims, count, slope):
    listing = rank_table(count, slope)
    pick = jax.random.randint(jax.random.fold_in(own_key, 1), dims, 0, int(listing[count - 1]))
    rank = jnp.searchsorted(jnp.asarray(listing, jnp.int32), pick, side="right")
    return jax.random.permutation(jax.random.fold_in(own_key, 2), count)[rank].astype(jnp.int32)


def profile(count, total, bound, skew):
    weights = [(1 << 20) // math.isqrt(rank ** skew) + 1 for rank in range(2, count + 1)]
    spare, counts = total - bound - (count - 1), [1] * (count - 1)
    while spare > 0:
        candidates = [i for i in range(count - 1) if counts[i] < bound]
        mass, budget = sum([weights[i] for i in candidates]), spare
        for i in candidates:
            addition = min(bound - counts[i], max(1, budget * weights[i] // mass), spare)
            counts[i] = counts[i] + addition
            spare = spare - addition
    return np.array([bound] + counts)


def uneven(rng, number_of, total, most, skew):
    if number_of == 2:
        one = jax.random.randint(rng, (), max(1, total - most), min(most, total - 1) + 1)
        return jnp.stack([one, total - one])
    tallies = jnp.asarray(profile(number_of, total, most, skew), jnp.int32)
    twos = (number_of - 1) // 2
    giver, sink = tallies[1:1 + 2 * twos:2], tallies[2:2 + 2 * twos:2]
    room = jnp.minimum(giver - 1, most - sink)
    moved = jax.random.randint(jax.random.fold_in(rng, 1), (twos,), 0, 1 << 20) % (room + 1)
    tallies = tallies.at[1:1 + 2 * twos:2].set(giver - moved).at[2:2 + 2 * twos:2].set(sink + moved)
    return tallies[jax.random.permutation(jax.random.fold_in(rng, 2), number_of)]


def assign_block(rng, own, number, rows, count, top, most, lean):
    order = jax.random.permutation(rng, count)
    crowded, usual = load_shares(count, rows * top, most, lean, True), load_shares(count, rows * top, most, lean, False)
    places = jnp.arange(count)

    def named(sizes, turn):
        used = int((sizes > 0).sum())
        fixed = max(1, used // 4)
        passed = fixed + (places - fixed + turn * (used - fixed)) % max(1, count - fixed)
        return jnp.zeros((count,), jnp.int32).at[order[jnp.where(places < fixed, places, passed)]].set(jnp.asarray(sizes, jnp.int32))

    sizes = jnp.where(number % 4 == 0, named(crowded, number // 4), named(usual, number - number // 4 - 1))
    mixed = jax.random.permutation(jax.random.fold_in(own, 3), count)
    source_of, receiver = mixed[0:count // 2 * 2:2], mixed[1:count // 2 * 2:2]
    margin = jnp.minimum(sizes[source_of] - 1, most - sizes[receiver]) // 2
    margin = jnp.where((source_of == order[0]) | (receiver == order[0]) | (sizes[receiver] == 0), 0, jnp.maximum(margin, 0))
    passed = jax.random.randint(jax.random.fold_in(own, 4), (count // 2,), 0, 1 << 20) % (margin + 1)
    sizes = sizes.at[source_of].add(-passed).at[receiver].add(passed)
    members = jnp.searchsorted(jnp.cumsum(sizes), jnp.arange(rows * top), side="right").astype(jnp.int32)
    table = members.reshape(top, rows).T
    table = table[jax.random.permutation(jax.random.fold_in(own, 1), rows)]
    turn = jax.random.randint(jax.random.fold_in(own, 2), (rows, 1), 0, top)
    return jnp.take_along_axis(table, (jnp.arange(top)[None, :] + turn) % top, axis=1)


def load_shares(count, total, most, slope, full):
    portions = [(1 << 20) // math.isqrt(grade ** slope) + 1 for grade in range(1, count + 1)]
    largest = most if full else min(most, max(-(-total // count), total * portions[0] // sum(portions)))
    least = 1 if total - largest >= count - 1 else 0
    counts, rest = [largest] + [least] * (count - 1), total - largest - least * (count - 1)
    while rest > 0:
        candidates = [i for i in range(1, count) if counts[i] < largest] or [i for i in range(1, count) if counts[i] < most]
        mass, remaining = sum([portions[i] for i in candidates]), rest
        for i in candidates:
            addition = min(most - counts[i], max(1, remaining * portions[i] // mass), rest)
            counts[i] = counts[i] + addition
            rest = rest - addition
    return np.array(counts)


def noise(stream_key, dims, deviation, bound, split=(), kind=jnp.bfloat16):
    entries = deviation * jax.random.normal(stream_key, dims, jnp.float32)
    if split:
        entries = entries * block_scale(stream_key, dims, split, -0.22, 0.18)
    return jnp.clip(entries, -bound, bound).astype(kind)


def setup_inputs(seed: int = 0) -> dict:
    splits = jax.random.split(jax.random.key(seed), 13)
    embed_table = noise(splits[0], (TABLE_ROWS, EMB), 1.0, 6.0, ((0, 32),))
    row_ids = place_ends(ranked_ids(splits[1], (DEVS, IDS_DEV), VOC, 1), jax.random.fold_in(splits[1], 3), 0, VOC - 1).astype(jnp.int32)
    row_owner_keys = jax.random.split(jax.random.fold_in(splits[2], 1), DEVS * IDS_DEV // IDS_DEV)
    row_owner_turns = jax.random.permutation(jax.random.fold_in(splits[2], 3), DEVS * IDS_DEV // IDS_DEV)
    row_owner = jax.vmap(lambda own, number: assign_block(jax.random.fold_in(splits[2], 2), own, number, IDS_DEV, N_SHARD, 1, CAP, 2))(row_owner_keys, row_owner_turns).reshape((DEVS, IDS_DEV, 1))
    lengths = jax.vmap(lambda own: uneven(own, BAGS_DEV, IDS_DEV, MAXLEN, 2))(jax.random.split(splits[3], DEVS)).reshape((DEVS, BAGS_DEV)).astype(jnp.int32)
    feature_slot = jax.vmap(lambda own: jax.random.permutation(own, F))(jax.random.split(splits[4], N_SHARD)).reshape((N_SHARD, F)).astype(jnp.int32)
    labels = place_ends((jax.random.randint(splits[5], (SAMPLES,), 0, 2) < 1).astype(jnp.int32), jax.random.fold_in(splits[5], 1), 0, 1)
    norm_gain = jnp.clip(1.0 + 0.18 * jax.random.normal(splits[6], (D,), jnp.float32), 0.1, 1.9)
    cross_weight = noise(splits[7], (CROSS, D, D), D ** -0.5, 0.1875)
    cross_bias = noise(splits[8], (CROSS, D), 0.5, 3.0, (), jnp.float32)
    deep_weight = noise(splits[9], (DEEP, D, D), D ** -0.5, 0.1875)
    deep_bias = noise(splits[10], (DEEP, D), 0.5, 3.0, (), jnp.float32)
    out_weight = noise(splits[11], (D,), D ** -0.5, 0.1875, (), jnp.float32)
    return dict(embed_table=embed_table, row_ids=row_ids, row_owner=row_owner, lengths=lengths, feature_slot=feature_slot, labels=labels, norm_gain=norm_gain, cross_weight=cross_weight, cross_bias=cross_bias, deep_weight=deep_weight, deep_bias=deep_bias, out_weight=out_weight)


def times_transposed(left, right):
    return lax.dot_general(left, right, (((1,), (1,)), ((), ())), preferred_element_type=jnp.float32)

def forward_backward(pooled, labels, norm_gain, cross_weight, cross_bias, deep_weight, deep_bias, out_weight):
    mean_square = lax.optimization_barrier(jnp.mean(pooled * pooled, axis=1, keepdims=True))
    inverse = lax.rsqrt(mean_square + 1e-06)
    start_row = (pooled * inverse * norm_gain).astype(jnp.bfloat16)
    start_float = start_row.astype(jnp.float32)
    current = start_row
    cross_terms = []
    for layer_number in range(cross_weight.shape[0]):
        product = jnp.dot(current, cross_weight[layer_number], preferred_element_type=jnp.float32) + cross_bias[layer_number]
        cross_terms.append(product)
        current = (start_float * product + current.astype(jnp.float32)).astype(jnp.bfloat16)
    deep_terms = []
    for layer_number in range(deep_weight.shape[0]):
        product = jnp.dot(current, deep_weight[layer_number], preferred_element_type=jnp.float32) + deep_bias[layer_number]
        deep_terms.append(product)
        current = (product * jax.nn.sigmoid(product)).astype(jnp.bfloat16)
    logits = lax.optimization_barrier(jnp.sum(current.astype(jnp.float32) * out_weight, axis=1))
    error = jax.nn.sigmoid(logits) - labels.astype(jnp.float32)
    grad = error[:, None] * out_weight[None, :]
    for layer_number in reversed(range(deep_weight.shape[0])):
        product = deep_terms[layer_number]
        sig = jax.nn.sigmoid(product)
        masked = (grad * sig * (1.0 + product * (1.0 - sig))).astype(jnp.bfloat16)
        grad = times_transposed(masked, deep_weight[layer_number])
    grad_start = jnp.zeros_like(grad)
    first_grad = jnp.zeros((start_row.shape[1], start_row.shape[1]), jnp.float32)
    for layer_number in reversed(range(cross_weight.shape[0])):
        grad_cross = (grad * start_float).astype(jnp.bfloat16)
        grad_start = grad_start + grad * cross_terms[layer_number]
        if layer_number == 0:
            first_grad = lax.dot_general(start_row, grad_cross, (((0,), (0,)), ((), ())), preferred_element_type=jnp.float32)
        grad = grad + times_transposed(grad_cross, cross_weight[layer_number])
    grad_start = grad_start + grad
    scaled = grad_start * norm_gain
    grad_pooled = inverse * scaled - pooled * inverse ** 3 * lax.optimization_barrier(jnp.mean(scaled * pooled, axis=1, keepdims=True))
    return (logits, grad_pooled.astype(jnp.bfloat16), first_grad)

def reference(embed_table, row_ids, row_owner, lengths, feature_slot, labels, norm_gain, cross_weight, cross_bias, deep_weight, deep_bias, out_weight):
    devices_all = row_ids.shape[0]
    ends = jnp.cumsum(lengths, axis=1, dtype=jnp.int32)
    positions = jnp.arange(IDS_DEV, dtype=jnp.int32)
    bag_index = jax.vmap(lambda row_ends: jnp.searchsorted(row_ends, positions, side='right').astype(jnp.int32))(ends).astype(jnp.int32)
    owners = row_owner[:, :, 0].astype(jnp.int32)
    local_row = feature_slot[owners, bag_index % F].astype(jnp.int32) * VOC + row_ids
    global_row = (owners * ROWS_DEV + local_row).reshape(-1).astype(jnp.int32)
    global_bag = (jnp.arange(devices_all, dtype=jnp.int32)[:, None] * BAGS_DEV + bag_index).reshape(-1).astype(jnp.int32)
    pooled = jax.ops.segment_sum(embed_table[global_row].astype(jnp.float32), global_bag, num_segments=devices_all * BAGS_DEV)
    logits, grad_pooled, first_grad = forward_backward(pooled.reshape(SAMPLES, D), labels, norm_gain, cross_weight, cross_bias, deep_weight, deep_bias, out_weight)
    values = grad_pooled.reshape(-1, EMB)[global_bag].astype(jnp.float32)
    row_grad = jax.ops.segment_sum(values, global_row, num_segments=TABLE_ROWS)
    return (row_grad, first_grad, logits)
```

```python
import functools

import jax
import jax.numpy as jnp
import numpy as np
from jax import lax
from jax.experimental import pallas as pl
from jax.experimental.pallas import tpu as pltpu
from jax.sharding import PartitionSpec as P

BF = jnp.bfloat16
F32 = jnp.float32
I32 = jnp.int32
OWNERS = 32
FEATS = 8
KEYS = OWNERS * FEATS
CAP = 512
VOC = 1024
ROWS = FEATS * VOC
EMB = 128
BAGS = 1024
SAMPLES = 128
WIDTH = FEATS * EMB
IDS = 8192
REPS = 4
PAIR = FEATS // REPS
LANES = 256
IDROWS = IDS // LANES
ACCS = 8
VMEM = 56 * 1024 * 1024

NT = (((1,), (1,)), ((), ()))
TN = (((0,), (0,)), ((), ()))


def dot(a, b, dims=(((1,), (0,)), ((), ()))):
    return lax.dot_general(a, b, dims, preferred_element_type=F32)


def iota(shape, dim):
    return lax.broadcasted_iota(I32, shape, dim)


def onehot(cond):
    return jnp.where(cond, 1.0, 0.0).astype(BF)


def index_kernel(ids_ref, owner_ref, len_ref, slot_ref, out_ref, bag_ref, key_ref):
    lens = len_ref[...].astype(F32).astype(BF)
    incl128 = onehot(iota((128, 128), 0) <= iota((128, 128), 1))
    within = dot(lens, incl128)
    total = jnp.broadcast_to(within[:, 127:128], (8, 128))
    high = jnp.floor(total * (1.0 / 256.0))
    low = total - high * 256.0
    below8 = onehot(iota((8, 8), 1) < iota((8, 8), 0))
    before = dot(below8, high.astype(BF)) * 256.0 + dot(below8, low.astype(BF))
    start = (within + before).astype(I32) - len_ref[...]
    start_hi = start >> 8
    start_lo = start & 255
    marks = jnp.zeros((IDROWS, LANES), F32)
    for r in range(8):
        a = onehot(iota((IDROWS, 128), 0) == start_hi[r : r + 1, :])
        b = onehot(iota((LANES, 128), 0) == start_lo[r : r + 1, :])
        marks = marks + dot(a, b, NT)
    marks = marks.astype(BF)
    incl = onehot(iota((LANES, LANES), 0) <= iota((LANES, LANES), 1))
    strict = onehot(iota((LANES, LANES), 0) < iota((LANES, LANES), 1))
    row_counts = dot(marks, jnp.ones((LANES, LANES), BF))
    below = onehot(iota((IDROWS, IDROWS), 1) < iota((IDROWS, IDROWS), 0))
    bag = (dot(marks, incl) + dot(below, row_counts.astype(BF))).astype(I32) - 1
    bag_ref[...] = bag
    key_ref[...] = owner_ref[...] * FEATS + (bag & (FEATS - 1))

    key_iota = iota((KEYS, LANES), 0)

    def count(r, acc):
        return acc + jnp.where(key_iota == key_ref[pl.ds(r, 1), :], 1.0, 0.0)

    counts = lax.fori_loop(0, IDROWS, count, jnp.zeros((KEYS, LANES), F32))
    totals = dot(counts.astype(BF), jnp.ones((LANES, LANES), BF))
    high = jnp.floor(totals * (1.0 / 256.0))
    low = totals - high * 256.0
    ki, kj = iota((KEYS, KEYS), 0), iota((KEYS, KEYS), 1)
    earlier = onehot((ki // FEATS == kj // FEATS) & (kj < ki))
    carry0 = dot(earlier, high.astype(BF)) * 256.0 + dot(earlier, low.astype(BF))

    rank_iota = iota((CAP, LANES), 0)
    owner_iota = iota((OWNERS, LANES), 0)
    slots = jnp.broadcast_to(slot_ref[...].astype(F32), (KEYS, LANES))

    def place(r, state):
        carry, acc = state
        same = key_iota == key_ref[pl.ds(r, 1), :]
        hot = jnp.where(same, 1.0, 0.0)
        prefix = dot(hot.astype(BF), strict)
        rank = jnp.sum(jnp.where(same, prefix + carry, 0.0), axis=0, keepdims=True)
        slot = jnp.sum(jnp.where(same, slots, 0.0), axis=0, keepdims=True)
        rank = rank.astype(I32)
        row = slot.astype(I32) * VOC + ids_ref[pl.ds(r, 1), :]
        value = (1 << 23) + (row << 10) + bag_ref[pl.ds(r, 1), :]
        mine = owner_iota == owner_ref[pl.ds(r, 1), :]
        pieces = [
            jnp.where(mine, jnp.broadcast_to(p.astype(F32), (OWNERS, LANES)), 0.0)
            for p in (value & 255, (value >> 8) & 255, value >> 16)
        ]
        left = jnp.concatenate(pieces, axis=0).astype(BF)
        right = onehot(rank_iota == rank)
        acc = acc + dot(left, right, NT)
        carry = carry + jnp.sum(hot, axis=1, keepdims=True)
        return carry, acc

    _, acc = lax.fori_loop(
        0, IDROWS, place, (carry0, jnp.zeros((3 * OWNERS, CAP), F32))
    )
    acc = acc.astype(I32)
    out_ref[...] = (
        acc[:OWNERS] + (acc[OWNERS : 2 * OWNERS] << 8) + (acc[2 * OWNERS :] << 16)
    )


def index_call(ids, owners, lengths, slots):
    return pl.pallas_call(
        index_kernel,
        out_shape=jax.ShapeDtypeStruct((OWNERS, CAP), I32),
        scratch_shapes=[pltpu.VMEM((IDROWS, LANES), I32), pltpu.VMEM((IDROWS, LANES), I32)],
        compiler_params=pltpu.CompilerParams(vmem_limit_bytes=VMEM),
        name="index",
    )(ids, owners, lengths, slots)


def gather_kernel(row_ref, table_ref, out_ref, wide, picked):
    step = pl.program_id(0)

    @pl.when(step == 0)
    def _():
        wide[...] = table_ref[...].astype(F32)

    base = step * CAP

    def some(i, _):
        at = i * 16
        for j in range(16):
            row = row_ref[base + at + j]
            picked[pl.ds(at + j, 1), :] = wide[pl.ds(row, 1), :]
        return 0

    lax.fori_loop(0, CAP // 16, some, 0)
    out_ref[0] = picked[...].astype(BF)


def gather_call(rows, table):
    return pl.pallas_call(
        gather_kernel,
        out_shape=jax.ShapeDtypeStruct((OWNERS, CAP, EMB), BF),
        grid_spec=pltpu.PrefetchScalarGridSpec(
            num_scalar_prefetch=1,
            grid=(OWNERS,),
            in_specs=[pl.BlockSpec((ROWS, EMB), lambda i, r: (0, 0))],
            out_specs=pl.BlockSpec((1, CAP, EMB), lambda i, r: (i, 0, 0)),
            scratch_shapes=[pltpu.VMEM((ROWS, EMB), F32), pltpu.VMEM((CAP, EMB), F32)],
        ),
        compiler_params=pltpu.CompilerParams(vmem_limit_bytes=VMEM),
        name="gather",
    )(rows, table)


def sigmoid(x):
    return 1.0 / (1.0 + jnp.exp(-x))


def tower_kernel(
    got_ref,
    packed_ref,
    labels_ref,
    gain_ref,
    cbias_ref,
    dbias_ref,
    out_w_ref,
    cross_hbm,
    deep_hbm,
    logits_ref,
    grads_ref,
    first_ref,
    pooled_ref,
    cross_w,
    deep_w,
    start_ref,
    cross_t,
    deep_t,
    gx_ref,
    sems,
):
    step = pl.program_id(0)

    def copies():
        out = []
        for layer in range(3):
            out.append(
                pltpu.make_async_copy(cross_hbm.at[layer], cross_w.at[layer], sems.at[layer])
            )
            out.append(
                pltpu.make_async_copy(deep_hbm.at[layer], deep_w.at[layer], sems.at[3 + layer])
            )
        return out

    @pl.when(step == 0)
    def _():
        for copy in copies():
            copy.start()
        pooled_ref[...] = jnp.zeros_like(pooled_ref)

    packed = packed_ref[pl.ds(step, 1), :]
    bag = packed & (BAGS - 1)
    place = jnp.where(packed > 0, (bag & (FEATS - 1)) * SAMPLES + (bag >> 3), -1)
    hot = onehot(iota((BAGS, CAP), 0) == place)
    pooled_ref[...] += dot(hot, got_ref[0])

    @pl.when(step == OWNERS - 1)
    def _():
        for copy in copies():
            copy.wait()
        gain = gain_ref[...]
        pooled = jnp.concatenate(
            [pooled_ref[f * SAMPLES : (f + 1) * SAMPLES, :] for f in range(FEATS)], axis=1
        )
        inverse = lax.rsqrt(jnp.mean(pooled * pooled, axis=1, keepdims=True) + 1e-06)
        start = (pooled * inverse * gain).astype(BF)
        start_ref[...] = start
        current = start
        for layer in range(3):
            product = dot(current, cross_w[layer]) + cbias_ref[layer : layer + 1, :]
            cross_t[layer] = product
            current = (start_ref[...].astype(F32) * product + current.astype(F32)).astype(BF)
        for layer in range(3):
            product = dot(current, deep_w[layer]) + dbias_ref[layer : layer + 1, :]
            deep_t[layer] = product
            current = (product * sigmoid(product)).astype(BF)
        out_w = out_w_ref[...]
        logits = jnp.sum(current.astype(F32) * out_w, axis=1, keepdims=True)
        logits_ref[...] = logits
        error = sigmoid(logits) - labels_ref[...].astype(F32)
        grad = error * out_w
        for layer in (2, 1, 0):
            product = deep_t[layer]
            sig = sigmoid(product)
            masked = (grad * sig * (1.0 + product * (1.0 - sig))).astype(BF)
            grad = dot(masked, deep_w[layer], NT)
        gx_ref[...] = jnp.zeros_like(gx_ref)
        for layer in (2, 1, 0):
            crossed = (grad * start_ref[...].astype(F32)).astype(BF)
            gx_ref[...] += grad * cross_t[layer]
            grad = grad + dot(crossed, cross_w[layer], NT)
            if layer == 0:
                first_ref[...] = dot(start_ref[...], crossed, TN).astype(first_ref.dtype)
        scaled = (gx_ref[...] + grad) * gain
        pooled = jnp.concatenate(
            [pooled_ref[f * SAMPLES : (f + 1) * SAMPLES, :] for f in range(FEATS)], axis=1
        )
        inverse = lax.rsqrt(jnp.mean(pooled * pooled, axis=1, keepdims=True) + 1e-06)
        mean = jnp.mean(scaled * pooled, axis=1, keepdims=True)
        result = (inverse * scaled - pooled * (inverse * inverse * inverse) * mean).astype(BF)
        for r in range(REPS):
            grads_ref[r] = result[:, r * PAIR * EMB : (r + 1) * PAIR * EMB]


def tower_call(got, packed, labels, gain, cross, cbias, deep, dbias, out_w):
    def whole(shape):
        return pl.BlockSpec(shape, lambda i: (0,) * len(shape))

    return pl.pallas_call(
        tower_kernel,
        grid=(OWNERS,),
        in_specs=[
            pl.BlockSpec((1, CAP, EMB), lambda i: (i, 0, 0)),
            whole((OWNERS, CAP)),
            whole((SAMPLES, 1)),
            whole((1, WIDTH)),
            whole((3, WIDTH)),
            whole((3, WIDTH)),
            whole((1, WIDTH)),
            pl.BlockSpec(memory_space=pl.ANY),
            pl.BlockSpec(memory_space=pl.ANY),
        ],
        out_specs=[
            whole((SAMPLES, 1)),
            whole((REPS, SAMPLES, PAIR * EMB)),
            whole((WIDTH, WIDTH)),
        ],
        out_shape=[
            jax.ShapeDtypeStruct((SAMPLES, 1), F32),
            jax.ShapeDtypeStruct((REPS, SAMPLES, PAIR * EMB), BF),
            jax.ShapeDtypeStruct((WIDTH, WIDTH), BF),
        ],
        scratch_shapes=[
            pltpu.VMEM((BAGS, EMB), F32),
            pltpu.VMEM((3, WIDTH, WIDTH), BF),
            pltpu.VMEM((3, WIDTH, WIDTH), BF),
            pltpu.VMEM((SAMPLES, WIDTH), BF),
            pltpu.VMEM((3, SAMPLES, WIDTH), F32),
            pltpu.VMEM((3, SAMPLES, WIDTH), F32),
            pltpu.VMEM((SAMPLES, WIDTH), F32),
            pltpu.SemaphoreType.DMA((6,)),
        ],
        compiler_params=pltpu.CompilerParams(vmem_limit_bytes=VMEM),
        name="tower",
    )(got, packed, labels, gain, cbias, dbias, out_w, cross, deep)


def scatter_kernel(word_ref, first_ref, last_ref, grads_ref, out_ref, wide, *accs):
    step = pl.program_id(0)

    @pl.when(step == 0)
    def _():
        for acc in accs:
            acc[...] = jnp.zeros_like(acc)

    group = grads_ref.shape[0]
    for g in range(group):
        for r in range(REPS):
            block = grads_ref[g, r]
            base = (g * REPS + r) * PAIR * SAMPLES
            for f in range(PAIR):
                wide[base + f * SAMPLES : base + (f + 1) * SAMPLES, :] = block[
                    :, f * EMB : (f + 1) * EMB
                ].astype(F32)

    def device(k, _):
        base = k * (PAIR * SAMPLES)
        listed = (k & (REPS - 1)) * OWNERS + step * group + k // REPS

        def some(i, _):
            at = listed * CAP + i * ACCS
            for j in range(ACCS):
                word = word_ref[at + j]
                source = base + (word & 255)
                target = word >> 8
                acc = accs[j]
                acc[pl.ds(target, 1), :] += wide[pl.ds(source, 1), :]
            return 0

        lax.fori_loop(first_ref[listed], last_ref[listed], some, 0)
        return 0

    lax.fori_loop(0, group * REPS, device, 0)

    @pl.when(step == pl.num_programs(0) - 1)
    def _():
        total = accs[0][: PAIR * VOC, :]
        for acc in accs[1:]:
            total = total + acc[: PAIR * VOC, :]
        out_ref[...] = total.astype(out_ref.dtype)


def scatter_call(words, first, last, grads, group=2):
    rows = PAIR * VOC
    return pl.pallas_call(
        scatter_kernel,
        out_shape=jax.ShapeDtypeStruct((rows, EMB), BF),
        grid_spec=pltpu.PrefetchScalarGridSpec(
            num_scalar_prefetch=3,
            grid=(OWNERS // group,),
            in_specs=[
                pl.BlockSpec(
                    (group, REPS, SAMPLES, PAIR * EMB), lambda i, w, a, b: (i, 0, 0, 0)
                )
            ],
            out_specs=pl.BlockSpec((rows, EMB), lambda i, w, a, b: (0, 0)),
            scratch_shapes=[pltpu.VMEM((group * REPS * PAIR * SAMPLES, EMB), F32)]
            + [pltpu.VMEM((rows + 8, EMB), F32) for _ in range(ACCS)],
        ),
        compiler_params=pltpu.CompilerParams(vmem_limit_bytes=VMEM),
        name="scatter",
    )(words, first, last, grads)


def widen_kernel(order_ref, in_ref, out_ref):
    del order_ref
    out_ref[...] = in_ref[0].astype(F32)


def widen_call(order, blocks):
    return pl.pallas_call(
        widen_kernel,
        out_shape=jax.ShapeDtypeStruct((ROWS, EMB), F32),
        grid_spec=pltpu.PrefetchScalarGridSpec(
            num_scalar_prefetch=1,
            grid=(FEATS,),
            in_specs=[pl.BlockSpec((1, VOC, EMB), lambda i, o: (o[i], 0, 0))],
            out_specs=pl.BlockSpec((VOC, EMB), lambda i, o: (i, 0)),
        ),
        name="widen",
    )(order, blocks)


def body(
    embed_table,
    row_ids,
    row_owner,
    lengths,
    feature_slot,
    labels,
    norm_gain,
    cross_weight,
    cross_bias,
    deep_weight,
    deep_bias,
    out_weight,
):
    packed = index_call(
        row_ids.reshape(IDROWS, LANES),
        row_owner.reshape(IDROWS, LANES),
        lengths.reshape(8, 128),
        feature_slot.reshape(KEYS, 1),
    )
    asked = lax.all_to_all(
        packed.reshape(OWNERS, 4, 128), "shard", split_axis=0, concat_axis=0, tiled=True
    )
    rows = ((asked >> 10) & (ROWS - 1)).reshape(-1)
    picked = gather_call(rows, embed_table)
    got = lax.all_to_all(picked, "shard", split_axis=0, concat_axis=0, tiled=True)

    everyone = lax.all_gather(asked, "rep", axis=0, tiled=True).reshape(REPS * OWNERS, CAP)
    rep = lax.axis_index("rep")
    feature = everyone & (FEATS - 1)
    valid = everyone > 0
    within = feature - rep * PAIR
    ours = valid & (within >= 0) & (within < PAIR)
    target = jnp.where(ours, within * VOC + ((everyone >> 10) & (VOC - 1)), PAIR * VOC)
    source = jnp.where(ours, within * SAMPLES + ((everyone >> 3) & (SAMPLES - 1)), 0)
    words = ((target << 8) | source).reshape(-1)
    below = jnp.sum((valid & (within < 0)).astype(I32), axis=1)
    upto = jnp.sum((valid & (within < PAIR)).astype(I32), axis=1)
    first = below // ACCS
    last = (upto + ACCS - 1) // ACCS

    logits, grads, first_local = tower_call(
        got,
        packed,
        labels.reshape(SAMPLES, 1),
        norm_gain.reshape(1, WIDTH),
        cross_weight,
        cross_bias,
        deep_weight,
        deep_bias,
        out_weight.reshape(1, WIDTH),
    )
    mine = lax.all_to_all(grads, "rep", split_axis=0, concat_axis=0, tiled=True)
    all_grads = lax.all_gather(mine, "shard", axis=0)
    part = scatter_call(words, first, last, all_grads)
    blocks = lax.all_gather(part, "rep", axis=0, tiled=True).reshape(FEATS, VOC, EMB)
    slots = feature_slot[lax.axis_index("shard")]
    order = jnp.argmax(
        slots[None, :] == jnp.arange(FEATS, dtype=I32)[:, None], axis=1
    ).astype(I32)
    row_grad = widen_call(order, blocks)
    first_grad = lax.psum(first_local, ("rep", "shard")).astype(F32)
    return (row_grad, first_grad, logits.reshape(SAMPLES))


def solution(mesh):
    both = ("rep", "shard")
    in_specs = (
        P("shard", None),
        P(both, None),
        P(both, None, None),
        P(both, None),
        P(),
        P(both),
        P(),
        P(),
        P(),
        P(),
        P(),
        P(),
    )
    out_specs = (P("shard", None), P(), P(both))
    return jax.shard_map(body, mesh=mesh, in_specs=in_specs, out_specs=out_specs, check_vma=False)
```

```python
import functools

import jax
import jax.numpy as jnp
import numpy as np
from jax import lax
from jax.experimental import pallas as pl
from jax.experimental.pallas import tpu as pltpu
from jax.sharding import PartitionSpec as P

BF = jnp.bfloat16
F32 = jnp.float32
I32 = jnp.int32
OWNERS = 32
FEATS = 8
KEYS = OWNERS * FEATS
CAP = 512
VOC = 1024
ROWS = FEATS * VOC
EMB = 128
BAGS = 1024
SAMPLES = 128
WIDTH = FEATS * EMB
IDS = 8192
REPS = 4
PAIR = FEATS // REPS
LANES = 256
IDROWS = IDS // LANES
ACCS = 8
VMEM = 56 * 1024 * 1024

NT = (((1,), (1,)), ((), ()))
TN = (((0,), (0,)), ((), ()))


def dot(a, b, dims=(((1,), (0,)), ((), ()))):
    return lax.dot_general(a, b, dims, preferred_element_type=F32)


def iota(shape, dim):
    return lax.broadcasted_iota(I32, shape, dim)


def onehot(cond):
    return jnp.where(cond, 1.0, 0.0).astype(BF)


def index_kernel(ids_ref, owner_ref, len_ref, slot_ref, out_ref, bag_ref, key_ref):
    lens = len_ref[...].astype(F32).astype(BF)
    incl128 = onehot(iota((128, 128), 0) <= iota((128, 128), 1))
    within = dot(lens, incl128)
    total = jnp.broadcast_to(within[:, 127:128], (8, 128))
    high = jnp.floor(total * (1.0 / 256.0))
    low = total - high * 256.0
    below8 = onehot(iota((8, 8), 1) < iota((8, 8), 0))
    before = dot(below8, high.astype(BF)) * 256.0 + dot(below8, low.astype(BF))
    start = (within + before).astype(I32) - len_ref[...]
    start_hi = start >> 8
    start_lo = start & 255
    marks = jnp.zeros((IDROWS, LANES), F32)
    for r in range(8):
        a = onehot(iota((IDROWS, 128), 0) == start_hi[r : r + 1, :])
        b = onehot(iota((LANES, 128), 0) == start_lo[r : r + 1, :])
        marks = marks + dot(a, b, NT)
    marks = marks.astype(BF)
    incl = onehot(iota((LANES, LANES), 0) <= iota((LANES, LANES), 1))
    strict = onehot(iota((LANES, LANES), 0) < iota((LANES, LANES), 1))
    row_counts = dot(marks, jnp.ones((LANES, LANES), BF))
    below = onehot(iota((IDROWS, IDROWS), 1) < iota((IDROWS, IDROWS), 0))
    bag = (dot(marks, incl) + dot(below, row_counts.astype(BF))).astype(I32) - 1
    bag_ref[...] = bag
    key_ref[...] = owner_ref[...] * FEATS + (bag & (FEATS - 1))

    key_iota = iota((KEYS, LANES), 0)

    def count(r, acc):
        return acc + jnp.where(key_iota == key_ref[pl.ds(r, 1), :], 1.0, 0.0)

    counts = lax.fori_loop(0, IDROWS, count, jnp.zeros((KEYS, LANES), F32))
    totals = dot(counts.astype(BF), jnp.ones((LANES, LANES), BF))
    high = jnp.floor(totals * (1.0 / 256.0))
    low = totals - high * 256.0
    ki, kj = iota((KEYS, KEYS), 0), iota((KEYS, KEYS), 1)
    earlier = onehot((ki // FEATS == kj // FEATS) & (kj < ki))
    carry0 = dot(earlier, high.astype(BF)) * 256.0 + dot(earlier, low.astype(BF))

    rank_iota = iota((CAP, LANES), 0)
    owner_iota = iota((OWNERS, LANES), 0)
    slots = jnp.broadcast_to(slot_ref[...].astype(F32), (KEYS, LANES))

    def place(r, state):
        carry, acc = state
        same = key_iota == key_ref[pl.ds(r, 1), :]
        hot = jnp.where(same, 1.0, 0.0)
        prefix = dot(hot.astype(BF), strict)
        rank = jnp.sum(jnp.where(same, prefix + carry, 0.0), axis=0, keepdims=True)
        slot = jnp.sum(jnp.where(same, slots, 0.0), axis=0, keepdims=True)
        rank = rank.astype(I32)
        row = slot.astype(I32) * VOC + ids_ref[pl.ds(r, 1), :]
        value = (1 << 23) + (row << 10) + bag_ref[pl.ds(r, 1), :]
        mine = owner_iota == owner_ref[pl.ds(r, 1), :]
        pieces = [
            jnp.where(mine, jnp.broadcast_to(p.astype(F32), (OWNERS, LANES)), 0.0)
            for p in (value & 255, (value >> 8) & 255, value >> 16)
        ]
        left = jnp.concatenate(pieces, axis=0).astype(BF)
        right = onehot(rank_iota == rank)
        acc = acc + dot(left, right, NT)
        carry = carry + jnp.sum(hot, axis=1, keepdims=True)
        return carry, acc

    _, acc = lax.fori_loop(
        0, IDROWS, place, (carry0, jnp.zeros((3 * OWNERS, CAP), F32))
    )
    acc = acc.astype(I32)
    out_ref[...] = (
        acc[:OWNERS] + (acc[OWNERS : 2 * OWNERS] << 8) + (acc[2 * OWNERS :] << 16)
    )


def index_call(ids, owners, lengths, slots):
    return pl.pallas_call(
        index_kernel,
        out_shape=jax.ShapeDtypeStruct((OWNERS, CAP), I32),
        scratch_shapes=[pltpu.VMEM((IDROWS, LANES), I32), pltpu.VMEM((IDROWS, LANES), I32)],
        compiler_params=pltpu.CompilerParams(vmem_limit_bytes=VMEM),
        name="index",
    )(ids, owners, lengths, slots)


def gather_kernel(row_ref, table_ref, out_ref, wide, picked):
    step = pl.program_id(0)

    @pl.when(step == 0)
    def _():
        wide[...] = table_ref[...].astype(F32)

    base = step * CAP

    def some(i, _):
        at = i * 16
        for j in range(16):
            row = row_ref[base + at + j]
            picked[pl.ds(at + j, 1), :] = wide[pl.ds(row, 1), :]
        return 0

    lax.fori_loop(0, CAP // 16, some, 0)
    out_ref[0] = picked[...].astype(BF)


def gather_call(rows, table):
    return pl.pallas_call(
        gather_kernel,
        out_shape=jax.ShapeDtypeStruct((OWNERS, CAP, EMB), BF),
        grid_spec=pltpu.PrefetchScalarGridSpec(
            num_scalar_prefetch=1,
            grid=(OWNERS,),
            in_specs=[pl.BlockSpec((ROWS, EMB), lambda i, r: (0, 0))],
            out_specs=pl.BlockSpec((1, CAP, EMB), lambda i, r: (i, 0, 0)),
            scratch_shapes=[pltpu.VMEM((ROWS, EMB), F32), pltpu.VMEM((CAP, EMB), F32)],
        ),
        compiler_params=pltpu.CompilerParams(vmem_limit_bytes=VMEM),
        name="gather",
    )(rows, table)


def sigmoid(x):
    return 1.0 / (1.0 + jnp.exp(-x))


def tower_kernel(
    got_ref,
    packed_ref,
    labels_ref,
    gain_ref,
    cbias_ref,
    dbias_ref,
    out_w_ref,
    cross_hbm,
    deep_hbm,
    logits_ref,
    grads_ref,
    first_ref,
    pooled_ref,
    cross_w,
    deep_w,
    start_ref,
    cross_t,
    deep_t,
    gx_ref,
    sems,
):
    step = pl.program_id(0)

    def copies():
        out = []
        for layer in range(3):
            out.append(
                pltpu.make_async_copy(cross_hbm.at[layer], cross_w.at[layer], sems.at[layer])
            )
            out.append(
                pltpu.make_async_copy(deep_hbm.at[layer], deep_w.at[layer], sems.at[3 + layer])
            )
        return out

    @pl.when(step == 0)
    def _():
        for copy in copies():
            copy.start()
        pooled_ref[...] = jnp.zeros_like(pooled_ref)

    packed = packed_ref[pl.ds(step, 1), :]
    bag = packed & (BAGS - 1)
    place = jnp.where(packed > 0, (bag & (FEATS - 1)) * SAMPLES + (bag >> 3), -1)
    hot = onehot(iota((BAGS, CAP), 0) == place)
    pooled_ref[...] += dot(hot, got_ref[0])

    @pl.when(step == OWNERS - 1)
    def _():
        for copy in copies():
            copy.wait()
        gain = gain_ref[...]
        pooled = jnp.concatenate(
            [pooled_ref[f * SAMPLES : (f + 1) * SAMPLES, :] for f in range(FEATS)], axis=1
        )
        inverse = lax.rsqrt(jnp.mean(pooled * pooled, axis=1, keepdims=True) + 1e-06)
        start = (pooled * inverse * gain).astype(BF)
        start_ref[...] = start
        current = start
        for layer in range(3):
            product = dot(current, cross_w[layer]) + cbias_ref[layer : layer + 1, :]
            cross_t[layer] = product
            current = (start_ref[...].astype(F32) * product + current.astype(F32)).astype(BF)
        for layer in range(3):
            product = dot(current, deep_w[layer]) + dbias_ref[layer : layer + 1, :]
            deep_t[layer] = product
            current = (product * sigmoid(product)).astype(BF)
        out_w = out_w_ref[...]
        logits = jnp.sum(current.astype(F32) * out_w, axis=1, keepdims=True)
        logits_ref[...] = logits
        error = sigmoid(logits) - labels_ref[...].astype(F32)
        grad = error * out_w
        for layer in (2, 1, 0):
            product = deep_t[layer]
            sig = sigmoid(product)
            masked = (grad * sig * (1.0 + product * (1.0 - sig))).astype(BF)
            grad = dot(masked, deep_w[layer], NT)
        gx_ref[...] = jnp.zeros_like(gx_ref)
        for layer in (2, 1, 0):
            crossed = (grad * start_ref[...].astype(F32)).astype(BF)
            gx_ref[...] += grad * cross_t[layer]
            grad = grad + dot(crossed, cross_w[layer], NT)
            if layer == 0:
                summed = dot(start_ref[...], crossed, TN).reshape(OWNERS, REPS, 8, WIDTH)
                for r in range(REPS):
                    first_ref[r] = summed[:, r].reshape(OWNERS * 8, WIDTH).astype(BF)
        scaled = (gx_ref[...] + grad) * gain
        pooled = jnp.concatenate(
            [pooled_ref[f * SAMPLES : (f + 1) * SAMPLES, :] for f in range(FEATS)], axis=1
        )
        inverse = lax.rsqrt(jnp.mean(pooled * pooled, axis=1, keepdims=True) + 1e-06)
        mean = jnp.mean(scaled * pooled, axis=1, keepdims=True)
        result = (inverse * scaled - pooled * (inverse * inverse * inverse) * mean).astype(BF)
        for r in range(REPS):
            grads_ref[r] = result[:, r * PAIR * EMB : (r + 1) * PAIR * EMB]


def tower_call(got, packed, labels, gain, cross, cbias, deep, dbias, out_w):
    def whole(shape):
        return pl.BlockSpec(shape, lambda i: (0,) * len(shape))

    return pl.pallas_call(
        tower_kernel,
        grid=(OWNERS,),
        in_specs=[
            pl.BlockSpec((1, CAP, EMB), lambda i: (i, 0, 0)),
            whole((OWNERS, CAP)),
            whole((SAMPLES, 1)),
            whole((1, WIDTH)),
            whole((3, WIDTH)),
            whole((3, WIDTH)),
            whole((1, WIDTH)),
            pl.BlockSpec(memory_space=pl.ANY),
            pl.BlockSpec(memory_space=pl.ANY),
        ],
        out_specs=[
            whole((SAMPLES, 1)),
            whole((REPS, SAMPLES, PAIR * EMB)),
            whole((REPS, OWNERS * 8, WIDTH)),
        ],
        out_shape=[
            jax.ShapeDtypeStruct((SAMPLES, 1), F32),
            jax.ShapeDtypeStruct((REPS, SAMPLES, PAIR * EMB), BF),
            jax.ShapeDtypeStruct((REPS, OWNERS * 8, WIDTH), BF),
        ],
        scratch_shapes=[
            pltpu.VMEM((BAGS, EMB), F32),
            pltpu.VMEM((3, WIDTH, WIDTH), BF),
            pltpu.VMEM((3, WIDTH, WIDTH), BF),
            pltpu.VMEM((SAMPLES, WIDTH), BF),
            pltpu.VMEM((3, SAMPLES, WIDTH), F32),
            pltpu.VMEM((3, SAMPLES, WIDTH), F32),
            pltpu.VMEM((SAMPLES, WIDTH), F32),
            pltpu.SemaphoreType.DMA((6,)),
        ],
        compiler_params=pltpu.CompilerParams(vmem_limit_bytes=VMEM),
        name="tower",
    )(got, packed, labels, gain, cbias, dbias, out_w, cross, deep)


def scatter_kernel(word_ref, first_ref, last_ref, grads_ref, out_ref, wide, *accs):
    step = pl.program_id(0)

    @pl.when(step == 0)
    def _():
        for acc in accs:
            acc[...] = jnp.zeros_like(acc)

    group = grads_ref.shape[0]
    for g in range(group):
        for r in range(REPS):
            block = grads_ref[g, r]
            base = (g * REPS + r) * PAIR * SAMPLES
            for f in range(PAIR):
                wide[base + f * SAMPLES : base + (f + 1) * SAMPLES, :] = block[
                    :, f * EMB : (f + 1) * EMB
                ].astype(F32)

    def device(k, _):
        base = k * (PAIR * SAMPLES)
        listed = (k & (REPS - 1)) * OWNERS + step * group + k // REPS

        def some(i, _):
            at = listed * CAP + i * ACCS
            for j in range(ACCS):
                word = word_ref[at + j]
                source = base + (word & 255)
                target = word >> 8
                acc = accs[j]
                acc[pl.ds(target, 1), :] += wide[pl.ds(source, 1), :]
            return 0

        lax.fori_loop(first_ref[listed], last_ref[listed], some, 0)
        return 0

    lax.fori_loop(0, group * REPS, device, 0)

    @pl.when(step == pl.num_programs(0) - 1)
    def _():
        total = accs[0][: PAIR * VOC, :]
        for acc in accs[1:]:
            total = total + acc[: PAIR * VOC, :]
        out_ref[...] = total.astype(out_ref.dtype)


def scatter_call(words, first, last, grads, group=2):
    rows = PAIR * VOC
    return pl.pallas_call(
        scatter_kernel,
        out_shape=jax.ShapeDtypeStruct((rows, EMB), BF),
        grid_spec=pltpu.PrefetchScalarGridSpec(
            num_scalar_prefetch=3,
            grid=(OWNERS // group,),
            in_specs=[
                pl.BlockSpec(
                    (group, REPS, SAMPLES, PAIR * EMB), lambda i, w, a, b: (i, 0, 0, 0)
                )
            ],
            out_specs=pl.BlockSpec((rows, EMB), lambda i, w, a, b: (0, 0)),
            scratch_shapes=[pltpu.VMEM((group * REPS * PAIR * SAMPLES, EMB), F32)]
            + [pltpu.VMEM((rows + 8, EMB), F32) for _ in range(ACCS)],
        ),
        compiler_params=pltpu.CompilerParams(vmem_limit_bytes=VMEM),
        name="scatter",
    )(words, first, last, grads)


def finish_kernel(order_ref, *refs):
    parts, first_ref, rows_ref, grad_ref = refs[:REPS], refs[REPS], refs[REPS + 1], refs[REPS + 2]
    source = order_ref[pl.program_id(0)]
    for k in range(REPS):

        @pl.when(source // PAIR == k)
        def _():
            rows_ref[...] = parts[k][lax.rem(source, PAIR)].astype(F32)

    grad_ref[...] = first_ref[...].astype(F32)


def finish_call(order, parts, first):
    rows = WIDTH // FEATS
    return pl.pallas_call(
        finish_kernel,
        out_shape=[
            jax.ShapeDtypeStruct((ROWS, EMB), F32),
            jax.ShapeDtypeStruct((WIDTH, WIDTH), F32),
        ],
        grid_spec=pltpu.PrefetchScalarGridSpec(
            num_scalar_prefetch=1,
            grid=(FEATS,),
            in_specs=[pl.BlockSpec((PAIR, VOC, EMB), lambda i, o: (0, 0, 0)) for _ in parts]
            + [pl.BlockSpec((rows, WIDTH), lambda i, o: (i, 0))],
            out_specs=[
                pl.BlockSpec((VOC, EMB), lambda i, o: (i, 0)),
                pl.BlockSpec((rows, WIDTH), lambda i, o: (i, 0)),
            ],
        ),
        compiler_params=pltpu.CompilerParams(vmem_limit_bytes=VMEM),
        name="finish",
    )(order, *parts, first)


def from_before(x, axis, k):
    n = lax.axis_size(axis)
    return lax.ppermute(x, axis, [(i, (i + k) % n) for i in range(n)])


def summed(x):
    return jnp.sum(x.astype(F32), axis=0).astype(BF)


def body(
    embed_table,
    row_ids,
    row_owner,
    lengths,
    feature_slot,
    labels,
    norm_gain,
    cross_weight,
    cross_bias,
    deep_weight,
    deep_bias,
    out_weight,
):
    packed = index_call(
        row_ids.reshape(IDROWS, LANES),
        row_owner.reshape(IDROWS, LANES),
        lengths.reshape(8, 128),
        feature_slot.reshape(KEYS, 1),
    )
    asked = lax.all_to_all(
        packed.reshape(OWNERS, 4, 128), "shard", split_axis=0, concat_axis=0, tiled=True
    )
    rows = ((asked >> 10) & (ROWS - 1)).reshape(-1)
    picked = gather_call(rows, embed_table)
    got = lax.all_to_all(picked, "shard", split_axis=0, concat_axis=0, tiled=True)

    everyone = lax.all_gather(asked, "rep", axis=0, tiled=True).reshape(REPS * OWNERS, CAP)
    rep = lax.axis_index("rep")
    feature = everyone & (FEATS - 1)
    valid = everyone > 0
    within = feature - rep * PAIR
    ours = valid & (within >= 0) & (within < PAIR)
    target = jnp.where(ours, within * VOC + ((everyone >> 10) & (VOC - 1)), PAIR * VOC)
    source = jnp.where(ours, within * SAMPLES + ((everyone >> 3) & (SAMPLES - 1)), 0)
    words = ((target << 8) | source).reshape(-1)
    below = jnp.sum((valid & (within < 0)).astype(I32), axis=1)
    upto = jnp.sum((valid & (within < PAIR)).astype(I32), axis=1)
    first_block = below // ACCS
    last_block = (upto + ACCS - 1) // ACCS

    logits, grads, first_local = tower_call(
        got,
        packed,
        labels.reshape(SAMPLES, 1),
        norm_gain.reshape(1, WIDTH),
        cross_weight,
        cross_bias,
        deep_weight,
        deep_bias,
        out_weight.reshape(1, WIDTH),
    )
    mine = lax.all_to_all(grads, "rep", split_axis=0, concat_axis=0, tiled=True)
    mine, first_local = lax.optimization_barrier((mine, first_local))
    all_grads = lax.all_gather(mine, "shard", axis=0)
    quarter = summed(
        lax.all_to_all(first_local, "rep", split_axis=0, concat_axis=0, tiled=True)
    )
    eight = summed(
        lax.all_to_all(
            quarter.reshape(OWNERS, 8, WIDTH), "shard", split_axis=0, concat_axis=0, tiled=True
        )
    )
    first = lax.all_gather(
        lax.all_gather(eight, "rep", axis=0, tiled=True), "shard", axis=0, tiled=True
    )

    part = scatter_call(words, first_block, last_block, all_grads).reshape(PAIR, VOC, EMB)
    parts = [part] + [from_before(part, "rep", k) for k in range(1, REPS)]
    slots = feature_slot[lax.axis_index("shard")]
    feature_of = jnp.argmax(
        slots[None, :] == jnp.arange(FEATS, dtype=I32)[:, None], axis=1
    ).astype(I32)
    order = ((rep - feature_of // PAIR) & (REPS - 1)) * PAIR + feature_of % PAIR
    row_grad, first_grad = finish_call(order, parts, first)
    return (row_grad, first_grad, logits.reshape(SAMPLES))


def solution(mesh):
    both = ("rep", "shard")
    in_specs = (
        P("shard", None),
        P(both, None),
        P(both, None, None),
        P(both, None),
        P(),
        P(both),
        P(),
        P(),
        P(),
        P(),
        P(),
        P(),
    )
    out_specs = (P("shard", None), P(), P(both))
    return jax.shard_map(body, mesh=mesh, in_specs=in_specs, out_specs=out_specs, check_vma=False)
```

```python
import functools

import jax
import jax.numpy as jnp
import numpy as np
from jax import lax
from jax.experimental import pallas as pl
from jax.experimental.pallas import tpu as pltpu
from jax.sharding import PartitionSpec as P

BF = jnp.bfloat16
F32 = jnp.float32
I32 = jnp.int32
OWNERS = 32
FEATS = 8
KEYS = OWNERS * FEATS
CAP = 512
VOC = 1024
ROWS = FEATS * VOC
EMB = 128
BAGS = 1024
SAMPLES = 128
WIDTH = FEATS * EMB
IDS = 8192
REPS = 4
PAIR = FEATS // REPS
LANES = 256
IDROWS = IDS // LANES
ACCS = 16
POOLED = 8
VMEM = 56 * 1024 * 1024

NT = (((1,), (1,)), ((), ()))
TN = (((0,), (0,)), ((), ()))


def dot(a, b, dims=(((1,), (0,)), ((), ()))):
    return lax.dot_general(a, b, dims, preferred_element_type=F32)


def iota(shape, dim):
    return lax.broadcasted_iota(I32, shape, dim)


def onehot(cond):
    return jnp.where(cond, 1.0, 0.0).astype(BF)


def index_kernel(ids_ref, owner_ref, len_ref, slot_ref, out_ref, bag_ref, key_ref):
    lens = len_ref[...].astype(F32).astype(BF)
    incl128 = onehot(iota((128, 128), 0) <= iota((128, 128), 1))
    within = dot(lens, incl128)
    total = jnp.broadcast_to(within[:, 127:128], (8, 128))
    high = jnp.floor(total * (1.0 / 256.0))
    low = total - high * 256.0
    below8 = onehot(iota((8, 8), 1) < iota((8, 8), 0))
    before = dot(below8, high.astype(BF)) * 256.0 + dot(below8, low.astype(BF))
    start = (within + before).astype(I32) - len_ref[...]
    start_hi = start >> 8
    start_lo = start & 255
    marks = jnp.zeros((IDROWS, LANES), F32)
    for r in range(8):
        a = onehot(iota((IDROWS, 128), 0) == start_hi[r : r + 1, :])
        b = onehot(iota((LANES, 128), 0) == start_lo[r : r + 1, :])
        marks = marks + dot(a, b, NT)
    marks = marks.astype(BF)
    incl = onehot(iota((LANES, LANES), 0) <= iota((LANES, LANES), 1))
    strict = onehot(iota((LANES, LANES), 0) < iota((LANES, LANES), 1))
    row_counts = dot(marks, jnp.ones((LANES, LANES), BF))
    below = onehot(iota((IDROWS, IDROWS), 1) < iota((IDROWS, IDROWS), 0))
    bag = (dot(marks, incl) + dot(below, row_counts.astype(BF))).astype(I32) - 1
    bag_ref[...] = bag
    key_ref[...] = owner_ref[...] * FEATS + (bag & (FEATS - 1))

    key_iota = iota((KEYS, LANES), 0)

    def count(r, acc):
        return acc + jnp.where(key_iota == key_ref[pl.ds(r, 1), :], 1.0, 0.0)

    counts = lax.fori_loop(0, IDROWS, count, jnp.zeros((KEYS, LANES), F32), unroll=4)
    totals = dot(counts.astype(BF), jnp.ones((LANES, LANES), BF))
    high = jnp.floor(totals * (1.0 / 256.0))
    low = totals - high * 256.0
    ki, kj = iota((KEYS, KEYS), 0), iota((KEYS, KEYS), 1)
    earlier = onehot((ki // FEATS == kj // FEATS) & (kj < ki))
    carry0 = dot(earlier, high.astype(BF)) * 256.0 + dot(earlier, low.astype(BF))

    rank_iota = iota((CAP, LANES), 0)
    owner_iota = iota((OWNERS, LANES), 0)

    carry0 = carry0 + jnp.broadcast_to(slot_ref[...].astype(F32), (KEYS, LANES)) * VOC

    def place(r, state):
        carry, acc = state
        same = key_iota == key_ref[pl.ds(r, 1), :]
        hot = jnp.where(same, 1.0, 0.0)
        prefix = dot(hot.astype(BF), strict)
        found = jnp.sum(jnp.where(same, prefix + carry, 0.0), axis=0, keepdims=True)
        found = found.astype(I32)
        rank = found & (VOC - 1)
        row = (found - rank) + ids_ref[pl.ds(r, 1), :]
        value = (1 << 23) + (row << 10) + bag_ref[pl.ds(r, 1), :]
        mine = owner_iota == owner_ref[pl.ds(r, 1), :]
        pieces = [
            jnp.where(mine, jnp.broadcast_to(p.astype(F32), (OWNERS, LANES)), 0.0)
            for p in (value & 255, (value >> 8) & 255, value >> 16)
        ]
        left = jnp.concatenate(pieces, axis=0).astype(BF)
        right = onehot(rank_iota == rank)
        acc = acc + dot(left, right, NT)
        carry = carry + (prefix + hot)[:, LANES - 1 : LANES]
        return carry, acc

    _, acc = lax.fori_loop(
        0, IDROWS, place, (carry0, jnp.zeros((3 * OWNERS, CAP), F32)), unroll=8
    )
    acc = acc.astype(I32)
    out_ref[...] = (
        acc[:OWNERS] + (acc[OWNERS : 2 * OWNERS] << 8) + (acc[2 * OWNERS :] << 16)
    )


def index_call(ids, owners, lengths, slots):
    return pl.pallas_call(
        index_kernel,
        out_shape=jax.ShapeDtypeStruct((OWNERS, CAP), I32),
        scratch_shapes=[pltpu.VMEM((IDROWS, LANES), I32), pltpu.VMEM((IDROWS, LANES), I32)],
        compiler_params=pltpu.CompilerParams(vmem_limit_bytes=VMEM),
        name="index",
    )(ids, owners, lengths, slots)


def gather_kernel(row_ref, table_ref, out_ref, wide, picked):
    step = pl.program_id(0)

    @pl.when(step == 0)
    def _():
        wide[...] = table_ref[...].astype(F32)

    base = step * CAP

    def some(i, _):
        at = i * 32
        rows = [wide[pl.ds(row_ref[base + at + j], 1), :] for j in range(32)]
        for j in range(32):
            picked[pl.ds(at + j, 1), :] = rows[j]
        return 0

    lax.fori_loop(0, CAP // 32, some, 0)
    out_ref[0] = picked[...].astype(BF)


def gather_call(rows, table):
    return pl.pallas_call(
        gather_kernel,
        out_shape=jax.ShapeDtypeStruct((OWNERS, CAP, EMB), BF),
        grid_spec=pltpu.PrefetchScalarGridSpec(
            num_scalar_prefetch=1,
            grid=(OWNERS,),
            in_specs=[pl.BlockSpec((ROWS, EMB), lambda i, r: (0, 0))],
            out_specs=pl.BlockSpec((1, CAP, EMB), lambda i, r: (i, 0, 0)),
            scratch_shapes=[pltpu.VMEM((ROWS, EMB), F32), pltpu.VMEM((CAP, EMB), F32)],
        ),
        compiler_params=pltpu.CompilerParams(vmem_limit_bytes=VMEM),
        name="gather",
    )(rows, table)


def sigmoid(x):
    return 1.0 / (1.0 + jnp.exp(-x))


def tower_kernel(
    got_ref,
    packed_ref,
    labels_ref,
    gain_ref,
    cbias_ref,
    dbias_ref,
    out_w_ref,
    cross_hbm,
    deep_hbm,
    logits_ref,
    grads_ref,
    first_ref,
    pooled_ref,
    cross_w,
    deep_w,
    start_ref,
    cross_t,
    deep_t,
    gx_ref,
    sems,
):
    step = pl.program_id(0)

    def copies():
        out = []
        for layer in range(3):
            out.append(
                pltpu.make_async_copy(cross_hbm.at[layer], cross_w.at[layer], sems.at[layer])
            )
            out.append(
                pltpu.make_async_copy(deep_hbm.at[layer], deep_w.at[layer], sems.at[3 + layer])
            )
        return out

    @pl.when(step == 0)
    def _():
        for copy in copies():
            copy.start()
        pooled_ref[...] = jnp.zeros_like(pooled_ref)

    rows, masked = [], []
    for i in range(POOLED):
        packed = packed_ref[pl.ds(step * POOLED + i, 1), :]
        bag = packed & (BAGS - 1)
        sample = jnp.where(packed > 0, bag >> 3, -1)
        rows.append(onehot(iota((SAMPLES, CAP), 0) == sample))
        feature = jnp.broadcast_to((bag & (FEATS - 1)).astype(F32), (EMB, CAP)).T.astype(BF)
        own = got_ref[i]
        masked.append(
            jnp.concatenate(
                [jnp.where(feature == f, own, jnp.zeros((), BF)) for f in range(FEATS)], axis=1
            )
        )
    sums = dot(jnp.concatenate(rows, axis=1), jnp.concatenate(masked, axis=0))
    pooled_ref[...] += sums

    @pl.when(step == OWNERS // POOLED - 1)
    def _():
        for copy in copies():
            copy.wait()
        gain = gain_ref[...]
        pooled = pooled_ref[...]
        inverse = lax.rsqrt(jnp.mean(pooled * pooled, axis=1, keepdims=True) + 1e-06)
        start = (pooled * inverse * gain).astype(BF)
        start_ref[...] = start
        current = start
        for layer in range(3):
            product = dot(current, cross_w[layer]) + cbias_ref[layer : layer + 1, :]
            cross_t[layer] = product
            current = (start_ref[...].astype(F32) * product + current.astype(F32)).astype(BF)
        for layer in range(3):
            product = dot(current, deep_w[layer]) + dbias_ref[layer : layer + 1, :]
            deep_t[layer] = product
            current = (product * sigmoid(product)).astype(BF)
        out_w = out_w_ref[...]
        logits = jnp.sum(current.astype(F32) * out_w, axis=1, keepdims=True)
        logits_ref[...] = logits
        error = sigmoid(logits) - labels_ref[...].astype(F32)
        grad = error * out_w
        for layer in (2, 1, 0):
            product = deep_t[layer]
            sig = sigmoid(product)
            masked = (grad * sig * (1.0 + product * (1.0 - sig))).astype(BF)
            grad = dot(masked, deep_w[layer], NT)
        gx_ref[...] = jnp.zeros_like(gx_ref)
        for layer in (2, 1, 0):
            crossed = (grad * start_ref[...].astype(F32)).astype(BF)
            gx_ref[...] += grad * cross_t[layer]
            grad = grad + dot(crossed, cross_w[layer], NT)
            if layer == 0:
                summed = dot(start_ref[...], crossed, TN).reshape(OWNERS, REPS, 8, WIDTH)
                for r in range(REPS):
                    first_ref[r] = summed[:, r].reshape(OWNERS * 8, WIDTH).astype(BF)
        scaled = (gx_ref[...] + grad) * gain
        pooled = pooled_ref[...]
        inverse = lax.rsqrt(jnp.mean(pooled * pooled, axis=1, keepdims=True) + 1e-06)
        mean = jnp.mean(scaled * pooled, axis=1, keepdims=True)
        result = (inverse * scaled - pooled * (inverse * inverse * inverse) * mean).astype(BF)
        for r in range(REPS):
            grads_ref[r] = result[:, r * PAIR * EMB : (r + 1) * PAIR * EMB]


def tower_call(got, packed, labels, gain, cross, cbias, deep, dbias, out_w):
    def whole(shape):
        return pl.BlockSpec(shape, lambda i: (0,) * len(shape))

    return pl.pallas_call(
        tower_kernel,
        grid=(OWNERS // POOLED,),
        in_specs=[
            pl.BlockSpec((POOLED, CAP, EMB), lambda i: (i, 0, 0)),
            whole((OWNERS, CAP)),
            whole((SAMPLES, 1)),
            whole((1, WIDTH)),
            whole((3, WIDTH)),
            whole((3, WIDTH)),
            whole((1, WIDTH)),
            pl.BlockSpec(memory_space=pl.ANY),
            pl.BlockSpec(memory_space=pl.ANY),
        ],
        out_specs=[
            whole((SAMPLES, 1)),
            whole((REPS, SAMPLES, PAIR * EMB)),
            whole((REPS, OWNERS * 8, WIDTH)),
        ],
        out_shape=[
            jax.ShapeDtypeStruct((SAMPLES, 1), F32),
            jax.ShapeDtypeStruct((REPS, SAMPLES, PAIR * EMB), BF),
            jax.ShapeDtypeStruct((REPS, OWNERS * 8, WIDTH), BF),
        ],
        scratch_shapes=[
            pltpu.VMEM((SAMPLES, WIDTH), F32),
            pltpu.VMEM((3, WIDTH, WIDTH), BF),
            pltpu.VMEM((3, WIDTH, WIDTH), BF),
            pltpu.VMEM((SAMPLES, WIDTH), BF),
            pltpu.VMEM((3, SAMPLES, WIDTH), F32),
            pltpu.VMEM((3, SAMPLES, WIDTH), F32),
            pltpu.VMEM((SAMPLES, WIDTH), F32),
            pltpu.SemaphoreType.DMA((6,)),
        ],
        compiler_params=pltpu.CompilerParams(vmem_limit_bytes=VMEM),
        name="tower",
    )(got, packed, labels, gain, cbias, dbias, out_w, cross, deep)


def scatter_kernel(rep_ref, word_ref, first_ref, last_ref, grads_ref, out_ref, wide, *accs):
    step = pl.program_id(0)

    @pl.when(step == 0)
    def _():
        for acc in accs:
            acc[...] = jnp.zeros_like(acc)

    group = grads_ref.shape[0]
    for g in range(group):
        for r in range(REPS):
            block = grads_ref[g, r]
            base = (g * REPS + r) * PAIR * SAMPLES
            for f in range(PAIR):
                wide[base + f * SAMPLES : base + (f + 1) * SAMPLES, :] = block[
                    :, f * EMB : (f + 1) * EMB
                ].astype(F32)

    def device(k, _):
        base = k * (PAIR * SAMPLES)
        before = (rep_ref[0] - k) & (REPS - 1)
        listed = before * OWNERS + step * group + k // REPS

        def some(i, _):
            at = listed * CAP + i * ACCS
            words = [word_ref[at + j] for j in range(ACCS)]
            rows = [wide[pl.ds(base + (word & 255), 1), :] for word in words]
            olds = [accs[j][pl.ds(words[j] >> 8, 1), :] for j in range(ACCS)]
            for j in range(ACCS):
                accs[j][pl.ds(words[j] >> 8, 1), :] = olds[j] + rows[j]
            return 0

        lax.fori_loop(first_ref[listed], last_ref[listed], some, 0)
        return 0

    lax.fori_loop(0, group * REPS, device, 0)

    @pl.when(step == pl.num_programs(0) - 1)
    def _():
        total = accs[0][: PAIR * VOC, :]
        for acc in accs[1:]:
            total = total + acc[: PAIR * VOC, :]
        out_ref[...] = total.astype(out_ref.dtype)


def scatter_call(rep, words, first, last, grads, group=8):
    rows = PAIR * VOC
    return pl.pallas_call(
        scatter_kernel,
        out_shape=jax.ShapeDtypeStruct((rows, EMB), BF),
        grid_spec=pltpu.PrefetchScalarGridSpec(
            num_scalar_prefetch=4,
            grid=(OWNERS // group,),
            in_specs=[
                pl.BlockSpec(
                    (group, REPS, SAMPLES, PAIR * EMB), lambda i, *_: (i, 0, 0, 0)
                )
            ],
            out_specs=pl.BlockSpec((rows, EMB), lambda i, *_: (0, 0)),
            scratch_shapes=[pltpu.VMEM((group * REPS * PAIR * SAMPLES, EMB), F32)]
            + [pltpu.VMEM((rows + 8, EMB), F32) for _ in range(ACCS)],
        ),
        compiler_params=pltpu.CompilerParams(vmem_limit_bytes=VMEM),
        name="scatter",
    )(rep, words, first, last, grads)


def finish_kernel(order_ref, *refs):
    parts, first_ref, rows_ref, grad_ref = refs[:REPS], refs[REPS], refs[REPS + 1], refs[REPS + 2]
    source = order_ref[pl.program_id(0)]
    for k in range(REPS):

        @pl.when(source // PAIR == k)
        def _():
            rows_ref[...] = parts[k][lax.rem(source, PAIR)].astype(F32)

    grad_ref[...] = first_ref[...].astype(F32)


def finish_call(order, parts, first):
    rows = WIDTH // FEATS
    return pl.pallas_call(
        finish_kernel,
        out_shape=[
            jax.ShapeDtypeStruct((ROWS, EMB), F32),
            jax.ShapeDtypeStruct((WIDTH, WIDTH), F32),
        ],
        grid_spec=pltpu.PrefetchScalarGridSpec(
            num_scalar_prefetch=1,
            grid=(FEATS,),
            in_specs=[pl.BlockSpec((PAIR, VOC, EMB), lambda i, o: (0, 0, 0)) for _ in parts]
            + [pl.BlockSpec((rows, WIDTH), lambda i, o: (i, 0))],
            out_specs=[
                pl.BlockSpec((VOC, EMB), lambda i, o: (i, 0)),
                pl.BlockSpec((rows, WIDTH), lambda i, o: (i, 0)),
            ],
        ),
        compiler_params=pltpu.CompilerParams(vmem_limit_bytes=VMEM),
        name="finish",
    )(order, *parts, first)


def from_before(x, axis, k):
    n = lax.axis_size(axis)
    return lax.ppermute(x, axis, [(i, (i + k) % n) for i in range(n)])


def in_order(x, axis, me):
    n = lax.axis_size(axis)
    back = [x] + [from_before(x, axis, k) for k in range(1, n)]
    twice = jnp.concatenate([back[(n - 1 - i) % n] for i in range(2 * n - 1)])
    return lax.dynamic_slice_in_dim(twice, (n - 1 - me) * x.shape[0], n * x.shape[0])


def summed(x):
    return jnp.sum(x.astype(F32), axis=0).astype(BF)


def body(
    embed_table,
    row_ids,
    row_owner,
    lengths,
    feature_slot,
    labels,
    norm_gain,
    cross_weight,
    cross_bias,
    deep_weight,
    deep_bias,
    out_weight,
):
    packed = index_call(
        row_ids.reshape(IDROWS, LANES),
        row_owner.reshape(IDROWS, LANES),
        lengths.reshape(8, 128),
        feature_slot.reshape(KEYS, 1),
    )
    asked = lax.all_to_all(
        packed.reshape(OWNERS, 4, 128), "shard", split_axis=0, concat_axis=0, tiled=True
    )
    rows = ((asked >> 10) & (ROWS - 1)).reshape(-1)
    picked = gather_call(rows, embed_table)
    picked, lists = lax.optimization_barrier((picked, asked))
    got = lax.all_to_all(picked, "shard", split_axis=0, concat_axis=0, tiled=True)

    rep = lax.axis_index("rep")
    everyone = jnp.concatenate(
        [lists] + [from_before(lists, "rep", k) for k in range(1, REPS)]
    ).reshape(REPS * OWNERS, CAP)
    feature = everyone & (FEATS - 1)
    valid = everyone > 0
    within = feature - rep * PAIR
    ours = valid & (within >= 0) & (within < PAIR)
    target = jnp.where(ours, within * VOC + ((everyone >> 10) & (VOC - 1)), PAIR * VOC)
    source = jnp.where(ours, within * SAMPLES + ((everyone >> 3) & (SAMPLES - 1)), 0)
    words = ((target << 8) | source).reshape(-1)
    below = jnp.sum((valid & (within < 0)).astype(I32), axis=1)
    upto = jnp.sum((valid & (within < PAIR)).astype(I32), axis=1)
    first_block = below // ACCS
    last_block = (upto + ACCS - 1) // ACCS
    got, words, first_block, last_block = lax.optimization_barrier(
        (got, words, first_block, last_block)
    )

    logits, grads, first_local = tower_call(
        got,
        packed,
        labels.reshape(SAMPLES, 1),
        norm_gain.reshape(1, WIDTH),
        cross_weight,
        cross_bias,
        deep_weight,
        deep_bias,
        out_weight.reshape(1, WIDTH),
    )
    mine = lax.all_to_all(grads, "rep", split_axis=0, concat_axis=0, tiled=True)
    mine, first_local = lax.optimization_barrier((mine, first_local))
    all_grads = lax.all_gather(mine, "shard", axis=0)
    quarter = summed(
        lax.all_to_all(first_local, "rep", split_axis=0, concat_axis=0, tiled=True)
    )
    eight = summed(
        lax.all_to_all(
            quarter.reshape(OWNERS, 8, WIDTH), "shard", split_axis=0, concat_axis=0, tiled=True
        )
    )
    first = lax.all_gather(in_order(eight, "rep", rep), "shard", axis=0, tiled=True)

    part = scatter_call(rep.reshape(1), words, first_block, last_block, all_grads).reshape(PAIR, VOC, EMB)
    parts = [part] + [from_before(part, "rep", k) for k in range(1, REPS)]
    slots = feature_slot[lax.axis_index("shard")]
    feature_of = jnp.argmax(
        slots[None, :] == jnp.arange(FEATS, dtype=I32)[:, None], axis=1
    ).astype(I32)
    order = ((rep - feature_of // PAIR) & (REPS - 1)) * PAIR + feature_of % PAIR
    row_grad, first_grad = finish_call(order, parts, first)
    return (row_grad, first_grad, logits.reshape(SAMPLES))


def solution(mesh):
    both = ("rep", "shard")
    in_specs = (
        P("shard", None),
        P(both, None),
        P(both, None, None),
        P(both, None),
        P(),
        P(both),
        P(),
        P(),
        P(),
        P(),
        P(),
        P(),
    )
    out_specs = (P("shard", None), P(), P(both))
    return jax.shard_map(body, mesh=mesh, in_specs=in_specs, out_specs=out_specs, check_vma=False)
```

```python
import functools

import jax
import jax.numpy as jnp
import numpy as np
from jax import lax
from jax.experimental import pallas as pl
from jax.experimental.pallas import tpu as pltpu
from jax.sharding import PartitionSpec as P

BF = jnp.bfloat16
F32 = jnp.float32
I32 = jnp.int32
OWNERS = 32
FEATS = 8
KEYS = OWNERS * FEATS
CAP = 512
VOC = 1024
ROWS = FEATS * VOC
EMB = 128
BAGS = 1024
SAMPLES = 128
WIDTH = FEATS * EMB
IDS = 8192
REPS = 4
PAIR = FEATS // REPS
LANES = 256
IDROWS = IDS // LANES
ACCS = 16
POOLED = 8
GROUP = 8
SOURCES = GROUP * REPS * PAIR * SAMPLES
SHIFT = 13
EARLY = 256
VMEM = 56 * 1024 * 1024

NT = (((1,), (1,)), ((), ()))
TN = (((0,), (0,)), ((), ()))


def dot(a, b, dims=(((1,), (0,)), ((), ()))):
    return lax.dot_general(a, b, dims, preferred_element_type=F32)


def iota(shape, dim):
    return lax.broadcasted_iota(I32, shape, dim)


def onehot(cond):
    return jnp.where(cond, 1.0, 0.0).astype(BF)


def index_kernel(
    ids_in, owner_in, len_in, slot_ref, out_ref, ids_ref, owner_ref, len_ref, bag_ref, key_ref
):
    for r in range(IDROWS):
        ids_ref[r : r + 1, :] = ids_in[:, r * LANES : (r + 1) * LANES]
        owner_ref[r : r + 1, :] = owner_in[:, r * LANES : (r + 1) * LANES]
    for r in range(BAGS // 128):
        len_ref[r : r + 1, :] = len_in[:, r * 128 : (r + 1) * 128]
    lens = len_ref[...].astype(F32).astype(BF)
    incl128 = onehot(iota((128, 128), 0) <= iota((128, 128), 1))
    within = dot(lens, incl128)
    total = jnp.broadcast_to(within[:, 127:128], (8, 128))
    high = jnp.floor(total * (1.0 / 256.0))
    low = total - high * 256.0
    below8 = onehot(iota((8, 8), 1) < iota((8, 8), 0))
    before = dot(below8, high.astype(BF)) * 256.0 + dot(below8, low.astype(BF))
    start = (within + before).astype(I32) - len_ref[...]
    start_hi = start >> 8
    start_lo = start & 255
    marks = jnp.zeros((IDROWS, LANES), F32)
    for r in range(8):
        a = onehot(iota((IDROWS, 128), 0) == start_hi[r : r + 1, :])
        b = onehot(iota((LANES, 128), 0) == start_lo[r : r + 1, :])
        marks = marks + dot(a, b, NT)
    marks = marks.astype(BF)
    incl = onehot(iota((LANES, LANES), 0) <= iota((LANES, LANES), 1))
    strict = onehot(iota((LANES, LANES), 0) < iota((LANES, LANES), 1))
    row_counts = dot(marks, jnp.ones((LANES, LANES), BF))
    below = onehot(iota((IDROWS, IDROWS), 1) < iota((IDROWS, IDROWS), 0))
    bag = (dot(marks, incl) + dot(below, row_counts.astype(BF))).astype(I32) - 1
    bag_ref[...] = bag
    key_ref[...] = owner_ref[...] * FEATS + (bag & (FEATS - 1))

    key_iota = iota((KEYS, LANES), 0)

    def count(r, acc):
        return acc + jnp.where(key_iota == key_ref[pl.ds(r, 1), :], 1.0, 0.0)

    counts = lax.fori_loop(0, IDROWS, count, jnp.zeros((KEYS, LANES), F32), unroll=4)
    totals = dot(counts.astype(BF), jnp.ones((LANES, LANES), BF))
    high = jnp.floor(totals * (1.0 / 256.0))
    low = totals - high * 256.0
    ki, kj = iota((KEYS, KEYS), 0), iota((KEYS, KEYS), 1)
    earlier = onehot((ki // FEATS == kj // FEATS) & (kj < ki))
    carry0 = dot(earlier, high.astype(BF)) * 256.0 + dot(earlier, low.astype(BF))

    rank_iota = iota((CAP, LANES), 0)
    owner_iota = iota((OWNERS, LANES), 0)

    of_owner = onehot(iota((KEYS, OWNERS), 0) // FEATS == iota((KEYS, OWNERS), 1))
    by_owner = dot(of_owner, slot_ref[...].astype(F32).astype(BF))
    is_feature = (iota((KEYS, FEATS), 0) & (FEATS - 1)) == iota((KEYS, FEATS), 1)
    slots = jnp.sum(jnp.where(is_feature, by_owner, 0.0), axis=1, keepdims=True)
    carry0 = carry0 + jnp.broadcast_to(slots, (KEYS, LANES)) * VOC

    def place(r, state):
        carry, acc = state
        same = key_iota == key_ref[pl.ds(r, 1), :]
        hot = jnp.where(same, 1.0, 0.0)
        prefix = dot(hot.astype(BF), strict)
        found = jnp.sum(jnp.where(same, prefix + carry, 0.0), axis=0, keepdims=True)
        found = found.astype(I32)
        rank = found & (VOC - 1)
        row = (found - rank) + ids_ref[pl.ds(r, 1), :]
        value = (1 << 23) + (row << 10) + bag_ref[pl.ds(r, 1), :]
        mine = owner_iota == owner_ref[pl.ds(r, 1), :]
        pieces = [
            jnp.where(mine, jnp.broadcast_to(p.astype(F32), (OWNERS, LANES)), 0.0)
            for p in (value & 255, (value >> 8) & 255, value >> 16)
        ]
        left = jnp.concatenate(pieces, axis=0).astype(BF)
        right = onehot(rank_iota == rank)
        acc = acc + dot(left, right, NT)
        carry = carry + (prefix + hot)[:, LANES - 1 : LANES]
        return carry, acc

    _, acc = lax.fori_loop(
        0, IDROWS, place, (carry0, jnp.zeros((3 * OWNERS, CAP), F32)), unroll=8
    )
    acc = acc.astype(I32)
    out_ref[...] = (
        acc[:OWNERS] + (acc[OWNERS : 2 * OWNERS] << 8) + (acc[2 * OWNERS :] << 16)
    )


def index_call(ids, owners, lengths, slots):
    return pl.pallas_call(
        index_kernel,
        out_shape=jax.ShapeDtypeStruct((OWNERS, CAP), I32),
        scratch_shapes=[
            pltpu.VMEM((IDROWS, LANES), I32),
            pltpu.VMEM((IDROWS, LANES), I32),
            pltpu.VMEM((BAGS // 128, 128), I32),
            pltpu.VMEM((IDROWS, LANES), I32),
            pltpu.VMEM((IDROWS, LANES), I32),
        ],
        compiler_params=pltpu.CompilerParams(vmem_limit_bytes=VMEM),
        name="index",
    )(ids, owners, lengths, slots)


def gather_kernel(row_ref, table_ref, out_ref, wide, picked):
    step = pl.program_id(0)
    depth = out_ref.shape[1]

    @pl.when(step == 0)
    def _():
        wide[...] = table_ref[...].astype(F32)

    base = step * depth

    def some(i, _):
        at = i * 32
        rows = [wide[pl.ds(row_ref[base + at + j], 1), :] for j in range(32)]
        for j in range(32):
            picked[pl.ds(at + j, 1), :] = rows[j]
        return 0

    lax.fori_loop(0, depth // 32, some, 0)
    out_ref[0] = picked[...].astype(BF)


def gather_call(rows, table):
    depth = rows.shape[1]
    return pl.pallas_call(
        gather_kernel,
        out_shape=jax.ShapeDtypeStruct((OWNERS, depth, EMB), BF),
        grid_spec=pltpu.PrefetchScalarGridSpec(
            num_scalar_prefetch=1,
            grid=(OWNERS,),
            in_specs=[pl.BlockSpec((ROWS, EMB), lambda i, r: (0, 0))],
            out_specs=pl.BlockSpec((1, depth, EMB), lambda i, r: (i, 0, 0)),
            scratch_shapes=[pltpu.VMEM((ROWS, EMB), F32), pltpu.VMEM((depth, EMB), F32)],
        ),
        compiler_params=pltpu.CompilerParams(vmem_limit_bytes=VMEM),
        name="gather",
    )(rows.reshape(-1), table)


def sums_of(packed_ref, got_ref, step, at):
    rows, masked = [], []
    depth = got_ref.shape[1]
    for i in range(POOLED):
        packed = packed_ref[pl.ds(step * POOLED + i, 1), at : at + depth]
        bag = packed & (BAGS - 1)
        sample = jnp.where(packed > 0, bag >> 3, -1)
        rows.append(onehot(iota((SAMPLES, depth), 0) == sample))
        feature = jnp.broadcast_to((bag & (FEATS - 1)).astype(F32), (EMB, depth)).T.astype(BF)
        own = got_ref[i]
        masked.append(
            jnp.concatenate(
                [jnp.where(feature == f, own, jnp.zeros((), BF)) for f in range(FEATS)], axis=1
            )
        )
    return dot(jnp.concatenate(rows, axis=1), jnp.concatenate(masked, axis=0))


def pool_kernel(at, got_ref, packed_ref, out_ref):
    step = pl.program_id(0)
    sums = sums_of(packed_ref, got_ref, step, at)

    @pl.when(step == 0)
    def _():
        out_ref[...] = sums

    @pl.when(step > 0)
    def _():
        out_ref[...] += sums


def pool_call(got, packed, at):
    depth = got.shape[1]
    return pl.pallas_call(
        functools.partial(pool_kernel, at),
        out_shape=jax.ShapeDtypeStruct((SAMPLES, WIDTH), F32),
        grid=(OWNERS // POOLED,),
        in_specs=[
            pl.BlockSpec((POOLED, depth, EMB), lambda i: (i, 0, 0)),
            pl.BlockSpec((OWNERS, CAP), lambda i: (0, 0)),
        ],
        out_specs=pl.BlockSpec((SAMPLES, WIDTH), lambda i: (0, 0)),
        compiler_params=pltpu.CompilerParams(vmem_limit_bytes=VMEM),
        name="pool",
    )(got, packed)


def sigmoid(x):
    return 1.0 / (1.0 + jnp.exp(-x))


def tower_kernel(
    at,
    got_ref,
    packed_ref,
    earlier_ref,
    labels_ref,
    gain_ref,
    cbias_ref,
    dbias_ref,
    out_w_ref,
    cross_hbm,
    deep_hbm,
    logits_ref,
    grads_ref,
    first_ref,
    pooled_ref,
    cross_w,
    deep_w,
    start_ref,
    cross_t,
    deep_t,
    gx_ref,
    sems,
):
    step = pl.program_id(0)

    def copies():
        out = []
        for layer in range(3):
            out.append(
                pltpu.make_async_copy(cross_hbm.at[layer], cross_w.at[layer], sems.at[layer])
            )
            out.append(
                pltpu.make_async_copy(deep_hbm.at[layer], deep_w.at[layer], sems.at[3 + layer])
            )
        return out

    @pl.when(step == 0)
    def _():
        for copy in copies():
            copy.start()
        pooled_ref[...] = earlier_ref[...]

    pooled_ref[...] += sums_of(packed_ref, got_ref, step, at)

    @pl.when(step == OWNERS // POOLED - 1)
    def _():
        for copy in copies():
            copy.wait()
        gain = gain_ref[...]
        pooled = pooled_ref[...]
        inverse = lax.rsqrt(jnp.mean(pooled * pooled, axis=1, keepdims=True) + 1e-06)
        start = (pooled * inverse * gain).astype(BF)
        start_ref[...] = start
        current = start
        for layer in range(3):
            product = dot(current, cross_w[layer]) + cbias_ref[layer : layer + 1, :]
            cross_t[layer] = product
            current = (start_ref[...].astype(F32) * product + current.astype(F32)).astype(BF)
        for layer in range(3):
            product = dot(current, deep_w[layer]) + dbias_ref[layer : layer + 1, :]
            deep_t[layer] = product
            current = (product * sigmoid(product)).astype(BF)
        out_w = out_w_ref[...]
        logits = jnp.sum(current.astype(F32) * out_w, axis=1, keepdims=True)
        logits_ref[...] = logits
        error = sigmoid(logits) - labels_ref[...].astype(F32)
        grad = error * out_w
        for layer in (2, 1, 0):
            product = deep_t[layer]
            sig = sigmoid(product)
            masked = (grad * sig * (1.0 + product * (1.0 - sig))).astype(BF)
            grad = dot(masked, deep_w[layer], NT)
        gx_ref[...] = jnp.zeros_like(gx_ref)
        for layer in (2, 1, 0):
            crossed = (grad * start_ref[...].astype(F32)).astype(BF)
            gx_ref[...] += grad * cross_t[layer]
            grad = grad + dot(crossed, cross_w[layer], NT)
            if layer == 0:
                first_ref[...] = dot(start_ref[...], crossed, TN).astype(BF)
        scaled = (gx_ref[...] + grad) * gain
        pooled = pooled_ref[...]
        inverse = lax.rsqrt(jnp.mean(pooled * pooled, axis=1, keepdims=True) + 1e-06)
        mean = jnp.mean(scaled * pooled, axis=1, keepdims=True)
        result = (inverse * scaled - pooled * (inverse * inverse * inverse) * mean).astype(BF)
        for r in range(REPS):
            grads_ref[r] = result[:, r * PAIR * EMB : (r + 1) * PAIR * EMB]


def tower_call(got, packed, earlier, labels, gain, cross, cbias, deep, dbias, out_w):
    def whole(shape):
        return pl.BlockSpec(shape, lambda i: (0,) * len(shape))

    return pl.pallas_call(
        functools.partial(tower_kernel, CAP - got.shape[1]),
        grid=(OWNERS // POOLED,),
        in_specs=[
            pl.BlockSpec((POOLED, got.shape[1], EMB), lambda i: (i, 0, 0)),
            whole((OWNERS, CAP)),
            whole((SAMPLES, WIDTH)),
            whole((SAMPLES, 1)),
            whole((1, WIDTH)),
            whole((3, WIDTH)),
            whole((3, WIDTH)),
            whole((1, WIDTH)),
            pl.BlockSpec(memory_space=pl.ANY),
            pl.BlockSpec(memory_space=pl.ANY),
        ],
        out_specs=[
            whole((SAMPLES, 1)),
            whole((REPS, SAMPLES, PAIR * EMB)),
            whole((WIDTH, WIDTH)),
        ],
        out_shape=[
            jax.ShapeDtypeStruct((SAMPLES, 1), F32),
            jax.ShapeDtypeStruct((REPS, SAMPLES, PAIR * EMB), BF),
            jax.ShapeDtypeStruct((WIDTH, WIDTH), BF),
        ],
        scratch_shapes=[
            pltpu.VMEM((SAMPLES, WIDTH), F32),
            pltpu.VMEM((3, WIDTH, WIDTH), BF),
            pltpu.VMEM((3, WIDTH, WIDTH), BF),
            pltpu.VMEM((SAMPLES, WIDTH), BF),
            pltpu.VMEM((3, SAMPLES, WIDTH), F32),
            pltpu.VMEM((3, SAMPLES, WIDTH), F32),
            pltpu.VMEM((SAMPLES, WIDTH), F32),
            pltpu.SemaphoreType.DMA((6,)),
        ],
        compiler_params=pltpu.CompilerParams(vmem_limit_bytes=VMEM),
        name="tower",
    )(got, packed, earlier, labels, gain, cbias, dbias, out_w, cross, deep)


def scatter_kernel(word_ref, first_ref, last_ref, grads_ref, out_ref, wide, *accs):
    step = pl.program_id(0)

    @pl.when(step == 0)
    def _():
        for acc in accs:
            acc[...] = jnp.zeros_like(acc)

    group = grads_ref.shape[0]
    for g in range(group):
        for r in range(REPS):
            block = grads_ref[g, r]
            base = (g * REPS + r) * PAIR * SAMPLES
            for f in range(PAIR):
                wide[base + f * SAMPLES : base + (f + 1) * SAMPLES, :] = block[
                    :, f * EMB : (f + 1) * EMB
                ].astype(F32)

    def device(k, _):
        listed = (k & (REPS - 1)) * OWNERS + step * group + k // REPS

        def some(i, _):
            at = listed * CAP + i * ACCS
            words = [word_ref[at + j] for j in range(ACCS)]
            rows = [wide[pl.ds(word & (SOURCES - 1), 1), :] for word in words]
            olds = [accs[j][pl.ds(words[j] >> SHIFT, 1), :] for j in range(ACCS)]
            for j in range(ACCS):
                accs[j][pl.ds(words[j] >> SHIFT, 1), :] = olds[j] + rows[j]
            return 0

        lax.fori_loop(first_ref[listed], last_ref[listed], some, 0)
        return 0

    lax.fori_loop(0, group * REPS, device, 0)

    @pl.when(step == pl.num_programs(0) - 1)
    def _():
        total = accs[0][: PAIR * VOC, :]
        for acc in accs[1:]:
            total = total + acc[: PAIR * VOC, :]
        out_ref[...] = total.astype(out_ref.dtype)


def scatter_call(words, first, last, grads, group=GROUP):
    rows = PAIR * VOC
    return pl.pallas_call(
        scatter_kernel,
        out_shape=jax.ShapeDtypeStruct((rows, EMB), BF),
        grid_spec=pltpu.PrefetchScalarGridSpec(
            num_scalar_prefetch=3,
            grid=(OWNERS // group,),
            in_specs=[
                pl.BlockSpec(
                    (group, REPS, SAMPLES, PAIR * EMB), lambda i, *_: (i, 0, 0, 0)
                )
            ],
            out_specs=pl.BlockSpec((rows, EMB), lambda i, *_: (0, 0)),
            scratch_shapes=[pltpu.VMEM((group * REPS * PAIR * SAMPLES, EMB), F32)]
            + [pltpu.VMEM((rows + 8, EMB), F32) for _ in range(ACCS)],
        ),
        compiler_params=pltpu.CompilerParams(vmem_limit_bytes=VMEM),
        name="scatter",
    )(words, first, last, grads)


def finish_kernel(order_ref, *refs):
    parts, rows_ref = refs[:REPS], refs[REPS]
    source = order_ref[pl.program_id(0)]
    for k in range(REPS):

        @pl.when(source // PAIR == k)
        def _():
            rows_ref[...] = parts[k][lax.rem(source, PAIR)].astype(F32)


def finish_call(order, parts):
    return pl.pallas_call(
        finish_kernel,
        out_shape=jax.ShapeDtypeStruct((ROWS, EMB), F32),
        grid_spec=pltpu.PrefetchScalarGridSpec(
            num_scalar_prefetch=1,
            grid=(FEATS,),
            in_specs=[pl.BlockSpec((PAIR, VOC, EMB), lambda i, o: (0, 0, 0)) for _ in parts],
            out_specs=pl.BlockSpec((VOC, EMB), lambda i, o: (i, 0)),
        ),
        compiler_params=pltpu.CompilerParams(vmem_limit_bytes=VMEM),
        name="finish",
    )(order, *parts)


def from_before(x, axis, k):
    if k == 0:
        return x
    n = lax.axis_size(axis)
    return lax.ppermute(x, axis, [(i, (i + k) % n) for i in range(n)])


def summed(x):
    return jnp.sum(x.astype(F32), axis=0).astype(BF)


def body(
    embed_table,
    row_ids,
    row_owner,
    lengths,
    feature_slot,
    labels,
    norm_gain,
    cross_weight,
    cross_bias,
    deep_weight,
    deep_bias,
    out_weight,
):
    packed = index_call(
        row_ids,
        row_owner.reshape(1, IDS),
        lengths,
        feature_slot,
    )
    asked = lax.all_to_all(
        packed.reshape(OWNERS, 4, 128), "shard", split_axis=0, concat_axis=0, tiled=True
    )
    rows = ((asked >> 10) & (ROWS - 1)).reshape(OWNERS, CAP)

    def exchange(x, axis):
        return lax.all_to_all(x, axis, split_axis=0, concat_axis=0, tiled=True)

    picked_early = gather_call(rows[:, :EARLY], embed_table)
    picked_early, lists = lax.optimization_barrier((picked_early, asked))
    got_early = exchange(picked_early, "shard")
    picked_late, lists = lax.optimization_barrier(
        (gather_call(rows[:, EARLY:], embed_table), lists)
    )
    got_late = exchange(picked_late, "shard")

    rep = lax.axis_index("rep")
    everyone = jnp.concatenate(
        [lists] + [from_before(lists, "rep", k) for k in range(1, REPS)]
    ).reshape(REPS * OWNERS, CAP)
    feature = everyone & (FEATS - 1)
    valid = everyone > 0
    within = feature - rep * PAIR
    ours = valid & (within >= 0) & (within < PAIR)
    target = jnp.where(ours, within * VOC + ((everyone >> 10) & (VOC - 1)), PAIR * VOC)
    device = lax.broadcasted_iota(I32, everyone.shape, 0)
    source = ((device & (GROUP - 1)) * REPS + device // OWNERS) * (PAIR * SAMPLES) + jnp.where(
        ours, within * SAMPLES + ((everyone >> 3) & (SAMPLES - 1)), 0
    )
    words = ((target << SHIFT) | source).reshape(-1)
    below = jnp.sum((valid & (within < 0)).astype(I32), axis=1)
    upto = jnp.sum((valid & (within < PAIR)).astype(I32), axis=1)
    first_block = below // ACCS
    last_block = (upto + ACCS - 1) // ACCS
    sums_early = pool_call(got_early, packed, 0)
    got_late, sums_early, words, first_block, last_block = lax.optimization_barrier(
        (got_late, sums_early, words, first_block, last_block)
    )

    logits, grads, first_local = tower_call(
        got_late,
        packed,
        sums_early,
        labels.reshape(SAMPLES, 1),
        norm_gain.reshape(1, WIDTH),
        cross_weight,
        cross_bias,
        deep_weight,
        deep_bias,
        out_weight.reshape(1, WIDTH),
    )
    mine = jnp.stack(
        [
            from_before(lax.dynamic_index_in_dim(grads, (rep + k) % REPS, 0, False), "rep", k)
            for k in range(REPS)
        ]
    )
    mine, first_local = lax.optimization_barrier((mine, first_local))
    all_grads = lax.all_gather(mine, "shard", axis=0)
    eight = summed(
        exchange(first_local.reshape(REPS * OWNERS, 8, WIDTH), ("rep", "shard"))
    )
    first_grad = lax.all_gather(eight, ("rep", "shard"), axis=0, tiled=True).astype(F32)

    part = scatter_call(words, first_block, last_block, all_grads).reshape(PAIR, VOC, EMB)
    parts = [part] + [from_before(part, "rep", k) for k in range(1, REPS)]
    slots = feature_slot[lax.axis_index("shard")]
    feature_of = jnp.argmax(
        slots[None, :] == jnp.arange(FEATS, dtype=I32)[:, None], axis=1
    ).astype(I32)
    order = ((rep - feature_of // PAIR) & (REPS - 1)) * PAIR + feature_of % PAIR
    row_grad = finish_call(order, parts)
    return (row_grad, first_grad, logits.reshape(SAMPLES))


def solution(mesh):
    both = ("rep", "shard")
    in_specs = (
        P("shard", None),
        P(both, None),
        P(both, None, None),
        P(both, None),
        P(),
        P(both),
        P(),
        P(),
        P(),
        P(),
        P(),
        P(),
    )
    out_specs = (P("shard", None), P(), P(both))
    return jax.shard_map(body, mesh=mesh, in_specs=in_specs, out_specs=out_specs, check_vma=False)
```

```python
import functools

import jax
import jax.numpy as jnp
import numpy as np
from jax import lax
from jax.experimental import pallas as pl
from jax.experimental.pallas import tpu as pltpu
from jax.sharding import PartitionSpec as P

BF = jnp.bfloat16
F32 = jnp.float32
I32 = jnp.int32
OWNERS = 32
FEATS = 8
KEYS = OWNERS * FEATS
CAP = 512
VOC = 1024
ROWS = FEATS * VOC
EMB = 128
BAGS = 1024
SAMPLES = 128
WIDTH = FEATS * EMB
IDS = 8192
REPS = 4
PAIR = FEATS // REPS
LANES = 256
IDROWS = IDS // LANES
ACCS = 16
POOLED = 8
GROUP = 4
LISTED = CAP + 64
LISTS = 4
SOURCES = GROUP * REPS * PAIR * SAMPLES
SHIFT = 13
EARLY = 256
VMEM = 56 * 1024 * 1024

NT = (((1,), (1,)), ((), ()))
TN = (((0,), (0,)), ((), ()))


def dot(a, b, dims=(((1,), (0,)), ((), ()))):
    return lax.dot_general(a, b, dims, preferred_element_type=F32)


def iota(shape, dim):
    return lax.broadcasted_iota(I32, shape, dim)


def onehot(cond):
    return jnp.where(cond, 1.0, 0.0).astype(BF)


def index_kernel(
    ids_in, owner_in, len_in, slot_ref, out_ref, ids_ref, owner_ref, len_ref, bag_ref, key_ref
):
    for r in range(IDROWS):
        ids_ref[r : r + 1, :] = ids_in[:, r * LANES : (r + 1) * LANES]
        owner_ref[r : r + 1, :] = owner_in[:, r * LANES : (r + 1) * LANES]
    for r in range(BAGS // 128):
        len_ref[r : r + 1, :] = len_in[:, r * 128 : (r + 1) * 128]
    lens = len_ref[...].astype(F32).astype(BF)
    incl128 = onehot(iota((128, 128), 0) <= iota((128, 128), 1))
    within = dot(lens, incl128)
    total = jnp.broadcast_to(within[:, 127:128], (8, 128))
    high = jnp.floor(total * (1.0 / 256.0))
    low = total - high * 256.0
    below8 = onehot(iota((8, 8), 1) < iota((8, 8), 0))
    before = dot(below8, high.astype(BF)) * 256.0 + dot(below8, low.astype(BF))
    start = (within + before).astype(I32) - len_ref[...]
    start_hi = start >> 8
    start_lo = start & 255
    marks = jnp.zeros((IDROWS, LANES), F32)
    for r in range(8):
        a = onehot(iota((IDROWS, 128), 0) == start_hi[r : r + 1, :])
        b = onehot(iota((LANES, 128), 0) == start_lo[r : r + 1, :])
        marks = marks + dot(a, b, NT)
    marks = marks.astype(BF)
    incl = onehot(iota((LANES, LANES), 0) <= iota((LANES, LANES), 1))
    strict = onehot(iota((LANES, LANES), 0) < iota((LANES, LANES), 1))
    row_counts = dot(marks, jnp.ones((LANES, LANES), BF))
    below = onehot(iota((IDROWS, IDROWS), 1) < iota((IDROWS, IDROWS), 0))
    bag = (dot(marks, incl) + dot(below, row_counts.astype(BF))).astype(I32) - 1
    bag_ref[...] = bag
    key_ref[...] = owner_ref[...] * FEATS + (bag & (FEATS - 1))

    key_iota = iota((KEYS, LANES), 0)

    def count(r, acc):
        return acc + jnp.where(key_iota == key_ref[pl.ds(r, 1), :], 1.0, 0.0)

    counts = lax.fori_loop(0, IDROWS, count, jnp.zeros((KEYS, LANES), F32), unroll=4)
    totals = dot(counts.astype(BF), jnp.ones((LANES, LANES), BF))
    high = jnp.floor(totals * (1.0 / 256.0))
    low = totals - high * 256.0
    ki, kj = iota((KEYS, KEYS), 0), iota((KEYS, KEYS), 1)
    earlier = onehot((ki // FEATS == kj // FEATS) & (kj < ki))
    carry0 = dot(earlier, high.astype(BF)) * 256.0 + dot(earlier, low.astype(BF))

    rank_iota = iota((CAP, LANES), 0)
    owner_iota = iota((OWNERS, LANES), 0)

    of_owner = onehot(iota((KEYS, OWNERS), 0) // FEATS == iota((KEYS, OWNERS), 1))
    by_owner = dot(of_owner, slot_ref[...].astype(F32).astype(BF))
    is_feature = (iota((KEYS, FEATS), 0) & (FEATS - 1)) == iota((KEYS, FEATS), 1)
    slots = jnp.sum(jnp.where(is_feature, by_owner, 0.0), axis=1, keepdims=True)
    carry0 = carry0 + jnp.broadcast_to(slots, (KEYS, LANES)) * VOC

    def place(r, state):
        carry, acc = state
        same = key_iota == key_ref[pl.ds(r, 1), :]
        hot = jnp.where(same, 1.0, 0.0)
        prefix = dot(hot.astype(BF), strict)
        found = jnp.sum(jnp.where(same, prefix + carry, 0.0), axis=0, keepdims=True)
        found = found.astype(I32)
        rank = found & (VOC - 1)
        row = (found - rank) + ids_ref[pl.ds(r, 1), :]
        value = (1 << 23) + (row << 10) + bag_ref[pl.ds(r, 1), :]
        mine = owner_iota == owner_ref[pl.ds(r, 1), :]
        pieces = [
            jnp.where(mine, jnp.broadcast_to(p.astype(F32), (OWNERS, LANES)), 0.0)
            for p in (value & 255, (value >> 8) & 255, value >> 16)
        ]
        left = jnp.concatenate(pieces, axis=0).astype(BF)
        right = onehot(rank_iota == rank)
        acc = acc + dot(left, right, NT)
        carry = carry + (prefix + hot)[:, LANES - 1 : LANES]
        return carry, acc

    _, acc = lax.fori_loop(
        0, IDROWS, place, (carry0, jnp.zeros((3 * OWNERS, CAP), F32)), unroll=8
    )
    acc = acc.astype(I32)
    out_ref[...] = (
        acc[:OWNERS] + (acc[OWNERS : 2 * OWNERS] << 8) + (acc[2 * OWNERS :] << 16)
    )


def index_call(ids, owners, lengths, slots):
    return pl.pallas_call(
        index_kernel,
        out_shape=jax.ShapeDtypeStruct((OWNERS, CAP), I32),
        scratch_shapes=[
            pltpu.VMEM((IDROWS, LANES), I32),
            pltpu.VMEM((IDROWS, LANES), I32),
            pltpu.VMEM((BAGS // 128, 128), I32),
            pltpu.VMEM((IDROWS, LANES), I32),
            pltpu.VMEM((IDROWS, LANES), I32),
        ],
        compiler_params=pltpu.CompilerParams(vmem_limit_bytes=VMEM),
        name="index",
    )(ids, owners, lengths, slots)


def gather_kernel(row_ref, table_ref, out_ref, wide, picked):
    step = pl.program_id(0)
    depth = out_ref.shape[1]

    @pl.when(step == 0)
    def _():
        wide[...] = table_ref[...].astype(F32)

    for part in range(LISTS):
        base = (step * LISTS + part) * depth

        def some(i, _):
            at = i * 32
            rows = [wide[pl.ds(row_ref[base + at + j], 1), :] for j in range(32)]
            for j in range(32):
                picked[pl.ds(part * depth + at + j, 1), :] = rows[j]
            return 0

        lax.fori_loop(0, depth // 32, some, 0)
        out_ref[part] = picked[part * depth : (part + 1) * depth, :].astype(BF)


def gather_call(rows, table):
    depth = rows.shape[1]
    return pl.pallas_call(
        gather_kernel,
        out_shape=jax.ShapeDtypeStruct((OWNERS, depth, EMB), BF),
        grid_spec=pltpu.PrefetchScalarGridSpec(
            num_scalar_prefetch=1,
            grid=(OWNERS // LISTS,),
            in_specs=[pl.BlockSpec((ROWS, EMB), lambda i, r: (0, 0))],
            out_specs=pl.BlockSpec((LISTS, depth, EMB), lambda i, r: (i, 0, 0)),
            scratch_shapes=[pltpu.VMEM((ROWS, EMB), F32), pltpu.VMEM((LISTS * depth, EMB), F32)],
        ),
        compiler_params=pltpu.CompilerParams(vmem_limit_bytes=VMEM),
        name="gather",
    )(rows.reshape(-1), table)


def sums_of(packed_ref, got_ref, step, at):
    rows, masked = [], []
    depth = got_ref.shape[1]
    for i in range(POOLED):
        packed = packed_ref[pl.ds(step * POOLED + i, 1), at : at + depth]
        bag = packed & (BAGS - 1)
        sample = jnp.where(packed > 0, bag >> 3, -1)
        rows.append(onehot(iota((SAMPLES, depth), 0) == sample))
        feature = jnp.broadcast_to((bag & (FEATS - 1)).astype(F32), (EMB, depth)).T.astype(BF)
        own = got_ref[i]
        masked.append(
            jnp.concatenate(
                [jnp.where(feature == f, own, jnp.zeros((), BF)) for f in range(FEATS)], axis=1
            )
        )
    return dot(jnp.concatenate(rows, axis=1), jnp.concatenate(masked, axis=0))


def pool_kernel(at, got_ref, packed_ref, out_ref):
    step = pl.program_id(0)
    sums = sums_of(packed_ref, got_ref, step, at)

    @pl.when(step == 0)
    def _():
        out_ref[...] = sums

    @pl.when(step > 0)
    def _():
        out_ref[...] += sums


def pool_call(got, packed, at):
    depth = got.shape[1]
    return pl.pallas_call(
        functools.partial(pool_kernel, at),
        out_shape=jax.ShapeDtypeStruct((SAMPLES, WIDTH), F32),
        grid=(OWNERS // POOLED,),
        in_specs=[
            pl.BlockSpec((POOLED, depth, EMB), lambda i: (i, 0, 0)),
            pl.BlockSpec((OWNERS, CAP), lambda i: (0, 0)),
        ],
        out_specs=pl.BlockSpec((SAMPLES, WIDTH), lambda i: (0, 0)),
        compiler_params=pltpu.CompilerParams(vmem_limit_bytes=VMEM),
        name="pool",
    )(got, packed)


def sigmoid(x):
    return 1.0 / (1.0 + jnp.exp(-x))


def tower_kernel(
    at,
    got_ref,
    packed_ref,
    earlier_ref,
    labels_ref,
    gain_ref,
    cbias_ref,
    dbias_ref,
    out_w_ref,
    cross_hbm,
    deep_hbm,
    logits_ref,
    grads_ref,
    first_ref,
    pooled_ref,
    cross_w,
    deep_w,
    start_ref,
    cross_t,
    deep_t,
    gx_ref,
    sems,
):
    step = pl.program_id(0)

    def copies():
        out = []
        for layer in range(3):
            out.append(
                pltpu.make_async_copy(cross_hbm.at[layer], cross_w.at[layer], sems.at[layer])
            )
            out.append(
                pltpu.make_async_copy(deep_hbm.at[layer], deep_w.at[layer], sems.at[3 + layer])
            )
        return out

    @pl.when(step == 0)
    def _():
        for copy in copies():
            copy.start()
        pooled_ref[...] = earlier_ref[...]

    pooled_ref[...] += sums_of(packed_ref, got_ref, step, at)

    @pl.when(step == OWNERS // POOLED - 1)
    def _():
        for copy in copies():
            copy.wait()
        gain = gain_ref[...]
        pooled = pooled_ref[...]
        inverse = lax.rsqrt(jnp.mean(pooled * pooled, axis=1, keepdims=True) + 1e-06)
        start = (pooled * inverse * gain).astype(BF)
        start_ref[...] = start
        current = start
        for layer in range(3):
            product = dot(current, cross_w[layer]) + cbias_ref[layer : layer + 1, :]
            cross_t[layer] = product
            current = (start_ref[...].astype(F32) * product + current.astype(F32)).astype(BF)
        for layer in range(3):
            product = dot(current, deep_w[layer]) + dbias_ref[layer : layer + 1, :]
            deep_t[layer] = product
            current = (product * sigmoid(product)).astype(BF)
        out_w = out_w_ref[...]
        logits = jnp.sum(current.astype(F32) * out_w, axis=1, keepdims=True)
        logits_ref[...] = logits
        error = sigmoid(logits) - labels_ref[...].astype(F32)
        grad = error * out_w
        for layer in (2, 1, 0):
            product = deep_t[layer]
            sig = sigmoid(product)
            masked = (grad * sig * (1.0 + product * (1.0 - sig))).astype(BF)
            grad = dot(masked, deep_w[layer], NT)
        gx_ref[...] = jnp.zeros_like(gx_ref)
        for layer in (2, 1, 0):
            crossed = (grad * start_ref[...].astype(F32)).astype(BF)
            gx_ref[...] += grad * cross_t[layer]
            grad = grad + dot(crossed, cross_w[layer], NT)
            if layer == 0:
                outer = dot(start_ref[...], crossed, TN).reshape(OWNERS, REPS, 8, WIDTH)
                for r in range(REPS):
                    first_ref[r] = outer[:, r].reshape(OWNERS * 8, WIDTH).astype(BF)
        scaled = (gx_ref[...] + grad) * gain
        pooled = pooled_ref[...]
        inverse = lax.rsqrt(jnp.mean(pooled * pooled, axis=1, keepdims=True) + 1e-06)
        mean = jnp.mean(scaled * pooled, axis=1, keepdims=True)
        result = (inverse * scaled - pooled * (inverse * inverse * inverse) * mean).astype(BF)
        for r in range(REPS):
            grads_ref[r] = result[:, r * PAIR * EMB : (r + 1) * PAIR * EMB]


def tower_call(got, packed, earlier, labels, gain, cross, cbias, deep, dbias, out_w):
    def whole(shape):
        return pl.BlockSpec(shape, lambda i: (0,) * len(shape))

    return pl.pallas_call(
        functools.partial(tower_kernel, CAP - got.shape[1]),
        grid=(OWNERS // POOLED,),
        in_specs=[
            pl.BlockSpec((POOLED, got.shape[1], EMB), lambda i: (i, 0, 0)),
            whole((OWNERS, CAP)),
            whole((SAMPLES, WIDTH)),
            whole((SAMPLES, 1)),
            whole((1, WIDTH)),
            whole((3, WIDTH)),
            whole((3, WIDTH)),
            whole((1, WIDTH)),
            pl.BlockSpec(memory_space=pl.ANY),
            pl.BlockSpec(memory_space=pl.ANY),
        ],
        out_specs=[
            whole((SAMPLES, 1)),
            whole((REPS, SAMPLES, PAIR * EMB)),
            whole((REPS, OWNERS * 8, WIDTH)),
        ],
        out_shape=[
            jax.ShapeDtypeStruct((SAMPLES, 1), F32),
            jax.ShapeDtypeStruct((REPS, SAMPLES, PAIR * EMB), BF),
            jax.ShapeDtypeStruct((REPS, OWNERS * 8, WIDTH), BF),
        ],
        scratch_shapes=[
            pltpu.VMEM((SAMPLES, WIDTH), F32),
            pltpu.VMEM((3, WIDTH, WIDTH), BF),
            pltpu.VMEM((3, WIDTH, WIDTH), BF),
            pltpu.VMEM((SAMPLES, WIDTH), BF),
            pltpu.VMEM((3, SAMPLES, WIDTH), F32),
            pltpu.VMEM((3, SAMPLES, WIDTH), F32),
            pltpu.VMEM((SAMPLES, WIDTH), F32),
            pltpu.SemaphoreType.DMA((6,)),
        ],
        compiler_params=pltpu.CompilerParams(vmem_limit_bytes=VMEM),
        name="tower",
    )(got, packed, earlier, labels, gain, cbias, dbias, out_w, cross, deep)


def scatter_kernel(first_ref, last_ref, word_ref, grads_ref, out_ref, wide, *accs):
    step = pl.program_id(0)

    @pl.when(step == 0)
    def _():
        for acc in accs:
            acc[...] = jnp.zeros_like(acc)

    group = grads_ref.shape[0]
    for g in range(group):
        for r in range(REPS):
            block = grads_ref[g, r]
            base = (g * REPS + r) * PAIR * SAMPLES
            for f in range(PAIR):
                wide[base + f * SAMPLES : base + (f + 1) * SAMPLES, :] = block[
                    :, f * EMB : (f + 1) * EMB
                ].astype(F32)

    def device(k, _):
        listed = step * group * REPS + k
        first = first_ref[listed]

        def some(i, _):
            at = k * LISTED + first + i * ACCS
            words = [word_ref[at + j] for j in range(ACCS)]
            rows = [wide[pl.ds(word & (SOURCES - 1), 1), :] for word in words]
            olds = [accs[j][pl.ds(words[j] >> SHIFT, 1), :] for j in range(ACCS)]
            for j in range(ACCS):
                accs[j][pl.ds(words[j] >> SHIFT, 1), :] = olds[j] + rows[j]
            return 0

        lax.fori_loop(0, (last_ref[listed] - first + ACCS - 1) // ACCS, some, 0)
        return 0

    lax.fori_loop(0, group * REPS, device, 0)

    @pl.when(step == pl.num_programs(0) - 1)
    def _():
        total = accs[0][: PAIR * VOC, :]
        for acc in accs[1:]:
            total = total + acc[: PAIR * VOC, :]
        out_ref[...] = total.astype(out_ref.dtype)


def scatter_call(words, first, last, grads, group=GROUP):
    rows = PAIR * VOC
    return pl.pallas_call(
        scatter_kernel,
        out_shape=jax.ShapeDtypeStruct((rows, EMB), BF),
        grid_spec=pltpu.PrefetchScalarGridSpec(
            num_scalar_prefetch=2,
            grid=(OWNERS // group,),
            in_specs=[
                pl.BlockSpec(
                    (group * REPS * LISTED,), lambda i, *_: (i,), memory_space=pltpu.SMEM
                ),
                pl.BlockSpec(
                    (group, REPS, SAMPLES, PAIR * EMB), lambda i, *_: (i, 0, 0, 0)
                ),
            ],
            out_specs=pl.BlockSpec((rows, EMB), lambda i, *_: (0, 0)),
            scratch_shapes=[pltpu.VMEM((group * REPS * PAIR * SAMPLES, EMB), F32)]
            + [pltpu.VMEM((rows + 8, EMB), F32) for _ in range(ACCS)],
        ),
        compiler_params=pltpu.CompilerParams(vmem_limit_bytes=VMEM),
        name="scatter",
    )(first, last, words, grads)


def finish_kernel(order_ref, *refs):
    parts, rows_ref = refs[:REPS], refs[REPS]
    source = order_ref[pl.program_id(0)]
    for k in range(REPS):

        @pl.when(source // PAIR == k)
        def _():
            rows_ref[...] = parts[k][lax.rem(source, PAIR)].astype(F32)


def finish_call(order, parts):
    return pl.pallas_call(
        finish_kernel,
        out_shape=jax.ShapeDtypeStruct((ROWS, EMB), F32),
        grid_spec=pltpu.PrefetchScalarGridSpec(
            num_scalar_prefetch=1,
            grid=(FEATS,),
            in_specs=[pl.BlockSpec((PAIR, VOC, EMB), lambda i, o: (0, 0, 0)) for _ in parts],
            out_specs=pl.BlockSpec((VOC, EMB), lambda i, o: (i, 0)),
        ),
        compiler_params=pltpu.CompilerParams(vmem_limit_bytes=VMEM),
        name="finish",
    )(order, *parts)


def from_before(x, axis, k):
    if k == 0:
        return x
    n = lax.axis_size(axis)
    return lax.ppermute(x, axis, [(i, (i + k) % n) for i in range(n)])


def in_order(x, axis, me):
    n = lax.axis_size(axis)
    back = [from_before(x, axis, k) for k in range(n)]
    twice = jnp.concatenate([back[(n - 1 - i) % n] for i in range(2 * n - 1)])
    return lax.dynamic_slice_in_dim(twice, (n - 1 - me) * x.shape[0], n * x.shape[0])


def summed(x):
    return jnp.sum(x.astype(F32), axis=0).astype(BF)


def body(
    embed_table,
    row_ids,
    row_owner,
    lengths,
    feature_slot,
    labels,
    norm_gain,
    cross_weight,
    cross_bias,
    deep_weight,
    deep_bias,
    out_weight,
):
    packed = index_call(
        row_ids,
        row_owner.reshape(1, IDS),
        lengths,
        feature_slot,
    )
    asked = lax.all_to_all(
        packed.reshape(OWNERS, 4, 128), "shard", split_axis=0, concat_axis=0, tiled=True
    )
    rows = ((asked >> 10) & (ROWS - 1)).reshape(OWNERS, CAP)

    def exchange(x, axis):
        return lax.all_to_all(x, axis, split_axis=0, concat_axis=0, tiled=True)

    picked_early = gather_call(rows[:, :EARLY], embed_table)
    picked_early, lists = lax.optimization_barrier((picked_early, asked))
    got_early = exchange(picked_early, "shard")
    picked_late, lists = lax.optimization_barrier(
        (gather_call(rows[:, EARLY:], embed_table), lists)
    )
    got_late = exchange(picked_late, "shard")

    rep = lax.axis_index("rep")
    everyone = jnp.stack(
        [
            from_before(lists, "rep", k).reshape(OWNERS // GROUP, GROUP, CAP)
            for k in range(REPS)
        ],
        axis=2,
    )
    feature = everyone & (FEATS - 1)
    valid = everyone > 0
    within = feature - rep * PAIR
    ours = valid & (within >= 0) & (within < PAIR)
    target = jnp.where(ours, within * VOC + ((everyone >> 10) & (VOC - 1)), PAIR * VOC)
    group = lax.broadcasted_iota(I32, everyone.shape, 1)
    back = lax.broadcasted_iota(I32, everyone.shape, 2)
    source = (group * REPS + back) * (PAIR * SAMPLES) + jnp.where(
        ours, within * SAMPLES + ((everyone >> 3) & (SAMPLES - 1)), 0
    )
    words = jnp.pad(
        (target << SHIFT) | source,
        ((0, 0), (0, 0), (0, 0), (0, LISTED - CAP)),
        constant_values=(PAIR * VOC) << SHIFT,
    ).reshape(-1)
    first_word = jnp.sum((valid & (within < 0)).astype(I32), axis=3).reshape(-1)
    last_word = jnp.sum((valid & (within < PAIR)).astype(I32), axis=3).reshape(-1)
    sums_early = pool_call(got_early, packed, 0)
    got_late, sums_early, words, first_word, last_word = lax.optimization_barrier(
        (got_late, sums_early, words, first_word, last_word)
    )

    logits, grads, first_local = tower_call(
        got_late,
        packed,
        sums_early,
        labels.reshape(SAMPLES, 1),
        norm_gain.reshape(1, WIDTH),
        cross_weight,
        cross_bias,
        deep_weight,
        deep_bias,
        out_weight.reshape(1, WIDTH),
    )
    mine = jnp.stack(
        [
            from_before(lax.dynamic_index_in_dim(grads, (rep + k) % REPS, 0, False), "rep", k)
            for k in range(REPS)
        ]
    )
    mine, first_local = lax.optimization_barrier((mine, first_local))
    all_grads = lax.all_gather(mine, "shard", axis=0)
    quarter = summed(exchange(first_local, "rep"))
    eight = summed(exchange(quarter.reshape(OWNERS, 8, WIDTH), "shard"))
    first_grad = lax.all_gather(
        in_order(eight, "rep", rep), "shard", axis=0, tiled=True
    ).astype(F32)

    part = scatter_call(words, first_word, last_word, all_grads).reshape(PAIR, VOC, EMB)
    parts = [part] + [from_before(part, "rep", k) for k in range(1, REPS)]
    slots = feature_slot[lax.axis_index("shard")]
    feature_of = jnp.argmax(
        slots[None, :] == jnp.arange(FEATS, dtype=I32)[:, None], axis=1
    ).astype(I32)
    order = ((rep - feature_of // PAIR) & (REPS - 1)) * PAIR + feature_of % PAIR
    row_grad = finish_call(order, parts)
    return (row_grad, first_grad, logits.reshape(SAMPLES))


def solution(mesh):
    both = ("rep", "shard")
    in_specs = (
        P("shard", None),
        P(both, None),
        P(both, None, None),
        P(both, None),
        P(),
        P(both),
        P(),
        P(),
        P(),
        P(),
        P(),
        P(),
    )
    out_specs = (P("shard", None), P(), P(both))
    return jax.shard_map(body, mesh=mesh, in_specs=in_specs, out_specs=out_specs, check_vma=False)
```

```python
import functools

import jax
import jax.numpy as jnp
import numpy as np
from jax import lax
from jax.experimental import pallas as pl
from jax.experimental.pallas import tpu as pltpu
from jax.sharding import PartitionSpec as P

BF = jnp.bfloat16
F32 = jnp.float32
I32 = jnp.int32
OWNERS = 32
FEATS = 8
KEYS = OWNERS * FEATS
CAP = 512
VOC = 1024
ROWS = FEATS * VOC
EMB = 128
BAGS = 1024
SAMPLES = 128
WIDTH = FEATS * EMB
IDS = 8192
REPS = 4
PAIR = FEATS // REPS
LANES = 256
IDROWS = IDS // LANES
ACCS = 16
POOLED = 8
GROUP = 4
LISTED = CAP + 64
LISTS = 4
SOURCES = GROUP * REPS * PAIR * SAMPLES
SHIFT = 13
EARLY = 256
VMEM = 56 * 1024 * 1024

NT = (((1,), (1,)), ((), ()))
TN = (((0,), (0,)), ((), ()))


def dot(a, b, dims=(((1,), (0,)), ((), ()))):
    return lax.dot_general(a, b, dims, preferred_element_type=F32)


def iota(shape, dim):
    return lax.broadcasted_iota(I32, shape, dim)


def onehot(cond):
    return jnp.where(cond, 1.0, 0.0).astype(BF)


def index_kernel(
    ids_in, owner_in, len_in, slot_ref, out_ref, ids_ref, owner_ref, len_ref, bag_ref, key_ref
):
    for r in range(IDROWS):
        ids_ref[r : r + 1, :] = ids_in[:, r * LANES : (r + 1) * LANES]
        owner_ref[r : r + 1, :] = owner_in[:, r * LANES : (r + 1) * LANES]
    for r in range(BAGS // 128):
        len_ref[r : r + 1, :] = len_in[:, r * 128 : (r + 1) * 128]
    lens = len_ref[...].astype(F32).astype(BF)
    incl128 = onehot(iota((128, 128), 0) <= iota((128, 128), 1))
    within = dot(lens, incl128)
    total = jnp.broadcast_to(within[:, 127:128], (8, 128))
    high = jnp.floor(total * (1.0 / 256.0))
    low = total - high * 256.0
    below8 = onehot(iota((8, 8), 1) < iota((8, 8), 0))
    before = dot(below8, high.astype(BF)) * 256.0 + dot(below8, low.astype(BF))
    start = (within + before).astype(I32) - len_ref[...]
    start_hi = start >> 8
    start_lo = start & 255
    marks = jnp.zeros((IDROWS, LANES), F32)
    for r in range(8):
        a = onehot(iota((IDROWS, 128), 0) == start_hi[r : r + 1, :])
        b = onehot(iota((LANES, 128), 0) == start_lo[r : r + 1, :])
        marks = marks + dot(a, b, NT)
    marks = marks.astype(BF)
    incl = onehot(iota((LANES, LANES), 0) <= iota((LANES, LANES), 1))
    strict = onehot(iota((LANES, LANES), 0) < iota((LANES, LANES), 1))
    row_counts = dot(marks, jnp.ones((LANES, LANES), BF))
    below = onehot(iota((IDROWS, IDROWS), 1) < iota((IDROWS, IDROWS), 0))
    bag = (dot(marks, incl) + dot(below, row_counts.astype(BF))).astype(I32) - 1
    bag_ref[...] = bag
    key_ref[...] = owner_ref[...] * FEATS + (bag & (FEATS - 1))

    key_iota = iota((KEYS, LANES), 0)

    def count(r, acc):
        return acc + jnp.where(key_iota == key_ref[pl.ds(r, 1), :], 1.0, 0.0)

    counts = lax.fori_loop(0, IDROWS, count, jnp.zeros((KEYS, LANES), F32), unroll=4)
    totals = dot(counts.astype(BF), jnp.ones((LANES, LANES), BF))
    high = jnp.floor(totals * (1.0 / 256.0))
    low = totals - high * 256.0
    ki, kj = iota((KEYS, KEYS), 0), iota((KEYS, KEYS), 1)
    earlier = onehot((ki // FEATS == kj // FEATS) & (kj < ki))
    carry0 = dot(earlier, high.astype(BF)) * 256.0 + dot(earlier, low.astype(BF))

    rank_iota = iota((CAP // 2, LANES), 0)
    owner_iota = iota((OWNERS, LANES), 0)

    of_owner = onehot(iota((KEYS, OWNERS), 0) // FEATS == iota((KEYS, OWNERS), 1))
    by_owner = dot(of_owner, slot_ref[...].astype(F32).astype(BF))
    is_feature = (iota((KEYS, FEATS), 0) & (FEATS - 1)) == iota((KEYS, FEATS), 1)
    slots = jnp.sum(jnp.where(is_feature, by_owner, 0.0), axis=1, keepdims=True)
    carry0 = carry0 + jnp.broadcast_to(slots, (KEYS, LANES)) * VOC

    def place(r, state):
        carry, acc = state
        same = key_iota == key_ref[pl.ds(r, 1), :]
        hot = jnp.where(same, 1.0, 0.0)
        prefix = dot(hot.astype(BF), strict)
        found = jnp.sum(jnp.where(same, prefix + carry, 0.0), axis=0, keepdims=True)
        found = found.astype(I32)
        rank = found & (VOC - 1)
        row = (found - rank) + ids_ref[pl.ds(r, 1), :]
        value = (1 << 23) + (row << 10) + bag_ref[pl.ds(r, 1), :]
        mine = owner_iota == owner_ref[pl.ds(r, 1), :]
        pieces = [
            jnp.where(mine, jnp.broadcast_to(p.astype(F32), (OWNERS, LANES)), 0.0)
            for p in (value & 255, (value >> 8) & 255, value >> 16)
        ]
        left = jnp.concatenate(pieces, axis=0).astype(BF)
        upper = rank >= CAP // 2
        left = jnp.concatenate([left * onehot(~upper), left * onehot(upper)], axis=0)
        right = onehot(rank_iota == (rank & (CAP // 2 - 1)))
        acc = acc + dot(left, right, NT)
        carry = carry + (prefix + hot)[:, LANES - 1 : LANES]
        return carry, acc

    _, acc = lax.fori_loop(
        0, IDROWS, place, (carry0, jnp.zeros((6 * OWNERS, CAP // 2), F32)), unroll=8
    )
    acc = jnp.concatenate([acc[: 3 * OWNERS], acc[3 * OWNERS :]], axis=1).astype(I32)
    out_ref[...] = (
        acc[:OWNERS] + (acc[OWNERS : 2 * OWNERS] << 8) + (acc[2 * OWNERS :] << 16)
    )


def index_call(ids, owners, lengths, slots):
    return pl.pallas_call(
        index_kernel,
        out_shape=jax.ShapeDtypeStruct((OWNERS, CAP), I32),
        scratch_shapes=[
            pltpu.VMEM((IDROWS, LANES), I32),
            pltpu.VMEM((IDROWS, LANES), I32),
            pltpu.VMEM((BAGS // 128, 128), I32),
            pltpu.VMEM((IDROWS, LANES), I32),
            pltpu.VMEM((IDROWS, LANES), I32),
        ],
        compiler_params=pltpu.CompilerParams(vmem_limit_bytes=VMEM),
        name="index",
    )(ids, owners, lengths, slots)


def gather_kernel(row_ref, table_ref, out_ref, wide, picked):
    step = pl.program_id(0)
    depth = out_ref.shape[1]

    @pl.when(step == 0)
    def _():
        wide[...] = table_ref[...].astype(F32)

    for part in range(LISTS):
        base = (step * LISTS + part) * depth

        def some(i, _):
            at = i * 32
            rows = [wide[pl.ds(row_ref[base + at + j], 1), :] for j in range(32)]
            for j in range(32):
                picked[pl.ds(part * depth + at + j, 1), :] = rows[j]
            return 0

        lax.fori_loop(0, depth // 32, some, 0)
        out_ref[part] = picked[part * depth : (part + 1) * depth, :].astype(BF)


def gather_call(rows, table):
    depth = rows.shape[1]
    return pl.pallas_call(
        gather_kernel,
        out_shape=jax.ShapeDtypeStruct((OWNERS, depth, EMB), BF),
        grid_spec=pltpu.PrefetchScalarGridSpec(
            num_scalar_prefetch=1,
            grid=(OWNERS // LISTS,),
            in_specs=[pl.BlockSpec((ROWS, EMB), lambda i, r: (0, 0))],
            out_specs=pl.BlockSpec((LISTS, depth, EMB), lambda i, r: (i, 0, 0)),
            scratch_shapes=[pltpu.VMEM((ROWS, EMB), F32), pltpu.VMEM((LISTS * depth, EMB), F32)],
        ),
        compiler_params=pltpu.CompilerParams(vmem_limit_bytes=VMEM),
        name="gather",
    )(rows.reshape(-1), table)


def sums_of(packed_ref, got_ref, step, at):
    rows, masked = [], []
    depth = got_ref.shape[1]
    for i in range(POOLED):
        packed = packed_ref[pl.ds(step * POOLED + i, 1), at : at + depth]
        bag = packed & (BAGS - 1)
        sample = jnp.where(packed > 0, bag >> 3, -1)
        rows.append(onehot(iota((SAMPLES, depth), 0) == sample))
        feature = jnp.broadcast_to((bag & (FEATS - 1)).astype(F32), (EMB, depth)).T.astype(BF)
        own = got_ref[i]
        masked.append(
            jnp.concatenate(
                [jnp.where(feature == f, own, jnp.zeros((), BF)) for f in range(FEATS)], axis=1
            )
        )
    return dot(jnp.concatenate(rows, axis=1), jnp.concatenate(masked, axis=0))


def pool_kernel(at, got_ref, packed_ref, out_ref):
    step = pl.program_id(0)
    sums = sums_of(packed_ref, got_ref, step, at)

    @pl.when(step == 0)
    def _():
        out_ref[...] = sums

    @pl.when(step > 0)
    def _():
        out_ref[...] += sums


def pool_call(got, packed, at):
    depth = got.shape[1]
    return pl.pallas_call(
        functools.partial(pool_kernel, at),
        out_shape=jax.ShapeDtypeStruct((SAMPLES, WIDTH), F32),
        grid=(OWNERS // POOLED,),
        in_specs=[
            pl.BlockSpec((POOLED, depth, EMB), lambda i: (i, 0, 0)),
            pl.BlockSpec((OWNERS, CAP), lambda i: (0, 0)),
        ],
        out_specs=pl.BlockSpec((SAMPLES, WIDTH), lambda i: (0, 0)),
        compiler_params=pltpu.CompilerParams(vmem_limit_bytes=VMEM),
        name="pool",
    )(got, packed)


def sigmoid(x):
    return 1.0 / (1.0 + jnp.exp(-x))


def tower_kernel(
    at,
    got_ref,
    packed_ref,
    earlier_ref,
    labels_ref,
    gain_ref,
    cbias_ref,
    dbias_ref,
    out_w_ref,
    cross_hbm,
    deep_hbm,
    logits_ref,
    grads_ref,
    first_ref,
    pooled_ref,
    cross_w,
    deep_w,
    start_ref,
    cross_t,
    deep_t,
    gx_ref,
    sems,
):
    step = pl.program_id(0)

    def copies():
        out = []
        for layer in range(3):
            out.append(
                pltpu.make_async_copy(cross_hbm.at[layer], cross_w.at[layer], sems.at[layer])
            )
            out.append(
                pltpu.make_async_copy(deep_hbm.at[layer], deep_w.at[layer], sems.at[3 + layer])
            )
        return out

    @pl.when(step == 0)
    def _():
        for copy in copies():
            copy.start()
        pooled_ref[...] = earlier_ref[...]

    pooled_ref[...] += sums_of(packed_ref, got_ref, step, at)

    @pl.when(step == OWNERS // POOLED - 1)
    def _():
        for copy in copies():
            copy.wait()
        gain = gain_ref[...]
        pooled = pooled_ref[...]
        inverse = lax.rsqrt(jnp.mean(pooled * pooled, axis=1, keepdims=True) + 1e-06)
        start = (pooled * inverse * gain).astype(BF)
        start_ref[...] = start
        current = start
        for layer in range(3):
            product = dot(current, cross_w[layer]) + cbias_ref[layer : layer + 1, :]
            cross_t[layer] = product
            current = (start_ref[...].astype(F32) * product + current.astype(F32)).astype(BF)
        for layer in range(3):
            product = dot(current, deep_w[layer]) + dbias_ref[layer : layer + 1, :]
            deep_t[layer] = product
            current = (product * sigmoid(product)).astype(BF)
        out_w = out_w_ref[...]
        logits = jnp.sum(current.astype(F32) * out_w, axis=1, keepdims=True)
        logits_ref[...] = logits
        error = sigmoid(logits) - labels_ref[...].astype(F32)
        grad = error * out_w
        for layer in (2, 1, 0):
            product = deep_t[layer]
            sig = sigmoid(product)
            masked = (grad * sig * (1.0 + product * (1.0 - sig))).astype(BF)
            grad = dot(masked, deep_w[layer], NT)
        gx_ref[...] = jnp.zeros_like(gx_ref)
        for layer in (2, 1, 0):
            crossed = (grad * start_ref[...].astype(F32)).astype(BF)
            gx_ref[...] += grad * cross_t[layer]
            grad = grad + dot(crossed, cross_w[layer], NT)
            if layer == 0:
                outer = dot(start_ref[...], crossed, TN).reshape(OWNERS, REPS, 8, WIDTH)
                for r in range(REPS):
                    first_ref[r] = outer[:, r].reshape(OWNERS * 8, WIDTH).astype(BF)
        scaled = (gx_ref[...] + grad) * gain
        pooled = pooled_ref[...]
        inverse = lax.rsqrt(jnp.mean(pooled * pooled, axis=1, keepdims=True) + 1e-06)
        mean = jnp.mean(scaled * pooled, axis=1, keepdims=True)
        result = (inverse * scaled - pooled * (inverse * inverse * inverse) * mean).astype(BF)
        for r in range(REPS):
            grads_ref[r] = result[:, r * PAIR * EMB : (r + 1) * PAIR * EMB]


def tower_call(got, packed, earlier, labels, gain, cross, cbias, deep, dbias, out_w):
    def whole(shape):
        return pl.BlockSpec(shape, lambda i: (0,) * len(shape))

    return pl.pallas_call(
        functools.partial(tower_kernel, CAP - got.shape[1]),
        grid=(OWNERS // POOLED,),
        in_specs=[
            pl.BlockSpec((POOLED, got.shape[1], EMB), lambda i: (i, 0, 0)),
            whole((OWNERS, CAP)),
            whole((SAMPLES, WIDTH)),
            whole((SAMPLES, 1)),
            whole((1, WIDTH)),
            whole((3, WIDTH)),
            whole((3, WIDTH)),
            whole((1, WIDTH)),
            pl.BlockSpec(memory_space=pl.ANY),
            pl.BlockSpec(memory_space=pl.ANY),
        ],
        out_specs=[
            whole((SAMPLES, 1)),
            whole((REPS, SAMPLES, PAIR * EMB)),
            whole((REPS, OWNERS * 8, WIDTH)),
        ],
        out_shape=[
            jax.ShapeDtypeStruct((SAMPLES, 1), F32),
            jax.ShapeDtypeStruct((REPS, SAMPLES, PAIR * EMB), BF),
            jax.ShapeDtypeStruct((REPS, OWNERS * 8, WIDTH), BF),
        ],
        scratch_shapes=[
            pltpu.VMEM((SAMPLES, WIDTH), F32),
            pltpu.VMEM((3, WIDTH, WIDTH), BF),
            pltpu.VMEM((3, WIDTH, WIDTH), BF),
            pltpu.VMEM((SAMPLES, WIDTH), BF),
            pltpu.VMEM((3, SAMPLES, WIDTH), F32),
            pltpu.VMEM((3, SAMPLES, WIDTH), F32),
            pltpu.VMEM((SAMPLES, WIDTH), F32),
            pltpu.SemaphoreType.DMA((6,)),
        ],
        compiler_params=pltpu.CompilerParams(vmem_limit_bytes=VMEM),
        name="tower",
    )(got, packed, earlier, labels, gain, cbias, dbias, out_w, cross, deep)


def scatter_kernel(which, first_ref, last_ref, word_ref, grads_ref, out_ref, wide, *accs):
    step = pl.program_id(0)
    ours = slice(which * VOC, (which + 1) * VOC)

    @pl.when(step == 0)
    def _():
        for acc in accs:
            acc[ours, :] = jnp.zeros((VOC, EMB), F32)

    for g in range(GROUP):
        for r in range(REPS):
            base = ((g * REPS + r) * PAIR + which) * SAMPLES
            wide[base : base + SAMPLES, :] = grads_ref[g, r].astype(F32)

    def device(k, _):
        listed = step * GROUP * REPS + k
        first = first_ref[listed]

        def some(i, _):
            at = k * LISTED + first + i * ACCS
            words = [word_ref[at + j] for j in range(ACCS)]
            rows = [wide[pl.ds(word & (SOURCES - 1), 1), :] for word in words]
            olds = [accs[j][pl.ds(words[j] >> SHIFT, 1), :] for j in range(ACCS)]
            for j in range(ACCS):
                accs[j][pl.ds(words[j] >> SHIFT, 1), :] = olds[j] + rows[j]
            return 0

        lax.fori_loop(0, (last_ref[listed] - first + ACCS - 1) // ACCS, some, 0)
        return 0

    lax.fori_loop(0, GROUP * REPS, device, 0)

    @pl.when(step == pl.num_programs(0) - 1)
    def _():
        total = accs[0][ours, :]
        for acc in accs[1:]:
            total = total + acc[ours, :]
        out_ref[...] = total.astype(out_ref.dtype)


def scatter_call(which, words, first, last, grads):
    return pl.pallas_call(
        functools.partial(scatter_kernel, which),
        out_shape=jax.ShapeDtypeStruct((VOC, EMB), BF),
        grid_spec=pltpu.PrefetchScalarGridSpec(
            num_scalar_prefetch=2,
            grid=(OWNERS // GROUP,),
            in_specs=[
                pl.BlockSpec(
                    (GROUP * REPS * LISTED,), lambda i, *_: (i,), memory_space=pltpu.SMEM
                ),
                pl.BlockSpec((GROUP, REPS, SAMPLES, EMB), lambda i, *_: (i, 0, 0, which)),
            ],
            out_specs=pl.BlockSpec((VOC, EMB), lambda i, *_: (0, 0)),
            scratch_shapes=[pltpu.VMEM((SOURCES, EMB), F32)]
            + [pltpu.VMEM((PAIR * VOC + 8, EMB), F32) for _ in range(ACCS)],
        ),
        compiler_params=pltpu.CompilerParams(vmem_limit_bytes=VMEM),
        cost_estimate=pl.CostEstimate(
            flops=IDS * EMB, bytes_accessed=60_000_000, transcendentals=0
        ),
        name="scatter",
    )(first, last, words, grads)


def finish_kernel(place_ref, *refs):
    parts, rows_ref = refs[:REPS], refs[-1]
    step = pl.program_id(0)
    for k in range(REPS):

        @pl.when(step == k)
        def _():
            rows_ref[...] = parts[k][...].astype(F32)


def finish_call(places, parts, earlier):
    whole = pl.BlockSpec((VOC, EMB), lambda i, p: (0, 0))
    more = [] if earlier is None else [earlier]
    return pl.pallas_call(
        finish_kernel,
        out_shape=jax.ShapeDtypeStruct((ROWS, EMB), F32),
        grid_spec=pltpu.PrefetchScalarGridSpec(
            num_scalar_prefetch=1,
            grid=(REPS,),
            in_specs=[whole] * REPS + [pl.BlockSpec(memory_space=pl.ANY)] * len(more),
            out_specs=pl.BlockSpec((VOC, EMB), lambda i, p: (p[i], 0)),
        ),
        input_output_aliases={1 + REPS: 0} if more else {},
        compiler_params=pltpu.CompilerParams(vmem_limit_bytes=VMEM),
        name="finish",
    )(places, *parts, *more)


def from_before(x, axis, k):
    if k == 0:
        return x
    n = lax.axis_size(axis)
    return lax.ppermute(x, axis, [(i, (i + k) % n) for i in range(n)])


def in_order(x, axis, me):
    n = lax.axis_size(axis)
    back = [from_before(x, axis, k) for k in range(n)]
    twice = jnp.concatenate([back[(n - 1 - i) % n] for i in range(2 * n - 1)])
    return lax.dynamic_slice_in_dim(twice, (n - 1 - me) * x.shape[0], n * x.shape[0])


def summed(x):
    return jnp.sum(x.astype(F32), axis=0).astype(BF)


def body(
    embed_table,
    row_ids,
    row_owner,
    lengths,
    feature_slot,
    labels,
    norm_gain,
    cross_weight,
    cross_bias,
    deep_weight,
    deep_bias,
    out_weight,
):
    packed = index_call(
        row_ids,
        row_owner.reshape(1, IDS),
        lengths,
        feature_slot,
    )
    asked = lax.all_to_all(
        packed.reshape(OWNERS, 4, 128), "shard", split_axis=0, concat_axis=0, tiled=True
    )
    rows = ((asked >> 10) & (ROWS - 1)).reshape(OWNERS, CAP)

    def exchange(x, axis):
        return lax.all_to_all(x, axis, split_axis=0, concat_axis=0, tiled=True)

    picked_early = gather_call(rows[:, :EARLY], embed_table)
    picked_early, lists = lax.optimization_barrier((picked_early, asked))
    got_early = exchange(picked_early, "shard")
    picked_late, lists = lax.optimization_barrier(
        (gather_call(rows[:, EARLY:], embed_table), lists)
    )
    got_late = exchange(picked_late, "shard")

    rep = lax.axis_index("rep")
    everyone = jnp.stack(
        [
            from_before(lists, "rep", k).reshape(OWNERS // GROUP, GROUP, CAP)
            for k in range(REPS)
        ],
        axis=2,
    )
    feature = everyone & (FEATS - 1)
    valid = everyone > 0
    within = feature - rep * PAIR
    ours = valid & (within >= 0) & (within < PAIR)
    target = jnp.where(ours, within * VOC + ((everyone >> 10) & (VOC - 1)), PAIR * VOC)
    group = lax.broadcasted_iota(I32, everyone.shape, 1)
    back = lax.broadcasted_iota(I32, everyone.shape, 2)
    source = (group * REPS + back) * (PAIR * SAMPLES) + jnp.where(
        ours, within * SAMPLES + ((everyone >> 3) & (SAMPLES - 1)), 0
    )
    words = jnp.pad(
        (target << SHIFT) | source,
        ((0, 0), (0, 0), (0, 0), (0, LISTED - CAP)),
        constant_values=(PAIR * VOC) << SHIFT,
    ).reshape(-1)
    bounds = [
        jnp.sum((valid & (within < f)).astype(I32), axis=3).reshape(-1) for f in range(PAIR + 1)
    ]
    sums_early = pool_call(got_early, packed, 0)
    got_late, sums_early, words, bounds = lax.optimization_barrier(
        (got_late, sums_early, words, bounds)
    )

    logits, grads, first_local = tower_call(
        got_late,
        packed,
        sums_early,
        labels.reshape(SAMPLES, 1),
        norm_gain.reshape(1, WIDTH),
        cross_weight,
        cross_bias,
        deep_weight,
        deep_bias,
        out_weight.reshape(1, WIDTH),
    )
    mine = jnp.stack(
        [
            from_before(lax.dynamic_index_in_dim(grads, (rep + k) % REPS, 0, False), "rep", k)
            for k in range(REPS)
        ]
    )
    mine, first_local = lax.optimization_barrier((mine, first_local))
    all_grads = lax.all_gather(mine, "shard", axis=0)
    quarter = summed(exchange(first_local, "rep"))
    eight = summed(exchange(quarter.reshape(OWNERS, 8, WIDTH), "shard"))
    first_grad = lax.all_gather(
        in_order(eight, "rep", rep), "shard", axis=0, tiled=True
    ).astype(F32)

    slots = feature_slot[lax.axis_index("shard")]
    row_grad = None
    for f in range(PAIR):
        part = scatter_call(f, words, bounds[f], bounds[f + 1], all_grads)
        parts = [from_before(part, "rep", k) for k in range(REPS)]
        holder = (rep - jnp.arange(REPS, dtype=I32)) % REPS
        row_grad = finish_call(slots[holder * PAIR + f], parts, row_grad)
    return (row_grad, first_grad, logits.reshape(SAMPLES))


def solution(mesh):
    both = ("rep", "shard")
    in_specs = (
        P("shard", None),
        P(both, None),
        P(both, None, None),
        P(both, None),
        P(),
        P(both),
        P(),
        P(),
        P(),
        P(),
        P(),
        P(),
    )
    out_specs = (P("shard", None), P(), P(both))
    return jax.shard_map(body, mesh=mesh, in_specs=in_specs, out_specs=out_specs, check_vma=False)
```

```python
import functools

import jax
import jax.numpy as jnp
import numpy as np
from jax import lax
from jax.experimental import pallas as pl
from jax.experimental.pallas import tpu as pltpu
from jax.sharding import PartitionSpec as P

BF = jnp.bfloat16
F32 = jnp.float32
I32 = jnp.int32
OWNERS = 32
FEATS = 8
KEYS = OWNERS * FEATS
CAP = 512
VOC = 1024
ROWS = FEATS * VOC
EMB = 128
BAGS = 1024
SAMPLES = 128
WIDTH = FEATS * EMB
IDS = 8192
REPS = 4
PAIR = FEATS // REPS
LANES = 256
IDROWS = IDS // LANES
ACCS = 16
POOLED = 8
GROUP = 4
LISTED = CAP + 64
LISTS = 4
SOURCES = GROUP * REPS * PAIR * SAMPLES
SHIFT = 13
EARLY = 256
VMEM = 62 * 1024 * 1024

NT = (((1,), (1,)), ((), ()))
TN = (((0,), (0,)), ((), ()))


def dot(a, b, dims=(((1,), (0,)), ((), ()))):
    return lax.dot_general(a, b, dims, preferred_element_type=F32)


def iota(shape, dim):
    return lax.broadcasted_iota(I32, shape, dim)


def onehot(cond):
    return jnp.where(cond, 1.0, 0.0).astype(BF)


def index_kernel(
    ids_in, owner_in, len_in, slot_ref, out_ref, ids_ref, owner_ref, len_ref, bag_ref, key_ref
):
    for r in range(IDROWS):
        ids_ref[r : r + 1, :] = ids_in[:, r * LANES : (r + 1) * LANES]
        owner_ref[r : r + 1, :] = owner_in[:, r * LANES : (r + 1) * LANES]
    for r in range(BAGS // 128):
        len_ref[r : r + 1, :] = len_in[:, r * 128 : (r + 1) * 128]
    lens = len_ref[...].astype(F32).astype(BF)
    incl128 = onehot(iota((128, 128), 0) <= iota((128, 128), 1))
    within = dot(lens, incl128)
    total = jnp.broadcast_to(within[:, 127:128], (8, 128))
    high = jnp.floor(total * (1.0 / 256.0))
    low = total - high * 256.0
    below8 = onehot(iota((8, 8), 1) < iota((8, 8), 0))
    before = dot(below8, high.astype(BF)) * 256.0 + dot(below8, low.astype(BF))
    start = (within + before).astype(I32) - len_ref[...]
    start_hi = start >> 8
    start_lo = start & 255
    marks = jnp.zeros((IDROWS, LANES), F32)
    for r in range(8):
        a = onehot(iota((IDROWS, 128), 0) == start_hi[r : r + 1, :])
        b = onehot(iota((LANES, 128), 0) == start_lo[r : r + 1, :])
        marks = marks + dot(a, b, NT)
    marks = marks.astype(BF)
    incl = onehot(iota((LANES, LANES), 0) <= iota((LANES, LANES), 1))
    strict = onehot(iota((LANES, LANES), 0) < iota((LANES, LANES), 1))
    row_counts = dot(marks, jnp.ones((LANES, LANES), BF))
    below = onehot(iota((IDROWS, IDROWS), 1) < iota((IDROWS, IDROWS), 0))
    bag = (dot(marks, incl) + dot(below, row_counts.astype(BF))).astype(I32) - 1
    bag_ref[...] = bag
    key_ref[...] = owner_ref[...] * FEATS + (bag & (FEATS - 1))

    key_iota = iota((KEYS, LANES), 0)

    def count(r, acc):
        return acc + jnp.where(key_iota == key_ref[pl.ds(r, 1), :], 1.0, 0.0)

    counts = lax.fori_loop(0, IDROWS, count, jnp.zeros((KEYS, LANES), F32), unroll=4)
    totals = dot(counts.astype(BF), jnp.ones((LANES, LANES), BF))
    high = jnp.floor(totals * (1.0 / 256.0))
    low = totals - high * 256.0
    ki, kj = iota((KEYS, KEYS), 0), iota((KEYS, KEYS), 1)
    earlier = onehot((ki // FEATS == kj // FEATS) & (kj < ki))
    carry0 = dot(earlier, high.astype(BF)) * 256.0 + dot(earlier, low.astype(BF))

    rank_iota = iota((CAP // 2, LANES), 0)
    owner_iota = iota((OWNERS, LANES), 0)

    of_owner = onehot(iota((KEYS, OWNERS), 0) // FEATS == iota((KEYS, OWNERS), 1))
    by_owner = dot(of_owner, slot_ref[...].astype(F32).astype(BF))
    is_feature = (iota((KEYS, FEATS), 0) & (FEATS - 1)) == iota((KEYS, FEATS), 1)
    slots = jnp.sum(jnp.where(is_feature, by_owner, 0.0), axis=1, keepdims=True)
    carry0 = carry0 + jnp.broadcast_to(slots, (KEYS, LANES)) * VOC

    def place(r, state):
        carry, acc = state
        same = key_iota == key_ref[pl.ds(r, 1), :]
        hot = jnp.where(same, 1.0, 0.0)
        prefix = dot(hot.astype(BF), strict)
        found = jnp.sum(jnp.where(same, prefix + carry, 0.0), axis=0, keepdims=True)
        found = found.astype(I32)
        rank = found & (VOC - 1)
        row = (found - rank) + ids_ref[pl.ds(r, 1), :]
        value = (1 << 23) + (row << 10) + bag_ref[pl.ds(r, 1), :]
        mine = owner_iota == owner_ref[pl.ds(r, 1), :]
        pieces = [
            jnp.where(mine, jnp.broadcast_to(p.astype(F32), (OWNERS, LANES)), 0.0)
            for p in (value & 255, (value >> 8) & 255, value >> 16)
        ]
        left = jnp.concatenate(pieces, axis=0).astype(BF)
        upper = rank >= CAP // 2
        left = jnp.concatenate([left * onehot(~upper), left * onehot(upper)], axis=0)
        right = onehot(rank_iota == (rank & (CAP // 2 - 1)))
        acc = acc + dot(left, right, NT)
        carry = carry + (prefix + hot)[:, LANES - 1 : LANES]
        return carry, acc

    _, acc = lax.fori_loop(
        0, IDROWS, place, (carry0, jnp.zeros((6 * OWNERS, CAP // 2), F32)), unroll=8
    )
    acc = jnp.concatenate([acc[: 3 * OWNERS], acc[3 * OWNERS :]], axis=1).astype(I32)
    out_ref[...] = (
        acc[:OWNERS] + (acc[OWNERS : 2 * OWNERS] << 8) + (acc[2 * OWNERS :] << 16)
    )


def index_call(ids, owners, lengths, slots):
    return pl.pallas_call(
        index_kernel,
        out_shape=jax.ShapeDtypeStruct((OWNERS, CAP), I32),
        scratch_shapes=[
            pltpu.VMEM((IDROWS, LANES), I32),
            pltpu.VMEM((IDROWS, LANES), I32),
            pltpu.VMEM((BAGS // 128, 128), I32),
            pltpu.VMEM((IDROWS, LANES), I32),
            pltpu.VMEM((IDROWS, LANES), I32),
        ],
        compiler_params=pltpu.CompilerParams(vmem_limit_bytes=VMEM),
        name="index",
    )(ids, owners, lengths, slots)


def gather_kernel(row_ref, table_ref, out_ref, wide, picked):
    step = pl.program_id(0)
    depth = out_ref.shape[1]

    @pl.when(step == 0)
    def _():
        wide[...] = table_ref[...].astype(F32)

    for part in range(LISTS):
        base = (step * LISTS + part) * depth

        def some(i, _):
            at = i * 32
            rows = [wide[pl.ds(row_ref[base + at + j], 1), :] for j in range(32)]
            for j in range(32):
                picked[pl.ds(part * depth + at + j, 1), :] = rows[j]
            return 0

        lax.fori_loop(0, depth // 32, some, 0)
        out_ref[part] = picked[part * depth : (part + 1) * depth, :].astype(BF)


def gather_call(rows, table):
    depth = rows.shape[1]
    return pl.pallas_call(
        gather_kernel,
        out_shape=jax.ShapeDtypeStruct((OWNERS, depth, EMB), BF),
        grid_spec=pltpu.PrefetchScalarGridSpec(
            num_scalar_prefetch=1,
            grid=(OWNERS // LISTS,),
            in_specs=[pl.BlockSpec((ROWS, EMB), lambda i, r: (0, 0))],
            out_specs=pl.BlockSpec((LISTS, depth, EMB), lambda i, r: (i, 0, 0)),
            scratch_shapes=[pltpu.VMEM((ROWS, EMB), F32), pltpu.VMEM((LISTS * depth, EMB), F32)],
        ),
        compiler_params=pltpu.CompilerParams(vmem_limit_bytes=VMEM),
        name="gather",
    )(rows.reshape(-1), table)


def sums_of(packed_ref, got_ref, step, at):
    rows, masked = [], []
    depth = got_ref.shape[1]
    for i in range(POOLED):
        packed = packed_ref[pl.ds(step * POOLED + i, 1), at : at + depth]
        bag = packed & (BAGS - 1)
        sample = jnp.where(packed > 0, bag >> 3, -1)
        rows.append(onehot(iota((SAMPLES, depth), 0) == sample))
        feature = jnp.broadcast_to((bag & (FEATS - 1)).astype(F32), (EMB, depth)).T.astype(BF)
        own = got_ref[i]
        masked.append(
            jnp.concatenate(
                [jnp.where(feature == f, own, jnp.zeros((), BF)) for f in range(FEATS)], axis=1
            )
        )
    return dot(jnp.concatenate(rows, axis=1), jnp.concatenate(masked, axis=0))


def pool_kernel(at, got_ref, packed_ref, out_ref):
    step = pl.program_id(0)
    sums = sums_of(packed_ref, got_ref, step, at)

    @pl.when(step == 0)
    def _():
        out_ref[...] = sums

    @pl.when(step > 0)
    def _():
        out_ref[...] += sums


def pool_call(got, packed, at):
    depth = got.shape[1]
    return pl.pallas_call(
        functools.partial(pool_kernel, at),
        out_shape=jax.ShapeDtypeStruct((SAMPLES, WIDTH), F32),
        grid=(OWNERS // POOLED,),
        in_specs=[
            pl.BlockSpec((POOLED, depth, EMB), lambda i: (i, 0, 0)),
            pl.BlockSpec((OWNERS, CAP), lambda i: (0, 0)),
        ],
        out_specs=pl.BlockSpec((SAMPLES, WIDTH), lambda i: (0, 0)),
        compiler_params=pltpu.CompilerParams(vmem_limit_bytes=VMEM),
        name="pool",
    )(got, packed)


def sigmoid(x):
    return 1.0 / (1.0 + jnp.exp(-x))


def tower_kernel(
    at,
    got_ref,
    packed_ref,
    earlier_ref,
    labels_ref,
    gain_ref,
    cbias_ref,
    dbias_ref,
    out_w_ref,
    cross_hbm,
    deep_hbm,
    logits_ref,
    grads_ref,
    first_ref,
    pooled_ref,
    cross_w,
    deep_w,
    start_ref,
    cross_t,
    deep_t,
    gx_ref,
    sems,
):
    step = pl.program_id(0)

    def cross_copy(layer):
        return pltpu.make_async_copy(cross_hbm.at[layer], cross_w.at[layer], sems.at[layer])

    def deep_copy(layer):
        return pltpu.make_async_copy(deep_hbm.at[layer], deep_w.at[layer], sems.at[3 + layer])

    @pl.when(step == 0)
    def _():
        for layer in range(3):
            cross_copy(layer).start()
        for layer in range(3):
            deep_copy(layer).start()
        pooled_ref[...] = earlier_ref[...]

    pooled_ref[...] += sums_of(packed_ref, got_ref, step, at)

    @pl.when(step == OWNERS // POOLED - 1)
    def _():
        gain = gain_ref[...]
        pooled = pooled_ref[...]
        inverse = lax.rsqrt(jnp.mean(pooled * pooled, axis=1, keepdims=True) + 1e-06)
        start = (pooled * inverse * gain).astype(BF)
        start_ref[...] = start
        current = start
        for layer in range(3):
            cross_copy(layer).wait()
            product = dot(current, cross_w[layer]) + cbias_ref[layer : layer + 1, :]
            cross_t[layer] = product
            current = (start_ref[...].astype(F32) * product + current.astype(F32)).astype(BF)
        for layer in range(3):
            deep_copy(layer).wait()
            product = dot(current, deep_w[layer]) + dbias_ref[layer : layer + 1, :]
            deep_t[layer] = product
            current = (product * sigmoid(product)).astype(BF)
        out_w = out_w_ref[...]
        logits = jnp.sum(current.astype(F32) * out_w, axis=1, keepdims=True)
        logits_ref[...] = logits
        error = sigmoid(logits) - labels_ref[...].astype(F32)
        grad = error * out_w
        for layer in (2, 1, 0):
            product = deep_t[layer]
            sig = sigmoid(product)
            masked = (grad * sig * (1.0 + product * (1.0 - sig))).astype(BF)
            grad = dot(masked, deep_w[layer], NT)
        gx_ref[...] = jnp.zeros_like(gx_ref)
        for layer in (2, 1, 0):
            crossed = (grad * start_ref[...].astype(F32)).astype(BF)
            gx_ref[...] += grad * cross_t[layer]
            grad = grad + dot(crossed, cross_w[layer], NT)
            if layer == 0:
                outer = dot(start_ref[...], crossed, TN).reshape(OWNERS, REPS, 8, WIDTH)
                for r in range(REPS):
                    first_ref[r] = outer[:, r].reshape(OWNERS * 8, WIDTH).astype(BF)
        scaled = (gx_ref[...] + grad) * gain
        pooled = pooled_ref[...]
        inverse = lax.rsqrt(jnp.mean(pooled * pooled, axis=1, keepdims=True) + 1e-06)
        mean = jnp.mean(scaled * pooled, axis=1, keepdims=True)
        result = (inverse * scaled - pooled * (inverse * inverse * inverse) * mean).astype(BF)
        for r in range(REPS):
            grads_ref[r] = result[:, r * PAIR * EMB : (r + 1) * PAIR * EMB]


def tower_call(got, packed, earlier, labels, gain, cross, cbias, deep, dbias, out_w):
    def whole(shape):
        return pl.BlockSpec(shape, lambda i: (0,) * len(shape))

    return pl.pallas_call(
        functools.partial(tower_kernel, CAP - got.shape[1]),
        grid=(OWNERS // POOLED,),
        in_specs=[
            pl.BlockSpec((POOLED, got.shape[1], EMB), lambda i: (i, 0, 0)),
            whole((OWNERS, CAP)),
            whole((SAMPLES, WIDTH)),
            whole((SAMPLES, 1)),
            whole((1, WIDTH)),
            whole((3, WIDTH)),
            whole((3, WIDTH)),
            whole((1, WIDTH)),
            pl.BlockSpec(memory_space=pl.ANY),
            pl.BlockSpec(memory_space=pl.ANY),
        ],
        out_specs=[
            whole((SAMPLES, 1)),
            whole((REPS, SAMPLES, PAIR * EMB)),
            whole((REPS, OWNERS * 8, WIDTH)),
        ],
        out_shape=[
            jax.ShapeDtypeStruct((SAMPLES, 1), F32),
            jax.ShapeDtypeStruct((REPS, SAMPLES, PAIR * EMB), BF),
            jax.ShapeDtypeStruct((REPS, OWNERS * 8, WIDTH), BF),
        ],
        scratch_shapes=[
            pltpu.VMEM((SAMPLES, WIDTH), F32),
            pltpu.VMEM((3, WIDTH, WIDTH), BF),
            pltpu.VMEM((3, WIDTH, WIDTH), BF),
            pltpu.VMEM((SAMPLES, WIDTH), BF),
            pltpu.VMEM((3, SAMPLES, WIDTH), F32),
            pltpu.VMEM((3, SAMPLES, WIDTH), F32),
            pltpu.VMEM((SAMPLES, WIDTH), F32),
            pltpu.SemaphoreType.DMA((6,)),
        ],
        compiler_params=pltpu.CompilerParams(vmem_limit_bytes=VMEM),
        name="tower",
    )(got, packed, earlier, labels, gain, cbias, dbias, out_w, cross, deep)


def scatter_kernel(first_ref, trips_ref, word_ref, grads_ref, out_ref, wide, *accs):
    step = pl.program_id(0)

    @pl.when(step == 0)
    def _():
        for acc in accs:
            acc[...] = jnp.zeros_like(acc)

    group = grads_ref.shape[0]
    for g in range(group):
        for r in range(REPS):
            block = grads_ref[g, r]
            base = (g * REPS + r) * PAIR * SAMPLES
            for f in range(PAIR):
                wide[base + f * SAMPLES : base + (f + 1) * SAMPLES, :] = block[
                    :, f * EMB : (f + 1) * EMB
                ].astype(F32)

    def device(k, _):
        listed = step * group * REPS + k
        first = first_ref[listed]

        def some(i, _):
            at = first + i * ACCS
            words = [word_ref[at + j] for j in range(ACCS)]
            rows = [wide[pl.ds(word & (SOURCES - 1), 1), :] for word in words]
            olds = [accs[j][pl.ds(words[j] >> SHIFT, 1), :] for j in range(ACCS)]
            for j in range(ACCS):
                accs[j][pl.ds(words[j] >> SHIFT, 1), :] = olds[j] + rows[j]
            return 0

        lax.fori_loop(0, trips_ref[listed], some, 0)
        return 0

    lax.fori_loop(0, group * REPS, device, 0)

    @pl.when(step == pl.num_programs(0) - 1)
    def _():
        total = accs[0][: PAIR * VOC, :]
        for acc in accs[1:]:
            total = total + acc[: PAIR * VOC, :]
        out_ref[...] = total.astype(out_ref.dtype)


def scatter_call(words, first, trips, grads, group=GROUP):
    rows = PAIR * VOC
    return pl.pallas_call(
        scatter_kernel,
        out_shape=jax.ShapeDtypeStruct((rows, EMB), BF),
        grid_spec=pltpu.PrefetchScalarGridSpec(
            num_scalar_prefetch=2,
            grid=(OWNERS // group,),
            in_specs=[
                pl.BlockSpec(
                    (group * REPS * LISTED,), lambda i, *_: (i,), memory_space=pltpu.SMEM
                ),
                pl.BlockSpec(
                    (group, REPS, SAMPLES, PAIR * EMB), lambda i, *_: (i, 0, 0, 0)
                ),
            ],
            out_specs=pl.BlockSpec((rows, EMB), lambda i, *_: (0, 0)),
            scratch_shapes=[pltpu.VMEM((group * REPS * PAIR * SAMPLES, EMB), F32)]
            + [pltpu.VMEM((rows + 8, EMB), F32) for _ in range(ACCS)],
        ),
        compiler_params=pltpu.CompilerParams(vmem_limit_bytes=VMEM),
        name="scatter",
    )(first, trips, words, grads)


def finish_kernel(place_ref, *refs):
    parts, out, wide, sems = refs[:REPS], refs[REPS], refs[REPS + 1], refs[REPS + 2]
    copies = []
    for k in range(REPS):
        for f in range(PAIR):
            n = k * PAIR + f
            wide[n] = parts[k][f].astype(F32)
            to = pl.multiple_of(place_ref[n] * VOC, VOC)
            copies.append(
                pltpu.make_async_copy(wide.at[n], out.at[pl.ds(to, VOC), :], sems.at[n])
            )
            copies[-1].start()
    for copy in copies:
        copy.wait()


def finish_call(places, parts):
    return pl.pallas_call(
        finish_kernel,
        out_shape=jax.ShapeDtypeStruct((ROWS, EMB), F32),
        in_specs=[pl.BlockSpec(memory_space=pltpu.SMEM)]
        + [pl.BlockSpec(memory_space=pltpu.VMEM) for _ in parts],
        out_specs=pl.BlockSpec(memory_space=pl.ANY),
        scratch_shapes=[
            pltpu.VMEM((FEATS, VOC, EMB), F32),
            pltpu.SemaphoreType.DMA((FEATS,)),
        ],
        compiler_params=pltpu.CompilerParams(vmem_limit_bytes=16 * 1024 * 1024),
        name="finish",
    )(places, *parts)


def from_before(x, axis, k):
    if k == 0:
        return x
    n = lax.axis_size(axis)
    return lax.ppermute(x, axis, [(i, (i + k) % n) for i in range(n)])


def in_order(x, axis, me):
    n = lax.axis_size(axis)
    back = [from_before(x, axis, k) for k in range(n)]
    twice = jnp.concatenate([back[(n - 1 - i) % n] for i in range(2 * n - 1)])
    return lax.dynamic_slice_in_dim(twice, (n - 1 - me) * x.shape[0], n * x.shape[0])


def summed(x):
    return jnp.sum(x.astype(F32), axis=0).astype(BF)


def body(
    embed_table,
    row_ids,
    row_owner,
    lengths,
    feature_slot,
    labels,
    norm_gain,
    cross_weight,
    cross_bias,
    deep_weight,
    deep_bias,
    out_weight,
):
    packed = index_call(
        row_ids,
        row_owner.reshape(1, IDS),
        lengths,
        feature_slot,
    )
    asked = lax.all_to_all(
        packed.reshape(OWNERS, 4, 128), "shard", split_axis=0, concat_axis=0, tiled=True
    )
    rows = ((asked >> 10) & (ROWS - 1)).reshape(OWNERS, CAP)

    def exchange(x, axis):
        return lax.all_to_all(x, axis, split_axis=0, concat_axis=0, tiled=True)

    picked_early = gather_call(rows[:, :EARLY], embed_table)
    picked_early, lists = lax.optimization_barrier((picked_early, asked))
    got_early = exchange(picked_early, "shard")
    picked_late, lists = lax.optimization_barrier(
        (gather_call(rows[:, EARLY:], embed_table), lists)
    )
    got_late = exchange(picked_late, "shard")

    rep = lax.axis_index("rep")
    everyone = jnp.stack(
        [
            from_before(lists, "rep", k).reshape(OWNERS // GROUP, GROUP, CAP)
            for k in range(REPS)
        ],
        axis=2,
    )
    feature = everyone & (FEATS - 1)
    valid = everyone > 0
    within = feature - rep * PAIR
    ours = valid & (within >= 0) & (within < PAIR)
    target = jnp.where(ours, within * VOC + ((everyone >> 10) & (VOC - 1)), PAIR * VOC)
    group = lax.broadcasted_iota(I32, everyone.shape, 1)
    back = lax.broadcasted_iota(I32, everyone.shape, 2)
    source = (group * REPS + back) * (PAIR * SAMPLES) + jnp.where(
        ours, within * SAMPLES + ((everyone >> 3) & (SAMPLES - 1)), 0
    )
    words = jnp.pad(
        (target << SHIFT) | source,
        ((0, 0), (0, 0), (0, 0), (0, LISTED - CAP)),
        constant_values=(PAIR * VOC) << SHIFT,
    ).reshape(-1)
    below = jnp.sum((valid & (within < 0)).astype(I32), axis=3)
    upto = jnp.sum((valid & (within < PAIR)).astype(I32), axis=3)
    places = lax.broadcasted_iota(I32, below.shape, 1) * REPS + lax.broadcasted_iota(
        I32, below.shape, 2
    )
    first_word = (places * LISTED + below).reshape(-1)
    trips = ((upto - below + ACCS - 1) >> (ACCS.bit_length() - 1)).reshape(-1)
    sums_early = pool_call(got_early, packed, 0)
    got_late, sums_early, words, first_word, trips = lax.optimization_barrier(
        (got_late, sums_early, words, first_word, trips)
    )

    logits, grads, first_local = tower_call(
        got_late,
        packed,
        sums_early,
        labels.reshape(SAMPLES, 1),
        norm_gain.reshape(1, WIDTH),
        cross_weight,
        cross_bias,
        deep_weight,
        deep_bias,
        out_weight.reshape(1, WIDTH),
    )
    mine = jnp.stack(
        [
            from_before(lax.dynamic_index_in_dim(grads, (rep + k) % REPS, 0, False), "rep", k)
            for k in range(REPS)
        ]
    )
    mine, first_local = lax.optimization_barrier((mine, first_local))
    all_grads = lax.all_gather(mine, "shard", axis=0)
    quarter = summed(exchange(first_local, "rep"))
    eight = summed(exchange(quarter.reshape(OWNERS, 8, WIDTH), "shard"))
    first_grad = lax.all_gather(
        in_order(eight, "rep", rep), "shard", axis=0, tiled=True
    ).astype(F32)

    part = scatter_call(words, first_word, trips, all_grads).reshape(PAIR, VOC, EMB)
    parts = [part] + [from_before(part, "rep", k) for k in range(1, REPS)]
    slots = feature_slot[lax.axis_index("shard")]
    holder = (rep - jnp.arange(REPS, dtype=I32)) % REPS
    features = holder[:, None] * PAIR + jnp.arange(PAIR, dtype=I32)[None, :]
    row_grad = finish_call(slots[features.reshape(-1)], parts)
    return (row_grad, first_grad, logits.reshape(SAMPLES))


def solution(mesh):
    both = ("rep", "shard")
    in_specs = (
        P("shard", None),
        P(both, None),
        P(both, None, None),
        P(both, None),
        P(),
        P(both),
        P(),
        P(),
        P(),
        P(),
        P(),
        P(),
    )
    out_specs = (P("shard", None), P(), P(both))
    return jax.shard_map(body, mesh=mesh, in_specs=in_specs, out_specs=out_specs, check_vma=False)
```

```python
import functools

import jax
import jax.numpy as jnp
import numpy as np
from jax import lax
from jax.experimental import pallas as pl
from jax.experimental.pallas import tpu as pltpu
from jax.sharding import PartitionSpec as P

BF = jnp.bfloat16
F32 = jnp.float32
I32 = jnp.int32
OWNERS = 32
FEATS = 8
KEYS = OWNERS * FEATS
CAP = 512
VOC = 1024
ROWS = FEATS * VOC
EMB = 128
BAGS = 1024
SAMPLES = 128
WIDTH = FEATS * EMB
IDS = 8192
REPS = 4
PAIR = FEATS // REPS
LANES = 256
IDROWS = IDS // LANES
ACCS = 16
POOLED = 8
GROUP = 4
LISTED = CAP + 64
LISTS = 4
SOURCES = GROUP * REPS * PAIR * SAMPLES
SHIFT = 13
EARLY = 128
VMEM = 62 * 1024 * 1024

NT = (((1,), (1,)), ((), ()))
TN = (((0,), (0,)), ((), ()))


def dot(a, b, dims=(((1,), (0,)), ((), ()))):
    return lax.dot_general(a, b, dims, preferred_element_type=F32)


def iota(shape, dim):
    return lax.broadcasted_iota(I32, shape, dim)


def onehot(cond):
    return jnp.where(cond, 1.0, 0.0).astype(BF)


def index_kernel(
    ids_in, owner_in, len_in, slot_ref, out_ref, send_ref, ids_ref, owner_ref, len_ref, bag_ref, key_ref
):
    for r in range(IDROWS):
        ids_ref[r : r + 1, :] = ids_in[:, r * LANES : (r + 1) * LANES]
        owner_ref[r : r + 1, :] = owner_in[:, r * LANES : (r + 1) * LANES]
    for r in range(BAGS // 128):
        len_ref[r : r + 1, :] = len_in[:, r * 128 : (r + 1) * 128]
    lens = len_ref[...].astype(F32).astype(BF)
    incl128 = onehot(iota((128, 128), 0) <= iota((128, 128), 1))
    within = dot(lens, incl128)
    total = jnp.broadcast_to(within[:, 127:128], (8, 128))
    high = jnp.floor(total * (1.0 / 256.0))
    low = total - high * 256.0
    below8 = onehot(iota((8, 8), 1) < iota((8, 8), 0))
    before = dot(below8, high.astype(BF)) * 256.0 + dot(below8, low.astype(BF))
    start = (within + before).astype(I32) - len_ref[...]
    start_hi = start >> 8
    start_lo = start & 255
    marks = jnp.zeros((IDROWS, LANES), F32)
    for r in range(8):
        a = onehot(iota((IDROWS, 128), 0) == start_hi[r : r + 1, :])
        b = onehot(iota((LANES, 128), 0) == start_lo[r : r + 1, :])
        marks = marks + dot(a, b, NT)
    marks = marks.astype(BF)
    incl = onehot(iota((LANES, LANES), 0) <= iota((LANES, LANES), 1))
    strict = onehot(iota((LANES, LANES), 0) < iota((LANES, LANES), 1))
    row_counts = dot(marks, jnp.ones((LANES, LANES), BF))
    below = onehot(iota((IDROWS, IDROWS), 1) < iota((IDROWS, IDROWS), 0))
    bag = (dot(marks, incl) + dot(below, row_counts.astype(BF))).astype(I32) - 1
    bag_ref[...] = bag
    key_ref[...] = owner_ref[...] * FEATS + (bag & (FEATS - 1))

    key_iota = iota((KEYS, LANES), 0)

    def count(r, acc):
        return acc + jnp.where(key_iota == key_ref[pl.ds(r, 1), :], 1.0, 0.0)

    counts = lax.fori_loop(0, IDROWS, count, jnp.zeros((KEYS, LANES), F32), unroll=4)
    totals = dot(counts.astype(BF), jnp.ones((LANES, LANES), BF))
    high = jnp.floor(totals * (1.0 / 256.0))
    low = totals - high * 256.0
    ki, kj = iota((KEYS, KEYS), 0), iota((KEYS, KEYS), 1)
    earlier = onehot((ki // FEATS == kj // FEATS) & (kj < ki))
    carry0 = dot(earlier, high.astype(BF)) * 256.0 + dot(earlier, low.astype(BF))

    rank_iota = iota((CAP // 2, LANES), 0)
    owner_iota = iota((OWNERS, LANES), 0)

    of_owner = onehot(iota((KEYS, OWNERS), 0) // FEATS == iota((KEYS, OWNERS), 1))
    by_owner = dot(of_owner, slot_ref[...].astype(F32).astype(BF), NT)
    is_feature = (iota((KEYS, FEATS), 0) & (FEATS - 1)) == iota((KEYS, FEATS), 1)
    slots = jnp.sum(jnp.where(is_feature, by_owner, 0.0), axis=1, keepdims=True)
    carry0 = carry0 + jnp.broadcast_to(slots, (KEYS, LANES)) * VOC

    def place(r, state):
        carry, acc = state
        same = key_iota == key_ref[pl.ds(r, 1), :]
        hot = jnp.where(same, 1.0, 0.0)
        prefix = dot(hot.astype(BF), strict)
        found = jnp.sum(jnp.where(same, prefix + carry, 0.0), axis=0, keepdims=True)
        found = found.astype(I32)
        rank = found & (VOC - 1)
        row = (found - rank) + ids_ref[pl.ds(r, 1), :]
        value = (1 << 23) + (row << 10) + bag_ref[pl.ds(r, 1), :]
        mine = owner_iota == owner_ref[pl.ds(r, 1), :]
        pieces = [
            jnp.where(mine, jnp.broadcast_to(p.astype(F32), (OWNERS, LANES)), 0.0)
            for p in (value & 255, (value >> 8) & 255, value >> 16)
        ]
        left = jnp.concatenate(pieces, axis=0).astype(BF)
        upper = rank >= CAP // 2
        left = jnp.concatenate([left * onehot(~upper), left * onehot(upper)], axis=0)
        right = onehot(rank_iota == (rank & (CAP // 2 - 1)))
        acc = acc + dot(left, right, NT)
        carry = carry + (prefix + hot)[:, LANES - 1 : LANES]
        return carry, acc

    _, acc = lax.fori_loop(
        0, IDROWS, place, (carry0, jnp.zeros((6 * OWNERS, CAP // 2), F32)), unroll=8
    )
    acc = jnp.concatenate([acc[: 3 * OWNERS], acc[3 * OWNERS :]], axis=1).astype(I32)
    packed = acc[:OWNERS] + (acc[OWNERS : 2 * OWNERS] << 8) + (acc[2 * OWNERS :] << 16)
    out_ref[...] = packed
    for c in range(CAP // 128):
        send_ref[:, c, :] = packed[:, c * 128 : (c + 1) * 128]


def index_call(ids, owners, lengths, slots):
    return pl.pallas_call(
        index_kernel,
        out_shape=[
            jax.ShapeDtypeStruct((OWNERS, CAP), I32),
            jax.ShapeDtypeStruct((OWNERS, CAP // 128, 128), I32),
        ],
        scratch_shapes=[
            pltpu.VMEM((IDROWS, LANES), I32),
            pltpu.VMEM((IDROWS, LANES), I32),
            pltpu.VMEM((BAGS // 128, 128), I32),
            pltpu.VMEM((IDROWS, LANES), I32),
            pltpu.VMEM((IDROWS, LANES), I32),
        ],
        compiler_params=pltpu.CompilerParams(vmem_limit_bytes=VMEM),
        name="index",
    )(ids, owners, lengths, slots)


def gather_kernel(offset, row_ref, table_ref, out_ref, wide, picked):
    step = pl.program_id(0)
    depth = out_ref.shape[1]

    @pl.when(step == 0)
    def _():
        wide[...] = table_ref[...].astype(F32)

    for part in range(LISTS):
        base = (step * LISTS + part) * CAP + offset

        def some(i, _):
            at = i * 32
            rows = [wide[pl.ds(row_ref[base + at + j], 1), :] for j in range(32)]
            for j in range(32):
                picked[pl.ds(part * depth + at + j, 1), :] = rows[j]
            return 0

        lax.fori_loop(0, depth // 32, some, 0)
        out_ref[part] = picked[part * depth : (part + 1) * depth, :].astype(BF)


def gather_call(rows, table, offset, depth):
    return pl.pallas_call(
        functools.partial(gather_kernel, offset),
        out_shape=jax.ShapeDtypeStruct((OWNERS, depth, EMB), BF),
        grid_spec=pltpu.PrefetchScalarGridSpec(
            num_scalar_prefetch=1,
            grid=(OWNERS // LISTS,),
            in_specs=[pl.BlockSpec((ROWS, EMB), lambda i, r: (0, 0))],
            out_specs=pl.BlockSpec((LISTS, depth, EMB), lambda i, r: (i, 0, 0)),
            scratch_shapes=[pltpu.VMEM((ROWS, EMB), F32), pltpu.VMEM((LISTS * depth, EMB), F32)],
        ),
        compiler_params=pltpu.CompilerParams(vmem_limit_bytes=VMEM),
        name="gather",
    )(rows, table)


def sums_of(packed_ref, got_ref, step, at):
    rows, masked = [], []
    depth = got_ref.shape[1]
    group = packed_ref[pl.ds(pl.multiple_of(step * POOLED, POOLED), POOLED), at : at + depth]
    for i in range(POOLED):
        packed = group[i : i + 1, :]
        bag = packed & (BAGS - 1)
        sample = jnp.where(packed > 0, bag >> 3, -1)
        rows.append(onehot(iota((SAMPLES, depth), 0) == sample))
        feature = jnp.broadcast_to((bag & (FEATS - 1)).astype(F32), (EMB, depth)).T.astype(BF)
        own = got_ref[i]
        masked.append(
            jnp.concatenate(
                [jnp.where(feature == f, own, jnp.zeros((), BF)) for f in range(FEATS)], axis=1
            )
        )
    return dot(jnp.concatenate(rows, axis=1), jnp.concatenate(masked, axis=0))


def pool_kernel(at, got_ref, packed_ref, out_ref):
    step = pl.program_id(0)
    sums = sums_of(packed_ref, got_ref, step, at)

    @pl.when(step == 0)
    def _():
        out_ref[...] = sums

    @pl.when(step > 0)
    def _():
        out_ref[...] += sums


def pool_call(got, packed, at):
    depth = got.shape[1]
    return pl.pallas_call(
        functools.partial(pool_kernel, at),
        out_shape=jax.ShapeDtypeStruct((SAMPLES, WIDTH), F32),
        grid=(OWNERS // POOLED,),
        in_specs=[
            pl.BlockSpec((POOLED, depth, EMB), lambda i: (i, 0, 0)),
            pl.BlockSpec((OWNERS, CAP), lambda i: (0, 0)),
        ],
        out_specs=pl.BlockSpec((SAMPLES, WIDTH), lambda i: (0, 0)),
        compiler_params=pltpu.CompilerParams(vmem_limit_bytes=VMEM),
        name="pool",
    )(got, packed)


def sigmoid(x):
    return 1.0 / (1.0 + jnp.exp(-x))


def tower_kernel(
    at,
    rep_ref,
    got_ref,
    packed_ref,
    earlier_ref,
    labels_ref,
    gain_ref,
    cbias_ref,
    dbias_ref,
    out_w_ref,
    cross_hbm,
    deep_hbm,
    logits_ref,
    first_ref,
    *refs,
):
    grad_refs = refs[:REPS]
    pooled_ref, cross_w, deep_w, start_ref, cross_t, deep_t, gx_ref, sems, result_ref = refs[REPS:]
    step = pl.program_id(0)

    def cross_copy(layer):
        return pltpu.make_async_copy(cross_hbm.at[layer], cross_w.at[layer], sems.at[layer])

    def deep_copy(layer):
        return pltpu.make_async_copy(deep_hbm.at[layer], deep_w.at[layer], sems.at[3 + layer])

    @pl.when(step == 0)
    def _():
        for layer in range(3):
            cross_copy(layer).start()
        for layer in range(3):
            deep_copy(layer).start()
        pooled_ref[...] = earlier_ref[...]

    pooled_ref[...] += sums_of(packed_ref, got_ref, step, at)

    @pl.when(step == OWNERS // POOLED - 1)
    def _():
        gain = gain_ref[...]
        pooled = pooled_ref[...]
        inverse = lax.rsqrt(jnp.mean(pooled * pooled, axis=1, keepdims=True) + 1e-06)
        start = (pooled * inverse * gain).astype(BF)
        start_ref[...] = start
        current = start
        for layer in range(3):
            cross_copy(layer).wait()
            product = dot(current, cross_w[layer]) + cbias_ref[layer : layer + 1, :]
            cross_t[layer] = product
            current = (start_ref[...].astype(F32) * product + current.astype(F32)).astype(BF)
        for layer in range(3):
            deep_copy(layer).wait()
            product = dot(current, deep_w[layer]) + dbias_ref[layer : layer + 1, :]
            deep_t[layer] = product
            current = (product * sigmoid(product)).astype(BF)
        out_w = out_w_ref[...]
        logits = jnp.sum(current.astype(F32) * out_w, axis=1, keepdims=True)
        logits_ref[...] = logits
        error = sigmoid(logits) - labels_ref[...].astype(F32)
        grad = error * out_w
        for layer in (2, 1, 0):
            product = deep_t[layer]
            sig = sigmoid(product)
            masked = (grad * sig * (1.0 + product * (1.0 - sig))).astype(BF)
            grad = dot(masked, deep_w[layer], NT)
        gx_ref[...] = jnp.zeros_like(gx_ref)
        for layer in (2, 1, 0):
            crossed = (grad * start_ref[...].astype(F32)).astype(BF)
            gx_ref[...] += grad * cross_t[layer]
            grad = grad + dot(crossed, cross_w[layer], NT)
            if layer == 0:
                outer = dot(start_ref[...], crossed, TN).reshape(OWNERS, REPS, 8, WIDTH)
                for r in range(REPS):
                    first_ref[r] = outer[:, r].reshape(OWNERS * 8, WIDTH).astype(BF)
        scaled = (gx_ref[...] + grad) * gain
        pooled = pooled_ref[...]
        inverse = lax.rsqrt(jnp.mean(pooled * pooled, axis=1, keepdims=True) + 1e-06)
        mean = jnp.mean(scaled * pooled, axis=1, keepdims=True)
        result = (inverse * scaled - pooled * (inverse * inverse * inverse) * mean).astype(BF)
        result_ref[...] = result
        for k in range(REPS):
            block = (rep_ref[0] + k) & (REPS - 1)
            columns = pl.ds(pl.multiple_of(block * (PAIR * EMB), PAIR * EMB), PAIR * EMB)
            grad_refs[k][...] = result_ref[:, columns]


def tower_call(rep, got, packed, earlier, labels, gain, cross, cbias, deep, dbias, out_w):
    def whole(shape):
        return pl.BlockSpec(shape, lambda i: (0,) * len(shape))

    return pl.pallas_call(
        functools.partial(tower_kernel, CAP - got.shape[1]),
        grid=(OWNERS // POOLED,),
        in_specs=[
            pl.BlockSpec(memory_space=pltpu.SMEM),
            pl.BlockSpec((POOLED, got.shape[1], EMB), lambda i: (i, 0, 0)),
            whole((OWNERS, CAP)),
            whole((SAMPLES, WIDTH)),
            whole((SAMPLES, 1)),
            whole((1, WIDTH)),
            whole((3, WIDTH)),
            whole((3, WIDTH)),
            whole((1, WIDTH)),
            pl.BlockSpec(memory_space=pl.ANY),
            pl.BlockSpec(memory_space=pl.ANY),
        ],
        out_specs=[
            whole((SAMPLES, 1)),
            whole((REPS, OWNERS * 8, WIDTH)),
        ]
        + [whole((SAMPLES, PAIR * EMB))] * REPS,
        out_shape=[
            jax.ShapeDtypeStruct((SAMPLES, 1), F32),
            jax.ShapeDtypeStruct((REPS, OWNERS * 8, WIDTH), BF),
        ]
        + [jax.ShapeDtypeStruct((SAMPLES, PAIR * EMB), BF)] * REPS,
        scratch_shapes=[
            pltpu.VMEM((SAMPLES, WIDTH), F32),
            pltpu.VMEM((3, WIDTH, WIDTH), BF),
            pltpu.VMEM((3, WIDTH, WIDTH), BF),
            pltpu.VMEM((SAMPLES, WIDTH), BF),
            pltpu.VMEM((3, SAMPLES, WIDTH), F32),
            pltpu.VMEM((3, SAMPLES, WIDTH), F32),
            pltpu.VMEM((SAMPLES, WIDTH), F32),
            pltpu.SemaphoreType.DMA((6,)),
            pltpu.VMEM((SAMPLES, WIDTH), BF),
        ],
        compiler_params=pltpu.CompilerParams(vmem_limit_bytes=VMEM),
        name="tower",
    )(rep, got, packed, earlier, labels, gain, cbias, dbias, out_w, cross, deep)


def scatter_kernel(first_ref, trips_ref, word_ref, grads_ref, out_ref, wide, *accs):
    step = pl.program_id(0)

    @pl.when(step == 0)
    def _():
        for acc in accs:
            acc[...] = jnp.zeros_like(acc)

    group = grads_ref.shape[0]
    for g in range(group):
        for r in range(REPS):
            block = grads_ref[g, r]
            base = (g * REPS + r) * PAIR * SAMPLES
            for f in range(PAIR):
                wide[base + f * SAMPLES : base + (f + 1) * SAMPLES, :] = block[
                    :, f * EMB : (f + 1) * EMB
                ].astype(F32)

    def device(k, _):
        listed = step * group * REPS + k
        first = first_ref[listed]

        def some(i, _):
            at = first + i * ACCS
            words = [word_ref[at + j] for j in range(ACCS)]
            rows = [wide[pl.ds(word & (SOURCES - 1), 1), :] for word in words]
            olds = [accs[j][pl.ds(words[j] >> SHIFT, 1), :] for j in range(ACCS)]
            for j in range(ACCS):
                accs[j][pl.ds(words[j] >> SHIFT, 1), :] = olds[j] + rows[j]
            return 0

        lax.fori_loop(0, trips_ref[listed], some, 0)
        return 0

    lax.fori_loop(0, group * REPS, device, 0)

    @pl.when(step == pl.num_programs(0) - 1)
    def _():
        total = accs[0][: PAIR * VOC, :]
        for acc in accs[1:]:
            total = total + acc[: PAIR * VOC, :]
        out_ref[...] = total.astype(out_ref.dtype)


def scatter_call(words, first, trips, grads, group=GROUP):
    rows = PAIR * VOC
    return pl.pallas_call(
        scatter_kernel,
        out_shape=jax.ShapeDtypeStruct((rows, EMB), BF),
        grid_spec=pltpu.PrefetchScalarGridSpec(
            num_scalar_prefetch=2,
            grid=(OWNERS // group,),
            in_specs=[
                pl.BlockSpec(
                    (group * REPS * LISTED,), lambda i, *_: (i,), memory_space=pltpu.SMEM
                ),
                pl.BlockSpec(
                    (group, REPS, SAMPLES, PAIR * EMB), lambda i, *_: (i, 0, 0, 0)
                ),
            ],
            out_specs=pl.BlockSpec((rows, EMB), lambda i, *_: (0, 0)),
            scratch_shapes=[pltpu.VMEM((group * REPS * PAIR * SAMPLES, EMB), F32)]
            + [pltpu.VMEM((rows + 8, EMB), F32) for _ in range(ACCS)],
        ),
        compiler_params=pltpu.CompilerParams(vmem_limit_bytes=VMEM),
        name="scatter",
    )(first, trips, words, grads)


def finish_kernel(place_ref, *refs):
    parts, out, wide, sems = refs[:REPS], refs[REPS], refs[REPS + 1], refs[REPS + 2]
    copies = []
    for k in range(REPS):
        for f in range(PAIR):
            n = k * PAIR + f
            wide[n] = parts[k][f].astype(F32)
            to = pl.multiple_of(place_ref[n] * VOC, VOC)
            copies.append(
                pltpu.make_async_copy(wide.at[n], out.at[pl.ds(to, VOC), :], sems.at[n])
            )
            copies[-1].start()
    for copy in copies:
        copy.wait()


def finish_call(places, parts):
    return pl.pallas_call(
        finish_kernel,
        out_shape=jax.ShapeDtypeStruct((ROWS, EMB), F32),
        in_specs=[pl.BlockSpec(memory_space=pltpu.SMEM)]
        + [pl.BlockSpec(memory_space=pltpu.VMEM) for _ in parts],
        out_specs=pl.BlockSpec(memory_space=pl.ANY),
        scratch_shapes=[
            pltpu.VMEM((FEATS, VOC, EMB), F32),
            pltpu.SemaphoreType.DMA((FEATS,)),
        ],
        compiler_params=pltpu.CompilerParams(vmem_limit_bytes=16 * 1024 * 1024),
        name="finish",
    )(places, *parts)


def from_before(x, axis, k):
    if k == 0:
        return x
    n = lax.axis_size(axis)
    return lax.ppermute(x, axis, [(i, (i + k) % n) for i in range(n)])


def in_order(x, axis, me):
    n = lax.axis_size(axis)
    back = [from_before(x, axis, k) for k in range(n)]
    twice = jnp.concatenate([back[(n - 1 - i) % n] for i in range(2 * n - 1)])
    return lax.dynamic_slice_in_dim(twice, (n - 1 - me) * x.shape[0], n * x.shape[0])


def summed(x):
    return jnp.sum(x.astype(F32), axis=0).astype(BF)


def body(
    embed_table,
    row_ids,
    row_owner,
    lengths,
    feature_slot,
    labels,
    norm_gain,
    cross_weight,
    cross_bias,
    deep_weight,
    deep_bias,
    out_weight,
):
    packed, sent = index_call(
        row_ids,
        row_owner.reshape(1, IDS),
        lengths,
        feature_slot.T,
    )
    asked = lax.all_to_all(sent, "shard", split_axis=0, concat_axis=0, tiled=True)
    rows = ((asked >> 10) & (ROWS - 1)).reshape(-1)

    def exchange(x, axis):
        return lax.all_to_all(x, axis, split_axis=0, concat_axis=0, tiled=True)

    picked_early = gather_call(rows, embed_table, 0, EARLY)
    picked_early, lists = lax.optimization_barrier((picked_early, asked))
    got_early = exchange(picked_early, "shard")
    picked_late, lists = lax.optimization_barrier(
        (gather_call(rows, embed_table, EARLY, CAP - EARLY), lists)
    )
    got_late = exchange(picked_late, "shard")

    rep = lax.axis_index("rep")
    everyone = jnp.stack(
        [
            from_before(lists, "rep", k).reshape(OWNERS // GROUP, GROUP, CAP)
            for k in range(REPS)
        ],
        axis=2,
    )
    feature = everyone & (FEATS - 1)
    valid = everyone > 0
    within = feature - rep * PAIR
    ours = valid & (within >= 0) & (within < PAIR)
    target = jnp.where(ours, within * VOC + ((everyone >> 10) & (VOC - 1)), PAIR * VOC)
    group = lax.broadcasted_iota(I32, everyone.shape, 1)
    back = lax.broadcasted_iota(I32, everyone.shape, 2)
    source = (group * REPS + back) * (PAIR * SAMPLES) + jnp.where(
        ours, within * SAMPLES + ((everyone >> 3) & (SAMPLES - 1)), 0
    )
    words = jnp.pad(
        (target << SHIFT) | source,
        ((0, 0), (0, 0), (0, 0), (0, LISTED - CAP)),
        constant_values=(PAIR * VOC) << SHIFT,
    ).reshape(-1)
    below = jnp.sum((valid & (within < 0)).astype(I32), axis=3)
    upto = jnp.sum((valid & (within < PAIR)).astype(I32), axis=3)
    places = lax.broadcasted_iota(I32, below.shape, 1) * REPS + lax.broadcasted_iota(
        I32, below.shape, 2
    )
    first_word = (places * LISTED + below).reshape(-1)
    trips = ((upto - below + ACCS - 1) >> (ACCS.bit_length() - 1)).reshape(-1)
    sums_early = pool_call(got_early, packed, 0)
    got_late, sums_early, words, first_word, trips = lax.optimization_barrier(
        (got_late, sums_early, words, first_word, trips)
    )

    logits, first_local, *grads = tower_call(
        rep.reshape(1),
        got_late,
        packed,
        sums_early,
        labels.reshape(SAMPLES, 1),
        norm_gain.reshape(1, WIDTH),
        cross_weight,
        cross_bias,
        deep_weight,
        deep_bias,
        out_weight.reshape(1, WIDTH),
    )
    mine = jnp.stack([from_before(grads[k], "rep", k) for k in range(REPS)])
    mine, first_local = lax.optimization_barrier((mine, first_local))
    all_grads = lax.all_gather(mine, "shard", axis=0)
    quarter = summed(exchange(first_local, "rep"))
    eight = summed(exchange(quarter.reshape(OWNERS, 8, WIDTH), "shard"))
    first_grad = lax.all_gather(
        in_order(eight, "rep", rep), "shard", axis=0, tiled=True
    ).astype(F32)

    part = scatter_call(words, first_word, trips, all_grads).reshape(PAIR, VOC, EMB)
    parts = [part] + [from_before(part, "rep", k) for k in range(1, REPS)]
    slots = feature_slot[lax.axis_index("shard")]
    holder = (rep - jnp.arange(REPS, dtype=I32)) % REPS
    features = holder[:, None] * PAIR + jnp.arange(PAIR, dtype=I32)[None, :]
    row_grad = finish_call(slots[features.reshape(-1)], parts)
    return (row_grad, first_grad, logits.reshape(SAMPLES))


def solution(mesh):
    both = ("rep", "shard")
    in_specs = (
        P("shard", None),
        P(both, None),
        P(both, None, None),
        P(both, None),
        P(),
        P(both),
        P(),
        P(),
        P(),
        P(),
        P(),
        P(),
    )
    out_specs = (P("shard", None), P(), P(both))
    return jax.shard_map(body, mesh=mesh, in_specs=in_specs, out_specs=out_specs, check_vma=False)
```

```python
import functools

import jax
import jax.numpy as jnp
import numpy as np
from jax import lax
from jax.experimental import pallas as pl
from jax.experimental.pallas import tpu as pltpu
from jax.sharding import PartitionSpec as P

BF = jnp.bfloat16
F32 = jnp.float32
I32 = jnp.int32
OWNERS = 32
FEATS = 8
KEYS = OWNERS * FEATS
CAP = 512
VOC = 1024
ROWS = FEATS * VOC
EMB = 128
BAGS = 1024
SAMPLES = 128
WIDTH = FEATS * EMB
IDS = 8192
REPS = 4
PAIR = FEATS // REPS
LANES = 256
IDROWS = IDS // LANES
ACCS = 16
POOLED = 16
GROUP = 4
LISTED = CAP + 64
LISTS = 8
SOURCES = GROUP * REPS * PAIR * SAMPLES
SHIFT = 13
EARLY = 128
VMEM = 62 * 1024 * 1024

NT = (((1,), (1,)), ((), ()))
TN = (((0,), (0,)), ((), ()))


def dot(a, b, dims=(((1,), (0,)), ((), ()))):
    return lax.dot_general(a, b, dims, preferred_element_type=F32)


def iota(shape, dim):
    return lax.broadcasted_iota(I32, shape, dim)


def onehot(cond):
    return jnp.where(cond, 1.0, 0.0).astype(BF)


def index_kernel(
    ids_in, owner_in, len_in, slot_ref, out_ref, send_ref, ids_ref, owner_ref, len_ref, bag_ref, key_ref
):
    for r in range(IDROWS):
        ids_ref[r : r + 1, :] = ids_in[:, r * LANES : (r + 1) * LANES]
        owner_ref[r : r + 1, :] = owner_in[:, r * LANES : (r + 1) * LANES]
    for r in range(BAGS // 128):
        len_ref[r : r + 1, :] = len_in[:, r * 128 : (r + 1) * 128]
    lens = len_ref[...].astype(F32).astype(BF)
    incl128 = onehot(iota((128, 128), 0) <= iota((128, 128), 1))
    within = dot(lens, incl128)
    total = jnp.broadcast_to(within[:, 127:128], (8, 128))
    high = jnp.floor(total * (1.0 / 256.0))
    low = total - high * 256.0
    below8 = onehot(iota((8, 8), 1) < iota((8, 8), 0))
    before = dot(below8, high.astype(BF)) * 256.0 + dot(below8, low.astype(BF))
    start = (within + before).astype(I32) - len_ref[...]
    start_hi = start >> 8
    start_lo = start & 255
    marks = jnp.zeros((IDROWS, LANES), F32)
    for r in range(8):
        a = onehot(iota((IDROWS, 128), 0) == start_hi[r : r + 1, :])
        b = onehot(iota((LANES, 128), 0) == start_lo[r : r + 1, :])
        marks = marks + dot(a, b, NT)
    marks = marks.astype(BF)
    incl = onehot(iota((LANES, LANES), 0) <= iota((LANES, LANES), 1))
    strict = onehot(iota((LANES, LANES), 0) < iota((LANES, LANES), 1))
    row_counts = dot(marks, jnp.ones((LANES, LANES), BF))
    below = onehot(iota((IDROWS, IDROWS), 1) < iota((IDROWS, IDROWS), 0))
    bag = (dot(marks, incl) + dot(below, row_counts.astype(BF))).astype(I32) - 1
    bag_ref[...] = bag
    key_ref[...] = owner_ref[...] * FEATS + (bag & (FEATS - 1))

    key_iota = iota((KEYS, LANES), 0)

    def count(r, acc):
        return acc + jnp.where(key_iota == key_ref[pl.ds(r, 1), :], 1.0, 0.0)

    counts = lax.fori_loop(0, IDROWS, count, jnp.zeros((KEYS, LANES), F32), unroll=4)
    totals = dot(counts.astype(BF), jnp.ones((LANES, LANES), BF))
    high = jnp.floor(totals * (1.0 / 256.0))
    low = totals - high * 256.0
    ki, kj = iota((KEYS, KEYS), 0), iota((KEYS, KEYS), 1)
    earlier = onehot((ki // FEATS == kj // FEATS) & (kj < ki))
    carry0 = dot(earlier, high.astype(BF)) * 256.0 + dot(earlier, low.astype(BF))

    rank_iota = iota((CAP // 2, LANES), 0)
    owner_iota = iota((OWNERS, LANES), 0)

    of_owner = onehot(iota((KEYS, OWNERS), 0) // FEATS == iota((KEYS, OWNERS), 1))
    by_owner = dot(of_owner, slot_ref[...].astype(F32).astype(BF), NT)
    is_feature = (iota((KEYS, FEATS), 0) & (FEATS - 1)) == iota((KEYS, FEATS), 1)
    slots = jnp.sum(jnp.where(is_feature, by_owner, 0.0), axis=1, keepdims=True)
    carry0 = carry0 + jnp.broadcast_to(slots, (KEYS, LANES)) * VOC

    def place(r, state):
        carry, acc = state
        same = key_iota == key_ref[pl.ds(r, 1), :]
        hot = jnp.where(same, 1.0, 0.0)
        prefix = dot(hot.astype(BF), strict)
        found = jnp.sum(jnp.where(same, prefix + carry, 0.0), axis=0, keepdims=True)
        found = found.astype(I32)
        rank = found & (VOC - 1)
        row = (found - rank) + ids_ref[pl.ds(r, 1), :]
        value = (1 << 23) + (row << 10) + bag_ref[pl.ds(r, 1), :]
        mine = owner_iota == owner_ref[pl.ds(r, 1), :]
        pieces = [
            jnp.where(mine, jnp.broadcast_to(p.astype(F32), (OWNERS, LANES)), 0.0)
            for p in (value & 255, (value >> 8) & 255, value >> 16)
        ]
        left = jnp.concatenate(pieces, axis=0).astype(BF)
        upper = rank >= CAP // 2
        left = jnp.concatenate([left * onehot(~upper), left * onehot(upper)], axis=0)
        right = onehot(rank_iota == (rank & (CAP // 2 - 1)))
        acc = acc + dot(left, right, NT)
        carry = carry + (prefix + hot)[:, LANES - 1 : LANES]
        return carry, acc

    _, acc = lax.fori_loop(
        0, IDROWS, place, (carry0, jnp.zeros((6 * OWNERS, CAP // 2), F32)), unroll=IDROWS
    )
    acc = jnp.concatenate([acc[: 3 * OWNERS], acc[3 * OWNERS :]], axis=1).astype(I32)
    packed = acc[:OWNERS] + (acc[OWNERS : 2 * OWNERS] << 8) + (acc[2 * OWNERS :] << 16)
    out_ref[...] = packed
    for c in range(CAP // 128):
        send_ref[:, c, :] = packed[:, c * 128 : (c + 1) * 128]


def index_call(ids, owners, lengths, slots):
    return pl.pallas_call(
        index_kernel,
        out_shape=[
            jax.ShapeDtypeStruct((OWNERS, CAP), I32),
            jax.ShapeDtypeStruct((OWNERS, CAP // 128, 128), I32),
        ],
        scratch_shapes=[
            pltpu.VMEM((IDROWS, LANES), I32),
            pltpu.VMEM((IDROWS, LANES), I32),
            pltpu.VMEM((BAGS // 128, 128), I32),
            pltpu.VMEM((IDROWS, LANES), I32),
            pltpu.VMEM((IDROWS, LANES), I32),
        ],
        compiler_params=pltpu.CompilerParams(vmem_limit_bytes=VMEM),
        name="index",
    )(ids, owners, lengths, slots)


def gather_kernel(offset, row_ref, table_ref, out_ref, wide, picked):
    step = pl.program_id(0)
    depth = out_ref.shape[1]

    @pl.when(step == 0)
    def _():
        wide[...] = table_ref[...].astype(F32)

    for part in range(LISTS):
        base = part * CAP + offset

        def some(i, _):
            at = i * 32
            rows = [wide[pl.ds(row_ref[base + at + j], 1), :] for j in range(32)]
            for j in range(32):
                picked[pl.ds(part * depth + at + j, 1), :] = rows[j]
            return 0

        lax.fori_loop(0, depth // 32, some, 0)
        out_ref[part] = picked[part * depth : (part + 1) * depth, :].astype(BF)


def gather_call(rows, table, offset, depth):
    return pl.pallas_call(
        functools.partial(gather_kernel, offset),
        out_shape=jax.ShapeDtypeStruct((OWNERS, depth, EMB), BF),
        grid=(OWNERS // LISTS,),
        in_specs=[
            pl.BlockSpec((LISTS * CAP,), lambda i: (i,), memory_space=pltpu.SMEM),
            pl.BlockSpec((ROWS, EMB), lambda i: (0, 0)),
        ],
        out_specs=pl.BlockSpec((LISTS, depth, EMB), lambda i: (i, 0, 0)),
        scratch_shapes=[pltpu.VMEM((ROWS, EMB), F32), pltpu.VMEM((LISTS * depth, EMB), F32)],
        compiler_params=pltpu.CompilerParams(vmem_limit_bytes=VMEM),
        name="gather",
    )(rows, table)


def sums_of(packed_ref, got_ref, step, at):
    rows, masked = [], []
    depth = got_ref.shape[1]
    group = packed_ref[pl.ds(pl.multiple_of(step * POOLED, POOLED), POOLED), at : at + depth]
    for i in range(POOLED):
        packed = group[i : i + 1, :]
        bag = packed & (BAGS - 1)
        sample = jnp.where(packed > 0, bag >> 3, -1)
        rows.append(onehot(iota((SAMPLES, depth), 0) == sample))
        feature = jnp.broadcast_to((bag & (FEATS - 1)).astype(F32), (EMB, depth)).T.astype(BF)
        own = got_ref[i]
        masked.append(
            jnp.concatenate(
                [jnp.where(feature == f, own, jnp.zeros((), BF)) for f in range(FEATS)], axis=1
            )
        )
    return dot(jnp.concatenate(rows, axis=1), jnp.concatenate(masked, axis=0))


def pool_kernel(at, got_ref, packed_ref, out_ref):
    step = pl.program_id(0)
    sums = sums_of(packed_ref, got_ref, step, at)

    @pl.when(step == 0)
    def _():
        out_ref[...] = sums

    @pl.when(step > 0)
    def _():
        out_ref[...] += sums


def pool_call(got, packed, at):
    depth = got.shape[1]
    return pl.pallas_call(
        functools.partial(pool_kernel, at),
        out_shape=jax.ShapeDtypeStruct((SAMPLES, WIDTH), F32),
        grid=(OWNERS // POOLED,),
        in_specs=[
            pl.BlockSpec((POOLED, depth, EMB), lambda i: (i, 0, 0)),
            pl.BlockSpec((OWNERS, CAP), lambda i: (0, 0)),
        ],
        out_specs=pl.BlockSpec((SAMPLES, WIDTH), lambda i: (0, 0)),
        compiler_params=pltpu.CompilerParams(vmem_limit_bytes=VMEM),
        name="pool",
    )(got, packed)


def sigmoid(x):
    return 1.0 / (1.0 + jnp.exp(-x))


def tower_kernel(
    at,
    rep_ref,
    got_ref,
    packed_ref,
    earlier_ref,
    labels_ref,
    gain_ref,
    cbias_ref,
    dbias_ref,
    out_w_ref,
    cross_hbm,
    deep_hbm,
    logits_ref,
    first_ref,
    *refs,
):
    grad_refs = refs[:REPS]
    pooled_ref, cross_w, deep_w, start_ref, cross_t, deep_t, gx_ref, sems, result_ref = refs[REPS:]
    step = pl.program_id(0)

    def cross_copy(layer):
        return pltpu.make_async_copy(cross_hbm.at[layer], cross_w.at[layer], sems.at[layer])

    def deep_copy(layer):
        return pltpu.make_async_copy(deep_hbm.at[layer], deep_w.at[layer], sems.at[3 + layer])

    @pl.when(step == 0)
    def _():
        for layer in range(3):
            cross_copy(layer).start()
        for layer in range(3):
            deep_copy(layer).start()
        pooled_ref[...] = earlier_ref[...]

    pooled_ref[...] += sums_of(packed_ref, got_ref, step, at)

    @pl.when(step == OWNERS // POOLED - 1)
    def _():
        gain = gain_ref[...]
        pooled = pooled_ref[...]
        inverse = lax.rsqrt(jnp.mean(pooled * pooled, axis=1, keepdims=True) + 1e-06)
        start = (pooled * inverse * gain).astype(BF)
        start_ref[...] = start
        current = start
        for layer in range(3):
            cross_copy(layer).wait()
            product = dot(current, cross_w[layer]) + cbias_ref[layer : layer + 1, :]
            cross_t[layer] = product
            current = (start_ref[...].astype(F32) * product + current.astype(F32)).astype(BF)
        for layer in range(3):
            deep_copy(layer).wait()
            product = dot(current, deep_w[layer]) + dbias_ref[layer : layer + 1, :]
            deep_t[layer] = product
            current = (product * sigmoid(product)).astype(BF)
        out_w = out_w_ref[...]
        logits = jnp.sum(current.astype(F32) * out_w, axis=1, keepdims=True)
        logits_ref[...] = logits
        error = sigmoid(logits) - labels_ref[...].astype(F32)
        grad = error * out_w
        for layer in (2, 1, 0):
            product = deep_t[layer]
            sig = sigmoid(product)
            masked = (grad * sig * (1.0 + product * (1.0 - sig))).astype(BF)
            grad = dot(masked, deep_w[layer], NT)
        gx_ref[...] = jnp.zeros_like(gx_ref)
        for layer in (2, 1, 0):
            crossed = (grad * start_ref[...].astype(F32)).astype(BF)
            gx_ref[...] += grad * cross_t[layer]
            grad = grad + dot(crossed, cross_w[layer], NT)
            if layer == 0:
                outer = dot(start_ref[...], crossed, TN).reshape(OWNERS, REPS, 8, WIDTH)
                for r in range(REPS):
                    first_ref[r] = outer[:, r].reshape(OWNERS * 8, WIDTH).astype(BF)
        scaled = (gx_ref[...] + grad) * gain
        pooled = pooled_ref[...]
        inverse = lax.rsqrt(jnp.mean(pooled * pooled, axis=1, keepdims=True) + 1e-06)
        mean = jnp.mean(scaled * pooled, axis=1, keepdims=True)
        result = (inverse * scaled - pooled * (inverse * inverse * inverse) * mean).astype(BF)
        result_ref[...] = result
        for k in range(REPS):
            block = (rep_ref[0] + k) & (REPS - 1)
            columns = pl.ds(pl.multiple_of(block * (PAIR * EMB), PAIR * EMB), PAIR * EMB)
            grad_refs[k][...] = result_ref[:, columns]


def tower_call(rep, got, packed, earlier, labels, gain, cross, cbias, deep, dbias, out_w):
    def whole(shape):
        return pl.BlockSpec(shape, lambda i: (0,) * len(shape))

    return pl.pallas_call(
        functools.partial(tower_kernel, CAP - got.shape[1]),
        grid=(OWNERS // POOLED,),
        in_specs=[
            pl.BlockSpec(memory_space=pltpu.SMEM),
            pl.BlockSpec((POOLED, got.shape[1], EMB), lambda i: (i, 0, 0)),
            whole((OWNERS, CAP)),
            whole((SAMPLES, WIDTH)),
            whole((SAMPLES, 1)),
            whole((1, WIDTH)),
            whole((3, WIDTH)),
            whole((3, WIDTH)),
            whole((1, WIDTH)),
            pl.BlockSpec(memory_space=pl.ANY),
            pl.BlockSpec(memory_space=pl.ANY),
        ],
        out_specs=[
            whole((SAMPLES, 1)),
            whole((REPS, OWNERS * 8, WIDTH)),
        ]
        + [whole((SAMPLES, PAIR * EMB))] * REPS,
        out_shape=[
            jax.ShapeDtypeStruct((SAMPLES, 1), F32),
            jax.ShapeDtypeStruct((REPS, OWNERS * 8, WIDTH), BF),
        ]
        + [jax.ShapeDtypeStruct((SAMPLES, PAIR * EMB), BF)] * REPS,
        scratch_shapes=[
            pltpu.VMEM((SAMPLES, WIDTH), F32),
            pltpu.VMEM((3, WIDTH, WIDTH), BF),
            pltpu.VMEM((3, WIDTH, WIDTH), BF),
            pltpu.VMEM((SAMPLES, WIDTH), BF),
            pltpu.VMEM((3, SAMPLES, WIDTH), F32),
            pltpu.VMEM((3, SAMPLES, WIDTH), F32),
            pltpu.VMEM((SAMPLES, WIDTH), F32),
            pltpu.SemaphoreType.DMA((6,)),
            pltpu.VMEM((SAMPLES, WIDTH), BF),
        ],
        compiler_params=pltpu.CompilerParams(vmem_limit_bytes=VMEM),
        name="tower",
    )(rep, got, packed, earlier, labels, gain, cbias, dbias, out_w, cross, deep)


def scatter_kernel(first_ref, trips_ref, word_ref, grads_ref, out_ref, wide, *accs):
    step = pl.program_id(0)

    @pl.when(step == 0)
    def _():
        for acc in accs:
            acc[...] = jnp.zeros_like(acc)

    group = grads_ref.shape[0]
    for g in range(group):
        for r in range(REPS):
            block = grads_ref[g, r]
            base = (g * REPS + r) * PAIR * SAMPLES
            for f in range(PAIR):
                wide[base + f * SAMPLES : base + (f + 1) * SAMPLES, :] = block[
                    :, f * EMB : (f + 1) * EMB
                ].astype(F32)

    def device(k, _):
        listed = step * group * REPS + k
        first = first_ref[listed]

        def some(i, _):
            at = first + i * ACCS
            words = [word_ref[at + j] for j in range(ACCS)]
            rows = [wide[pl.ds(word & (SOURCES - 1), 1), :] for word in words]
            olds = [accs[j][pl.ds(words[j] >> SHIFT, 1), :] for j in range(ACCS)]
            for j in range(ACCS):
                accs[j][pl.ds(words[j] >> SHIFT, 1), :] = olds[j] + rows[j]
            return 0

        lax.fori_loop(0, trips_ref[listed], some, 0)
        return 0

    lax.fori_loop(0, group * REPS, device, 0)

    @pl.when(step == pl.num_programs(0) - 1)
    def _():
        total = accs[0][: PAIR * VOC, :]
        for acc in accs[1:]:
            total = total + acc[: PAIR * VOC, :]
        out_ref[...] = total.astype(out_ref.dtype)


def scatter_call(words, first, trips, grads, group=GROUP):
    rows = PAIR * VOC
    return pl.pallas_call(
        scatter_kernel,
        out_shape=jax.ShapeDtypeStruct((rows, EMB), BF),
        grid_spec=pltpu.PrefetchScalarGridSpec(
            num_scalar_prefetch=2,
            grid=(OWNERS // group,),
            in_specs=[
                pl.BlockSpec(
                    (group * REPS * LISTED,), lambda i, *_: (i,), memory_space=pltpu.SMEM
                ),
                pl.BlockSpec(
                    (group, REPS, SAMPLES, PAIR * EMB), lambda i, *_: (i, 0, 0, 0)
                ),
            ],
            out_specs=pl.BlockSpec((rows, EMB), lambda i, *_: (0, 0)),
            scratch_shapes=[pltpu.VMEM((group * REPS * PAIR * SAMPLES, EMB), F32)]
            + [pltpu.VMEM((rows + 8, EMB), F32) for _ in range(ACCS)],
        ),
        compiler_params=pltpu.CompilerParams(vmem_limit_bytes=VMEM),
        name="scatter",
    )(first, trips, words, grads)


def finish_kernel(place_ref, *refs):
    parts, out, wide, sems = refs[:REPS], refs[REPS], refs[REPS + 1], refs[REPS + 2]
    copies = []
    for k in range(REPS):
        for f in range(PAIR):
            n = k * PAIR + f
            wide[n] = parts[k][f].astype(F32)
            to = pl.multiple_of(place_ref[n] * VOC, VOC)
            copies.append(
                pltpu.make_async_copy(wide.at[n], out.at[pl.ds(to, VOC), :], sems.at[n])
            )
            copies[-1].start()
    for copy in copies:
        copy.wait()


def finish_call(places, parts):
    return pl.pallas_call(
        finish_kernel,
        out_shape=jax.ShapeDtypeStruct((ROWS, EMB), F32),
        in_specs=[pl.BlockSpec(memory_space=pltpu.SMEM)]
        + [pl.BlockSpec(memory_space=pltpu.VMEM) for _ in parts],
        out_specs=pl.BlockSpec(memory_space=pl.ANY),
        scratch_shapes=[
            pltpu.VMEM((FEATS, VOC, EMB), F32),
            pltpu.SemaphoreType.DMA((FEATS,)),
        ],
        compiler_params=pltpu.CompilerParams(vmem_limit_bytes=16 * 1024 * 1024),
        name="finish",
    )(places, *parts)


def from_before(x, axis, k):
    if k == 0:
        return x
    n = lax.axis_size(axis)
    return lax.ppermute(x, axis, [(i, (i + k) % n) for i in range(n)])


def in_order(x, axis, me):
    n = lax.axis_size(axis)
    back = [from_before(x, axis, k) for k in range(n)]
    twice = jnp.concatenate([back[(n - 1 - i) % n] for i in range(2 * n - 1)])
    return lax.dynamic_slice_in_dim(twice, (n - 1 - me) * x.shape[0], n * x.shape[0])


def summed(x):
    return jnp.sum(x.astype(F32), axis=0).astype(BF)


def body(
    embed_table,
    row_ids,
    row_owner,
    lengths,
    feature_slot,
    labels,
    norm_gain,
    cross_weight,
    cross_bias,
    deep_weight,
    deep_bias,
    out_weight,
):
    packed, sent = index_call(
        row_ids,
        row_owner.reshape(1, IDS),
        lengths,
        feature_slot.T,
    )
    asked = lax.all_to_all(sent, "shard", split_axis=0, concat_axis=0, tiled=True)
    rows = ((asked >> 10) & (ROWS - 1)).reshape(-1)

    def exchange(x, axis):
        return lax.all_to_all(x, axis, split_axis=0, concat_axis=0, tiled=True)

    picked_early = gather_call(rows, embed_table, 0, EARLY)
    picked_early, lists = lax.optimization_barrier((picked_early, asked))
    got_early = exchange(picked_early, "shard")
    picked_late, lists = lax.optimization_barrier(
        (gather_call(rows, embed_table, EARLY, CAP - EARLY), lists)
    )
    got_late = exchange(picked_late, "shard")

    rep = lax.axis_index("rep")
    everyone = jnp.stack(
        [
            from_before(lists, "rep", k).reshape(OWNERS // GROUP, GROUP, CAP)
            for k in range(REPS)
        ],
        axis=2,
    )
    feature = everyone & (FEATS - 1)
    valid = everyone > 0
    within = feature - rep * PAIR
    ours = valid & (within >= 0) & (within < PAIR)
    target = jnp.where(ours, within * VOC + ((everyone >> 10) & (VOC - 1)), PAIR * VOC)
    group = lax.broadcasted_iota(I32, everyone.shape, 1)
    back = lax.broadcasted_iota(I32, everyone.shape, 2)
    source = (group * REPS + back) * (PAIR * SAMPLES) + jnp.where(
        ours, within * SAMPLES + ((everyone >> 3) & (SAMPLES - 1)), 0
    )
    words = jnp.pad(
        (target << SHIFT) | source,
        ((0, 0), (0, 0), (0, 0), (0, LISTED - CAP)),
        constant_values=(PAIR * VOC) << SHIFT,
    ).reshape(-1)
    below = jnp.sum((valid & (within < 0)).astype(I32), axis=3)
    upto = jnp.sum((valid & (within < PAIR)).astype(I32), axis=3)
    places = lax.broadcasted_iota(I32, below.shape, 1) * REPS + lax.broadcasted_iota(
        I32, below.shape, 2
    )
    first_word = (places * LISTED + below).reshape(-1)
    trips = ((upto - below + ACCS - 1) >> (ACCS.bit_length() - 1)).reshape(-1)
    sums_early = pool_call(got_early, packed, 0)
    got_late, sums_early, words, first_word, trips = lax.optimization_barrier(
        (got_late, sums_early, words, first_word, trips)
    )

    logits, first_local, *grads = tower_call(
        rep.reshape(1),
        got_late,
        packed,
        sums_early,
        labels.reshape(SAMPLES, 1),
        norm_gain.reshape(1, WIDTH),
        cross_weight,
        cross_bias,
        deep_weight,
        deep_bias,
        out_weight.reshape(1, WIDTH),
    )
    mine = jnp.stack([from_before(grads[k], "rep", k) for k in range(REPS)])
    mine, first_local = lax.optimization_barrier((mine, first_local))
    all_grads = lax.all_gather(mine, "shard", axis=0)
    quarter = summed(exchange(first_local, "rep"))
    eight = summed(exchange(quarter.reshape(OWNERS, 8, WIDTH), "shard"))
    first_grad = lax.all_gather(
        in_order(eight, "rep", rep), "shard", axis=0, tiled=True
    ).astype(F32)

    part = scatter_call(words, first_word, trips, all_grads).reshape(PAIR, VOC, EMB)
    parts = [part] + [from_before(part, "rep", k) for k in range(1, REPS)]
    slots = feature_slot[lax.axis_index("shard")]
    holder = (rep - jnp.arange(REPS, dtype=I32)) % REPS
    features = holder[:, None] * PAIR + jnp.arange(PAIR, dtype=I32)[None, :]
    row_grad = finish_call(slots[features.reshape(-1)], parts)
    return (row_grad, first_grad, logits.reshape(SAMPLES))


def solution(mesh):
    both = ("rep", "shard")
    in_specs = (
        P("shard", None),
        P(both, None),
        P(both, None, None),
        P(both, None),
        P(),
        P(both),
        P(),
        P(),
        P(),
        P(),
        P(),
        P(),
    )
    out_specs = (P("shard", None), P(), P(both))
    return jax.shard_map(body, mesh=mesh, in_specs=in_specs, out_specs=out_specs, check_vma=False)
```

```python
import functools

import jax
import jax.numpy as jnp
import numpy as np
from jax import lax
from jax.experimental import pallas as pl
from jax.experimental.pallas import tpu as pltpu
from jax.sharding import PartitionSpec as P

BF = jnp.bfloat16
F32 = jnp.float32
I32 = jnp.int32
OWNERS = 32
FEATS = 8
KEYS = OWNERS * FEATS
CAP = 512
VOC = 1024
ROWS = FEATS * VOC
EMB = 128
BAGS = 1024
SAMPLES = 128
WIDTH = FEATS * EMB
IDS = 8192
REPS = 4
PAIR = FEATS // REPS
LANES = 256
IDROWS = IDS // LANES
ACCS = 16
POOLED = 16
GROUP = 4
LISTED = CAP + 64
LISTS = 8
SOURCES = GROUP * REPS * PAIR * SAMPLES
SHIFT = 13
EARLY = 128
VMEM = 62 * 1024 * 1024

NT = (((1,), (1,)), ((), ()))
TN = (((0,), (0,)), ((), ()))


def dot(a, b, dims=(((1,), (0,)), ((), ()))):
    return lax.dot_general(a, b, dims, preferred_element_type=F32)


def iota(shape, dim):
    return lax.broadcasted_iota(I32, shape, dim)


def onehot(cond):
    return jnp.where(cond, 1.0, 0.0).astype(BF)


def index_kernel(
    ids_in, owner_in, len_in, slot_ref, out_ref, send_ref, ids_ref, owner_ref, len_ref, bag_ref, key_ref
):
    for r in range(IDROWS):
        ids_ref[r : r + 1, :] = ids_in[:, r * LANES : (r + 1) * LANES]
        owner_ref[r : r + 1, :] = owner_in[:, r * LANES : (r + 1) * LANES]
    for r in range(BAGS // 128):
        len_ref[r : r + 1, :] = len_in[:, r * 128 : (r + 1) * 128]
    lens = len_ref[...].astype(F32).astype(BF)
    incl128 = onehot(iota((128, 128), 0) <= iota((128, 128), 1))
    within = dot(lens, incl128)
    total = jnp.broadcast_to(within[:, 127:128], (8, 128))
    high = jnp.floor(total * (1.0 / 256.0))
    low = total - high * 256.0
    below8 = onehot(iota((8, 8), 1) < iota((8, 8), 0))
    before = dot(below8, high.astype(BF)) * 256.0 + dot(below8, low.astype(BF))
    start = (within + before).astype(I32) - len_ref[...]
    start_hi = start >> 8
    start_lo = start & 255
    marks = jnp.zeros((IDROWS, LANES), F32)
    for r in range(8):
        a = onehot(iota((IDROWS, 128), 0) == start_hi[r : r + 1, :])
        b = onehot(iota((LANES, 128), 0) == start_lo[r : r + 1, :])
        marks = marks + dot(a, b, NT)
    marks = marks.astype(BF)
    incl = onehot(iota((LANES, LANES), 0) <= iota((LANES, LANES), 1))
    strict = onehot(iota((LANES, LANES), 0) < iota((LANES, LANES), 1))
    row_counts = dot(marks, jnp.ones((LANES, LANES), BF))
    below = onehot(iota((IDROWS, IDROWS), 1) < iota((IDROWS, IDROWS), 0))
    bag = (dot(marks, incl) + dot(below, row_counts.astype(BF))).astype(I32) - 1
    bag_ref[...] = bag
    key_ref[...] = owner_ref[...] * FEATS + (bag & (FEATS - 1))

    key_iota = iota((KEYS, LANES), 0)

    def count(r, acc):
        return acc + jnp.where(key_iota == key_ref[pl.ds(r, 1), :], 1.0, 0.0)

    counts = lax.fori_loop(0, IDROWS, count, jnp.zeros((KEYS, LANES), F32), unroll=4)
    totals = dot(counts.astype(BF), jnp.ones((LANES, LANES), BF))
    high = jnp.floor(totals * (1.0 / 256.0))
    low = totals - high * 256.0
    ki, kj = iota((KEYS, KEYS), 0), iota((KEYS, KEYS), 1)
    earlier = onehot((ki // FEATS == kj // FEATS) & (kj < ki))
    carry0 = dot(earlier, high.astype(BF)) * 256.0 + dot(earlier, low.astype(BF))

    rank_iota = iota((CAP // 2, LANES), 0)
    owner_iota = iota((OWNERS, LANES), 0)

    of_owner = onehot(iota((KEYS, OWNERS), 0) // FEATS == iota((KEYS, OWNERS), 1))
    by_owner = dot(of_owner, slot_ref[...].astype(F32).astype(BF), NT)
    is_feature = (iota((KEYS, FEATS), 0) & (FEATS - 1)) == iota((KEYS, FEATS), 1)
    slots = jnp.sum(jnp.where(is_feature, by_owner, 0.0), axis=1, keepdims=True)
    carry0 = carry0 + jnp.broadcast_to(slots, (KEYS, LANES)) * VOC

    def place(r, state):
        carry, acc = state
        same = key_iota == key_ref[pl.ds(r, 1), :]
        hot = jnp.where(same, 1.0, 0.0)
        prefix = dot(hot.astype(BF), strict)
        found = jnp.sum(jnp.where(same, prefix + carry, 0.0), axis=0, keepdims=True)
        found = found.astype(I32)
        rank = found & (VOC - 1)
        row = (found - rank) + ids_ref[pl.ds(r, 1), :]
        value = (1 << 23) + (row << 10) + bag_ref[pl.ds(r, 1), :]
        mine = owner_iota == owner_ref[pl.ds(r, 1), :]
        pieces = [
            jnp.where(mine, jnp.broadcast_to(p.astype(F32), (OWNERS, LANES)), 0.0)
            for p in (value & 255, (value >> 8) & 255, value >> 16)
        ]
        left = jnp.concatenate(pieces, axis=0).astype(BF)
        upper = rank >= CAP // 2
        left = jnp.concatenate([left * onehot(~upper), left * onehot(upper)], axis=0)
        right = onehot(rank_iota == (rank & (CAP // 2 - 1)))
        acc = acc + dot(left, right, NT)
        carry = carry + (prefix + hot)[:, LANES - 1 : LANES]
        return carry, acc

    _, acc = lax.fori_loop(
        0, IDROWS, place, (carry0, jnp.zeros((6 * OWNERS, CAP // 2), F32)), unroll=IDROWS
    )
    acc = jnp.concatenate([acc[: 3 * OWNERS], acc[3 * OWNERS :]], axis=1).astype(I32)
    packed = acc[:OWNERS] + (acc[OWNERS : 2 * OWNERS] << 8) + (acc[2 * OWNERS :] << 16)
    out_ref[...] = packed
    for c in range(CAP // 128):
        send_ref[:, c, :] = packed[:, c * 128 : (c + 1) * 128]


def index_call(ids, owners, lengths, slots):
    return pl.pallas_call(
        index_kernel,
        out_shape=[
            jax.ShapeDtypeStruct((OWNERS, CAP), I32),
            jax.ShapeDtypeStruct((OWNERS, CAP // 128, 128), I32),
        ],
        scratch_shapes=[
            pltpu.VMEM((IDROWS, LANES), I32),
            pltpu.VMEM((IDROWS, LANES), I32),
            pltpu.VMEM((BAGS // 128, 128), I32),
            pltpu.VMEM((IDROWS, LANES), I32),
            pltpu.VMEM((IDROWS, LANES), I32),
        ],
        compiler_params=pltpu.CompilerParams(vmem_limit_bytes=VMEM),
        name="index",
    )(ids, owners, lengths, slots)


def gather_kernel(offset, row_ref, table_ref, out_ref, wide, picked):
    step = pl.program_id(0)
    depth = out_ref.shape[1]

    @pl.when(step == 0)
    def _():
        wide[...] = table_ref[...].astype(F32)

    for part in range(LISTS):
        base = part * CAP + offset

        def some(i, _):
            at = i * 32
            rows = [wide[pl.ds(row_ref[base + at + j], 1), :] for j in range(32)]
            for j in range(32):
                picked[pl.ds(part * depth + at + j, 1), :] = rows[j]
            return 0

        lax.fori_loop(0, depth // 32, some, 0)
        out_ref[part] = picked[part * depth : (part + 1) * depth, :].astype(BF)


def gather_call(rows, table, offset, depth):
    return pl.pallas_call(
        functools.partial(gather_kernel, offset),
        out_shape=jax.ShapeDtypeStruct((OWNERS, depth, EMB), BF),
        grid=(OWNERS // LISTS,),
        in_specs=[
            pl.BlockSpec((LISTS * CAP,), lambda i: (i,), memory_space=pltpu.SMEM),
            pl.BlockSpec((ROWS, EMB), lambda i: (0, 0)),
        ],
        out_specs=pl.BlockSpec((LISTS, depth, EMB), lambda i: (i, 0, 0)),
        scratch_shapes=[pltpu.VMEM((ROWS, EMB), F32), pltpu.VMEM((LISTS * depth, EMB), F32)],
        compiler_params=pltpu.CompilerParams(vmem_limit_bytes=VMEM),
        name="gather",
    )(rows, table)


def sums_of(packed_ref, got_ref, step, at):
    rows, masked = [], []
    depth = got_ref.shape[1]
    group = packed_ref[pl.ds(pl.multiple_of(step * POOLED, POOLED), POOLED), at : at + depth]
    for i in range(POOLED):
        packed = group[i : i + 1, :]
        bag = packed & (BAGS - 1)
        sample = jnp.where(packed > 0, bag >> 3, -1)
        rows.append(onehot(iota((SAMPLES, depth), 0) == sample))
        feature = jnp.broadcast_to((bag & (FEATS - 1)).astype(F32), (EMB, depth)).T.astype(BF)
        own = got_ref[i]
        masked.append(
            jnp.concatenate(
                [jnp.where(feature == f, own, jnp.zeros((), BF)) for f in range(FEATS)], axis=1
            )
        )
    return dot(jnp.concatenate(rows, axis=1), jnp.concatenate(masked, axis=0))


def pool_kernel(at, got_ref, packed_ref, out_ref):
    step = pl.program_id(0)
    sums = sums_of(packed_ref, got_ref, step, at)

    @pl.when(step == 0)
    def _():
        out_ref[...] = sums

    @pl.when(step > 0)
    def _():
        out_ref[...] += sums


def pool_call(got, packed, at):
    depth = got.shape[1]
    return pl.pallas_call(
        functools.partial(pool_kernel, at),
        out_shape=jax.ShapeDtypeStruct((SAMPLES, WIDTH), F32),
        grid=(OWNERS // POOLED,),
        in_specs=[
            pl.BlockSpec((POOLED, depth, EMB), lambda i: (i, 0, 0)),
            pl.BlockSpec((OWNERS, CAP), lambda i: (0, 0)),
        ],
        out_specs=pl.BlockSpec((SAMPLES, WIDTH), lambda i: (0, 0)),
        compiler_params=pltpu.CompilerParams(vmem_limit_bytes=VMEM),
        name="pool",
    )(got, packed)


def sigmoid(x):
    return 1.0 / (1.0 + jnp.exp(-x))


def tower_kernel(
    at,
    rep_ref,
    got_ref,
    packed_ref,
    earlier_ref,
    labels_ref,
    gain_ref,
    cbias_ref,
    dbias_ref,
    out_w_ref,
    cross_hbm,
    deep_hbm,
    logits_ref,
    first_ref,
    *refs,
):
    grad_refs = refs[:REPS]
    pooled_ref, cross_w, deep_w, start_ref, cross_t, deep_t, deep_s, gx_ref, sems, result_ref = refs[
        REPS:
    ]
    step = pl.program_id(0)

    def cross_copy(layer):
        return pltpu.make_async_copy(cross_hbm.at[layer], cross_w.at[layer], sems.at[layer])

    def deep_copy(layer):
        return pltpu.make_async_copy(deep_hbm.at[layer], deep_w.at[layer], sems.at[3 + layer])

    @pl.when(step == 0)
    def _():
        for layer in range(3):
            cross_copy(layer).start()
        for layer in range(3):
            deep_copy(layer).start()
        pooled_ref[...] = earlier_ref[...]

    pooled_ref[...] += sums_of(packed_ref, got_ref, step, at)

    @pl.when(step == OWNERS // POOLED - 1)
    def _():
        gain = gain_ref[...]
        pooled = pooled_ref[...]
        inverse = lax.rsqrt(jnp.mean(pooled * pooled, axis=1, keepdims=True) + 1e-06)
        start = (pooled * inverse * gain).astype(BF)
        start_ref[...] = start
        current = start
        for layer in range(3):
            cross_copy(layer).wait()
            product = dot(current, cross_w[layer]) + cbias_ref[layer : layer + 1, :]
            cross_t[layer] = product
            current = (start_ref[...].astype(F32) * product + current.astype(F32)).astype(BF)
        for layer in range(3):
            deep_copy(layer).wait()
            product = dot(current, deep_w[layer]) + dbias_ref[layer : layer + 1, :]
            deep_t[layer] = product
            sig = sigmoid(product)
            deep_s[layer] = sig
            current = (product * sig).astype(BF)
        out_w = out_w_ref[...]
        logits = jnp.sum(current.astype(F32) * out_w, axis=1, keepdims=True)
        logits_ref[...] = logits
        error = sigmoid(logits) - labels_ref[...].astype(F32)
        grad = error * out_w
        for layer in (2, 1, 0):
            product = deep_t[layer]
            sig = deep_s[layer]
            masked = (grad * sig * (1.0 + product * (1.0 - sig))).astype(BF)
            grad = dot(masked, deep_w[layer], NT)
        gx_ref[...] = jnp.zeros_like(gx_ref)
        for layer in (2, 1, 0):
            crossed = (grad * start_ref[...].astype(F32)).astype(BF)
            gx_ref[...] += grad * cross_t[layer]
            grad = grad + dot(crossed, cross_w[layer], NT)
            if layer == 0:
                outer = dot(start_ref[...], crossed, TN).reshape(OWNERS, REPS, 8, WIDTH)
                for r in range(REPS):
                    first_ref[r] = outer[:, r].reshape(OWNERS * 8, WIDTH).astype(BF)
        scaled = (gx_ref[...] + grad) * gain
        pooled = pooled_ref[...]
        inverse = lax.rsqrt(jnp.mean(pooled * pooled, axis=1, keepdims=True) + 1e-06)
        mean = jnp.mean(scaled * pooled, axis=1, keepdims=True)
        result = (inverse * scaled - pooled * (inverse * inverse * inverse) * mean).astype(BF)
        result_ref[...] = result
        for k in range(REPS):
            block = (rep_ref[0] + k) & (REPS - 1)
            columns = pl.ds(pl.multiple_of(block * (PAIR * EMB), PAIR * EMB), PAIR * EMB)
            grad_refs[k][...] = result_ref[:, columns]


def tower_call(rep, got, packed, earlier, labels, gain, cross, cbias, deep, dbias, out_w):
    def whole(shape):
        return pl.BlockSpec(shape, lambda i: (0,) * len(shape))

    return pl.pallas_call(
        functools.partial(tower_kernel, CAP - got.shape[1]),
        grid=(OWNERS // POOLED,),
        in_specs=[
            pl.BlockSpec(memory_space=pltpu.SMEM),
            pl.BlockSpec((POOLED, got.shape[1], EMB), lambda i: (i, 0, 0)),
            whole((OWNERS, CAP)),
            whole((SAMPLES, WIDTH)),
            whole((SAMPLES, 1)),
            whole((1, WIDTH)),
            whole((3, WIDTH)),
            whole((3, WIDTH)),
            whole((1, WIDTH)),
            pl.BlockSpec(memory_space=pl.ANY),
            pl.BlockSpec(memory_space=pl.ANY),
        ],
        out_specs=[
            whole((SAMPLES, 1)),
            whole((REPS, OWNERS * 8, WIDTH)),
        ]
        + [whole((SAMPLES, PAIR * EMB))] * REPS,
        out_shape=[
            jax.ShapeDtypeStruct((SAMPLES, 1), F32),
            jax.ShapeDtypeStruct((REPS, OWNERS * 8, WIDTH), BF),
        ]
        + [jax.ShapeDtypeStruct((SAMPLES, PAIR * EMB), BF)] * REPS,
        scratch_shapes=[
            pltpu.VMEM((SAMPLES, WIDTH), F32),
            pltpu.VMEM((3, WIDTH, WIDTH), BF),
            pltpu.VMEM((3, WIDTH, WIDTH), BF),
            pltpu.VMEM((SAMPLES, WIDTH), BF),
            pltpu.VMEM((3, SAMPLES, WIDTH), F32),
            pltpu.VMEM((3, SAMPLES, WIDTH), F32),
            pltpu.VMEM((3, SAMPLES, WIDTH), F32),
            pltpu.VMEM((SAMPLES, WIDTH), F32),
            pltpu.SemaphoreType.DMA((6,)),
            pltpu.VMEM((SAMPLES, WIDTH), BF),
        ],
        compiler_params=pltpu.CompilerParams(vmem_limit_bytes=VMEM),
        name="tower",
    )(rep, got, packed, earlier, labels, gain, cbias, dbias, out_w, cross, deep)


def scatter_kernel(first_ref, trips_ref, word_ref, grads_ref, out_ref, wide, *accs):
    step = pl.program_id(0)

    @pl.when(step == 0)
    def _():
        for acc in accs:
            acc[...] = jnp.zeros_like(acc)

    group = grads_ref.shape[0]
    for g in range(group):
        for r in range(REPS):
            block = grads_ref[g, r]
            base = (g * REPS + r) * PAIR * SAMPLES
            for f in range(PAIR):
                wide[base + f * SAMPLES : base + (f + 1) * SAMPLES, :] = block[
                    :, f * EMB : (f + 1) * EMB
                ].astype(F32)

    def device(k, _):
        listed = step * group * REPS + k
        first = first_ref[listed]

        def some(i, _):
            at = first + i * ACCS
            words = [word_ref[at + j] for j in range(ACCS)]
            rows = [wide[pl.ds(word & (SOURCES - 1), 1), :] for word in words]
            olds = [accs[j][pl.ds(words[j] >> SHIFT, 1), :] for j in range(ACCS)]
            for j in range(ACCS):
                accs[j][pl.ds(words[j] >> SHIFT, 1), :] = olds[j] + rows[j]
            return 0

        lax.fori_loop(0, trips_ref[listed], some, 0)
        return 0

    lax.fori_loop(0, group * REPS, device, 0)

    @pl.when(step == pl.num_programs(0) - 1)
    def _():
        total = accs[0][: PAIR * VOC, :]
        for acc in accs[1:]:
            total = total + acc[: PAIR * VOC, :]
        out_ref[...] = total.astype(out_ref.dtype)


def scatter_call(words, first, trips, grads, group=GROUP):
    rows = PAIR * VOC
    return pl.pallas_call(
        scatter_kernel,
        out_shape=jax.ShapeDtypeStruct((rows, EMB), BF),
        grid_spec=pltpu.PrefetchScalarGridSpec(
            num_scalar_prefetch=2,
            grid=(OWNERS // group,),
            in_specs=[
                pl.BlockSpec(
                    (group * REPS * LISTED,), lambda i, *_: (i,), memory_space=pltpu.SMEM
                ),
                pl.BlockSpec(
                    (group, REPS, SAMPLES, PAIR * EMB), lambda i, *_: (i, 0, 0, 0)
                ),
            ],
            out_specs=pl.BlockSpec((rows, EMB), lambda i, *_: (0, 0)),
            scratch_shapes=[pltpu.VMEM((group * REPS * PAIR * SAMPLES, EMB), F32)]
            + [pltpu.VMEM((rows + 8, EMB), F32) for _ in range(ACCS)],
        ),
        compiler_params=pltpu.CompilerParams(vmem_limit_bytes=VMEM),
        name="scatter",
    )(first, trips, words, grads)


def finish_kernel(count, place_ref, *refs):
    blocks, (out, wide, sems) = refs[:count], refs[-3:]
    copies = []
    n = 0
    for block in blocks:
        for f in range(block.shape[0]):
            wide[n] = block[f].astype(F32)
            to = pl.multiple_of(place_ref[n] * VOC, VOC)
            copies.append(
                pltpu.make_async_copy(wide.at[n], out.at[pl.ds(to, VOC), :], sems.at[n])
            )
            copies[-1].start()
            n += 1
    for copy in copies:
        copy.wait()


def finish_call(places, blocks, earlier=None):
    more = [] if earlier is None else [earlier]
    total = sum(block.shape[0] for block in blocks)
    return pl.pallas_call(
        functools.partial(finish_kernel, len(blocks)),
        out_shape=jax.ShapeDtypeStruct((ROWS, EMB), F32),
        in_specs=[pl.BlockSpec(memory_space=pltpu.SMEM)]
        + [pl.BlockSpec(memory_space=pltpu.VMEM) for _ in blocks]
        + [pl.BlockSpec(memory_space=pl.ANY) for _ in more],
        out_specs=pl.BlockSpec(memory_space=pl.ANY),
        scratch_shapes=[
            pltpu.VMEM((total, VOC, EMB), F32),
            pltpu.SemaphoreType.DMA((total,)),
        ],
        input_output_aliases={1 + len(blocks): 0} if more else {},
        compiler_params=pltpu.CompilerParams(vmem_limit_bytes=16 * 1024 * 1024),
        name="finish",
    )(places, *blocks, *more)


def from_before(x, axis, k):
    if k == 0:
        return x
    n = lax.axis_size(axis)
    return lax.ppermute(x, axis, [(i, (i + k) % n) for i in range(n)])


def in_order(x, axis, me):
    n = lax.axis_size(axis)
    back = [from_before(x, axis, k) for k in range(n)]
    twice = jnp.concatenate([back[(n - 1 - i) % n] for i in range(2 * n - 1)])
    return lax.dynamic_slice_in_dim(twice, (n - 1 - me) * x.shape[0], n * x.shape[0])


def summed(x):
    return jnp.sum(x.astype(F32), axis=0).astype(BF)


def body(
    embed_table,
    row_ids,
    row_owner,
    lengths,
    feature_slot,
    labels,
    norm_gain,
    cross_weight,
    cross_bias,
    deep_weight,
    deep_bias,
    out_weight,
):
    packed, sent = index_call(
        row_ids,
        row_owner.reshape(1, IDS),
        lengths,
        feature_slot.T,
    )
    asked = lax.all_to_all(sent, "shard", split_axis=0, concat_axis=0, tiled=True)
    rows = ((asked >> 10) & (ROWS - 1)).reshape(-1)

    def exchange(x, axis):
        return lax.all_to_all(x, axis, split_axis=0, concat_axis=0, tiled=True)

    picked_early = gather_call(rows, embed_table, 0, EARLY)
    picked_early, lists = lax.optimization_barrier((picked_early, asked))
    got_early = exchange(picked_early, "shard")
    picked_late, lists = lax.optimization_barrier(
        (gather_call(rows, embed_table, EARLY, CAP - EARLY), lists)
    )
    got_late = exchange(picked_late, "shard")

    rep = lax.axis_index("rep")
    everyone = jnp.stack(
        [
            from_before(lists, "rep", k).reshape(OWNERS // GROUP, GROUP, CAP)
            for k in range(REPS)
        ],
        axis=2,
    )
    feature = everyone & (FEATS - 1)
    valid = everyone > 0
    within = feature - rep * PAIR
    ours = valid & (within >= 0) & (within < PAIR)
    target = jnp.where(ours, within * VOC + ((everyone >> 10) & (VOC - 1)), PAIR * VOC)
    group = lax.broadcasted_iota(I32, everyone.shape, 1)
    back = lax.broadcasted_iota(I32, everyone.shape, 2)
    source = (group * REPS + back) * (PAIR * SAMPLES) + jnp.where(
        ours, within * SAMPLES + ((everyone >> 3) & (SAMPLES - 1)), 0
    )
    words = jnp.pad(
        (target << SHIFT) | source,
        ((0, 0), (0, 0), (0, 0), (0, LISTED - CAP)),
        constant_values=(PAIR * VOC) << SHIFT,
    ).reshape(-1)
    below = jnp.sum((valid & (within < 0)).astype(I32), axis=3)
    upto = jnp.sum((valid & (within < PAIR)).astype(I32), axis=3)
    places = lax.broadcasted_iota(I32, below.shape, 1) * REPS + lax.broadcasted_iota(
        I32, below.shape, 2
    )
    first_word = (places * LISTED + below).reshape(-1)
    trips = ((upto - below + ACCS - 1) >> (ACCS.bit_length() - 1)).reshape(-1)
    sums_early = pool_call(got_early, packed, 0)
    got_late, sums_early, words, first_word, trips = lax.optimization_barrier(
        (got_late, sums_early, words, first_word, trips)
    )

    logits, first_local, *grads = tower_call(
        rep.reshape(1),
        got_late,
        packed,
        sums_early,
        labels.reshape(SAMPLES, 1),
        norm_gain.reshape(1, WIDTH),
        cross_weight,
        cross_bias,
        deep_weight,
        deep_bias,
        out_weight.reshape(1, WIDTH),
    )
    mine = jnp.stack([from_before(grads[k], "rep", k) for k in range(REPS)])
    mine, first_local = lax.optimization_barrier((mine, first_local))
    all_grads = lax.all_gather(mine, "shard", axis=0)
    quarter = summed(exchange(first_local, "rep"))
    eight = summed(exchange(quarter.reshape(OWNERS, 8, WIDTH), "shard"))
    first_grad = lax.all_gather(
        in_order(eight, "rep", rep), "shard", axis=0, tiled=True
    ).astype(F32)

    part = scatter_call(words, first_word, trips, all_grads).reshape(PAIR, VOC, EMB)
    before = from_before(part, "rep", 1)
    after = from_before(part, "rep", REPS - 1)
    across = [
        from_before(before[:1], "rep", 1),
        from_before(after[1:], "rep", REPS - 1),
    ]
    slots = feature_slot[lax.axis_index("shard")]
    holder = (rep - jnp.array([0, 1, 3, 2], I32)) % REPS
    features = holder[:, None] * PAIR + jnp.arange(PAIR, dtype=I32)[None, :]
    places = slots[features.reshape(-1)]
    near, far = places[: 3 * PAIR], places[3 * PAIR :]
    row_grad = finish_call(near, [part, before, after])
    row_grad = finish_call(far, across, row_grad)
    return (row_grad, first_grad, logits.reshape(SAMPLES))


def solution(mesh):
    both = ("rep", "shard")
    in_specs = (
        P("shard", None),
        P(both, None),
        P(both, None, None),
        P(both, None),
        P(),
        P(both),
        P(),
        P(),
        P(),
        P(),
        P(),
        P(),
    )
    out_specs = (P("shard", None), P(), P(both))
    return jax.shard_map(body, mesh=mesh, in_specs=in_specs, out_specs=out_specs, check_vma=False)
```

```python
import functools

import jax
import jax.numpy as jnp
import numpy as np
from jax import lax
from jax.experimental import pallas as pl
from jax.experimental.pallas import tpu as pltpu
from jax.sharding import PartitionSpec as P

BF = jnp.bfloat16
F32 = jnp.float32
I32 = jnp.int32
OWNERS = 32
FEATS = 8
KEYS = OWNERS * FEATS
CAP = 512
VOC = 1024
ROWS = FEATS * VOC
EMB = 128
BAGS = 1024
SAMPLES = 128
WIDTH = FEATS * EMB
IDS = 8192
REPS = 4
PAIR = FEATS // REPS
LANES = 256
IDROWS = IDS // LANES
ACCS = 16
POOLED = 16
GROUP = 4
LISTED = CAP + 64
LISTS = 16
SOURCES = GROUP * REPS * PAIR * SAMPLES
SHIFT = 13
EARLY = 128
VMEM = 62 * 1024 * 1024

NT = (((1,), (1,)), ((), ()))
TN = (((0,), (0,)), ((), ()))


def dot(a, b, dims=(((1,), (0,)), ((), ()))):
    return lax.dot_general(a, b, dims, preferred_element_type=F32)


def iota(shape, dim):
    return lax.broadcasted_iota(I32, shape, dim)


def onehot(cond):
    return jnp.where(cond, 1.0, 0.0).astype(BF)


def index_kernel(
    ids_in, owner_in, len_in, slot_ref, out_ref, send_ref, ids_ref, owner_ref, len_ref, bag_ref, key_ref
):
    for r in range(IDROWS):
        ids_ref[r : r + 1, :] = ids_in[:, r * LANES : (r + 1) * LANES]
        owner_ref[r : r + 1, :] = owner_in[:, r * LANES : (r + 1) * LANES]
    for r in range(BAGS // 128):
        len_ref[r : r + 1, :] = len_in[:, r * 128 : (r + 1) * 128]
    lens = len_ref[...].astype(F32).astype(BF)
    incl128 = onehot(iota((128, 128), 0) <= iota((128, 128), 1))
    within = dot(lens, incl128)
    total = jnp.broadcast_to(within[:, 127:128], (8, 128))
    high = jnp.floor(total * (1.0 / 256.0))
    low = total - high * 256.0
    below8 = onehot(iota((8, 8), 1) < iota((8, 8), 0))
    before = dot(below8, high.astype(BF)) * 256.0 + dot(below8, low.astype(BF))
    start = (within + before).astype(I32) - len_ref[...]
    start_hi = start >> 8
    start_lo = start & 255
    marks = jnp.zeros((IDROWS, LANES), F32)
    for r in range(8):
        a = onehot(iota((IDROWS, 128), 0) == start_hi[r : r + 1, :])
        b = onehot(iota((LANES, 128), 0) == start_lo[r : r + 1, :])
        marks = marks + dot(a, b, NT)
    marks = marks.astype(BF)
    incl = onehot(iota((LANES, LANES), 0) <= iota((LANES, LANES), 1))
    strict = onehot(iota((LANES, LANES), 0) < iota((LANES, LANES), 1))
    row_counts = dot(marks, jnp.ones((LANES, LANES), BF))
    below = onehot(iota((IDROWS, IDROWS), 1) < iota((IDROWS, IDROWS), 0))
    bag = (dot(marks, incl) + dot(below, row_counts.astype(BF))).astype(I32) - 1
    bag_ref[...] = bag
    key_ref[...] = owner_ref[...] * FEATS + (bag & (FEATS - 1))

    key_iota = iota((KEYS, LANES), 0)

    def count(r, acc):
        return acc + jnp.where(key_iota == key_ref[pl.ds(r, 1), :], 1.0, 0.0)

    counts = lax.fori_loop(0, IDROWS, count, jnp.zeros((KEYS, LANES), F32), unroll=4)
    totals = dot(counts.astype(BF), jnp.ones((LANES, LANES), BF))
    high = jnp.floor(totals * (1.0 / 256.0))
    low = totals - high * 256.0
    ki, kj = iota((KEYS, KEYS), 0), iota((KEYS, KEYS), 1)
    earlier = onehot((ki // FEATS == kj // FEATS) & (kj < ki))
    carry0 = dot(earlier, high.astype(BF)) * 256.0 + dot(earlier, low.astype(BF))

    rank_iota = iota((CAP // 2, LANES), 0)
    owner_iota = iota((OWNERS, LANES), 0)

    of_owner = onehot(iota((KEYS, OWNERS), 0) // FEATS == iota((KEYS, OWNERS), 1))
    by_owner = dot(of_owner, slot_ref[...].astype(F32).astype(BF), NT)
    is_feature = (iota((KEYS, FEATS), 0) & (FEATS - 1)) == iota((KEYS, FEATS), 1)
    slots = jnp.sum(jnp.where(is_feature, by_owner, 0.0), axis=1, keepdims=True)
    carry0 = carry0 + jnp.broadcast_to(slots, (KEYS, LANES)) * VOC

    def place(r, state):
        carry, acc = state
        same = key_iota == key_ref[pl.ds(r, 1), :]
        hot = jnp.where(same, 1.0, 0.0)
        prefix = dot(hot.astype(BF), strict)
        found = jnp.sum(jnp.where(same, prefix + carry, 0.0), axis=0, keepdims=True)
        found = found.astype(I32)
        rank = found & (VOC - 1)
        row = (found - rank) + ids_ref[pl.ds(r, 1), :]
        value = (1 << 23) + (row << 10) + bag_ref[pl.ds(r, 1), :]
        mine = owner_iota == owner_ref[pl.ds(r, 1), :]
        pieces = [
            jnp.where(mine, jnp.broadcast_to(p.astype(F32), (OWNERS, LANES)), 0.0)
            for p in (value & 255, (value >> 8) & 255, value >> 16)
        ]
        left = jnp.concatenate(pieces, axis=0).astype(BF)
        upper = rank >= CAP // 2
        left = jnp.concatenate([left * onehot(~upper), left * onehot(upper)], axis=0)
        right = onehot(rank_iota == (rank & (CAP // 2 - 1)))
        acc = acc + dot(left, right, NT)
        carry = carry + (prefix + hot)[:, LANES - 1 : LANES]
        return carry, acc

    _, acc = lax.fori_loop(
        0, IDROWS, place, (carry0, jnp.zeros((6 * OWNERS, CAP // 2), F32)), unroll=IDROWS
    )
    acc = jnp.concatenate([acc[: 3 * OWNERS], acc[3 * OWNERS :]], axis=1).astype(I32)
    packed = acc[:OWNERS] + (acc[OWNERS : 2 * OWNERS] << 8) + (acc[2 * OWNERS :] << 16)
    out_ref[...] = packed
    for c in range(CAP // 128):
        send_ref[:, c, :] = packed[:, c * 128 : (c + 1) * 128]


def index_call(ids, owners, lengths, slots):
    return pl.pallas_call(
        index_kernel,
        out_shape=[
            jax.ShapeDtypeStruct((OWNERS, CAP), I32),
            jax.ShapeDtypeStruct((OWNERS, CAP // 128, 128), I32),
        ],
        scratch_shapes=[
            pltpu.VMEM((IDROWS, LANES), I32),
            pltpu.VMEM((IDROWS, LANES), I32),
            pltpu.VMEM((BAGS // 128, 128), I32),
            pltpu.VMEM((IDROWS, LANES), I32),
            pltpu.VMEM((IDROWS, LANES), I32),
        ],
        compiler_params=pltpu.CompilerParams(vmem_limit_bytes=VMEM),
        name="index",
    )(ids, owners, lengths, slots)


def gather_kernel(offset, row_ref, table_ref, out_ref, wide, picked):
    step = pl.program_id(0)
    depth = out_ref.shape[1]

    @pl.when(step == 0)
    def _():
        wide[...] = table_ref[...].astype(F32)

    for part in range(LISTS):
        base = part * CAP + offset

        def some(i, _):
            at = i * 32
            rows = [wide[pl.ds(row_ref[base + at + j], 1), :] for j in range(32)]
            for j in range(32):
                picked[pl.ds(part * depth + at + j, 1), :] = rows[j]
            return 0

        lax.fori_loop(0, depth // 32, some, 0)
        out_ref[part] = picked[part * depth : (part + 1) * depth, :].astype(BF)


def gather_call(rows, table, offset, depth):
    return pl.pallas_call(
        functools.partial(gather_kernel, offset),
        out_shape=jax.ShapeDtypeStruct((OWNERS, depth, EMB), BF),
        grid=(OWNERS // LISTS,),
        in_specs=[
            pl.BlockSpec((LISTS * CAP,), lambda i: (i,), memory_space=pltpu.SMEM),
            pl.BlockSpec((ROWS, EMB), lambda i: (0, 0)),
        ],
        out_specs=pl.BlockSpec((LISTS, depth, EMB), lambda i: (i, 0, 0)),
        scratch_shapes=[pltpu.VMEM((ROWS, EMB), F32), pltpu.VMEM((LISTS * depth, EMB), F32)],
        compiler_params=pltpu.CompilerParams(vmem_limit_bytes=VMEM),
        name="gather",
    )(rows, table)


def sums_of(packed_ref, got_ref, step, at):
    rows, masked = [], []
    depth = got_ref.shape[1]
    group = packed_ref[pl.ds(pl.multiple_of(step * POOLED, POOLED), POOLED), at : at + depth]
    for i in range(POOLED):
        packed = group[i : i + 1, :]
        bag = packed & (BAGS - 1)
        sample = jnp.where(packed > 0, bag >> 3, -1)
        rows.append(onehot(iota((SAMPLES, depth), 0) == sample))
        feature = jnp.broadcast_to((bag & (FEATS - 1)).astype(F32), (EMB, depth)).T.astype(BF)
        own = got_ref[i]
        masked.append(
            jnp.concatenate(
                [jnp.where(feature == f, own, jnp.zeros((), BF)) for f in range(FEATS)], axis=1
            )
        )
    return dot(jnp.concatenate(rows, axis=1), jnp.concatenate(masked, axis=0))


def pool_kernel(at, got_ref, packed_ref, out_ref):
    step = pl.program_id(0)
    sums = sums_of(packed_ref, got_ref, step, at)

    @pl.when(step == 0)
    def _():
        out_ref[...] = sums

    @pl.when(step > 0)
    def _():
        out_ref[...] += sums


def pool_call(got, packed, at):
    depth = got.shape[1]
    return pl.pallas_call(
        functools.partial(pool_kernel, at),
        out_shape=jax.ShapeDtypeStruct((SAMPLES, WIDTH), F32),
        grid=(OWNERS // POOLED,),
        in_specs=[
            pl.BlockSpec((POOLED, depth, EMB), lambda i: (i, 0, 0)),
            pl.BlockSpec((OWNERS, CAP), lambda i: (0, 0)),
        ],
        out_specs=pl.BlockSpec((SAMPLES, WIDTH), lambda i: (0, 0)),
        compiler_params=pltpu.CompilerParams(vmem_limit_bytes=VMEM),
        name="pool",
    )(got, packed)


def sigmoid(x):
    return 1.0 / (1.0 + jnp.exp(-x))


def tower_kernel(
    at,
    rep_ref,
    got_ref,
    packed_ref,
    earlier_ref,
    labels_ref,
    gain_ref,
    cbias_ref,
    dbias_ref,
    out_w_ref,
    cross_hbm,
    deep_hbm,
    logits_ref,
    first_ref,
    *refs,
):
    grad_refs = refs[:REPS]
    pooled_ref, cross_w, deep_w, start_ref, cross_t, deep_t, deep_s, gx_ref, sems, result_ref = refs[
        REPS:
    ]
    step = pl.program_id(0)

    def cross_copy(layer):
        return pltpu.make_async_copy(cross_hbm.at[layer], cross_w.at[layer], sems.at[layer])

    def deep_copy(layer):
        return pltpu.make_async_copy(deep_hbm.at[layer], deep_w.at[layer], sems.at[3 + layer])

    @pl.when(step == 0)
    def _():
        for layer in range(3):
            cross_copy(layer).start()
        for layer in range(3):
            deep_copy(layer).start()
        pooled_ref[...] = earlier_ref[...]

    pooled_ref[...] += sums_of(packed_ref, got_ref, step, at)

    @pl.when(step == OWNERS // POOLED - 1)
    def _():
        gain = gain_ref[...]
        pooled = pooled_ref[...]
        inverse = lax.rsqrt(jnp.mean(pooled * pooled, axis=1, keepdims=True) + 1e-06)
        start = (pooled * inverse * gain).astype(BF)
        start_ref[...] = start
        current = start
        for layer in range(3):
            cross_copy(layer).wait()
            product = dot(current, cross_w[layer]) + cbias_ref[layer : layer + 1, :]
            cross_t[layer] = product
            current = (start_ref[...].astype(F32) * product + current.astype(F32)).astype(BF)
        for layer in range(3):
            deep_copy(layer).wait()
            product = dot(current, deep_w[layer]) + dbias_ref[layer : layer + 1, :]
            deep_t[layer] = product
            sig = sigmoid(product)
            deep_s[layer] = sig
            current = (product * sig).astype(BF)
        out_w = out_w_ref[...]
        logits = jnp.sum(current.astype(F32) * out_w, axis=1, keepdims=True)
        logits_ref[...] = logits
        error = sigmoid(logits) - labels_ref[...].astype(F32)
        grad = error * out_w
        for layer in (2, 1, 0):
            product = deep_t[layer]
            sig = deep_s[layer]
            masked = (grad * sig * (1.0 + product * (1.0 - sig))).astype(BF)
            grad = dot(masked, deep_w[layer], NT)
        gx_ref[...] = jnp.zeros_like(gx_ref)
        for layer in (2, 1, 0):
            crossed = (grad * start_ref[...].astype(F32)).astype(BF)
            gx_ref[...] += grad * cross_t[layer]
            grad = grad + dot(crossed, cross_w[layer], NT)
            if layer == 0:
                outer = dot(start_ref[...], crossed, TN).reshape(OWNERS, REPS, 8, WIDTH)
                for r in range(REPS):
                    first_ref[r] = outer[:, r].reshape(OWNERS * 8, WIDTH).astype(BF)
        scaled = (gx_ref[...] + grad) * gain
        pooled = pooled_ref[...]
        inverse = lax.rsqrt(jnp.mean(pooled * pooled, axis=1, keepdims=True) + 1e-06)
        mean = jnp.mean(scaled * pooled, axis=1, keepdims=True)
        result = (inverse * scaled - pooled * (inverse * inverse * inverse) * mean).astype(BF)
        result_ref[...] = result
        for k in range(REPS):
            block = (rep_ref[0] + k) & (REPS - 1)
            columns = pl.ds(pl.multiple_of(block * (PAIR * EMB), PAIR * EMB), PAIR * EMB)
            grad_refs[k][...] = result_ref[:, columns]


def tower_call(rep, got, packed, earlier, labels, gain, cross, cbias, deep, dbias, out_w):
    def whole(shape):
        return pl.BlockSpec(shape, lambda i: (0,) * len(shape))

    return pl.pallas_call(
        functools.partial(tower_kernel, CAP - got.shape[1]),
        grid=(OWNERS // POOLED,),
        in_specs=[
            pl.BlockSpec(memory_space=pltpu.SMEM),
            pl.BlockSpec((POOLED, got.shape[1], EMB), lambda i: (i, 0, 0)),
            whole((OWNERS, CAP)),
            whole((SAMPLES, WIDTH)),
            whole((SAMPLES, 1)),
            whole((1, WIDTH)),
            whole((3, WIDTH)),
            whole((3, WIDTH)),
            whole((1, WIDTH)),
            pl.BlockSpec(memory_space=pl.ANY),
            pl.BlockSpec(memory_space=pl.ANY),
        ],
        out_specs=[
            whole((SAMPLES, 1)),
            whole((REPS, OWNERS * 8, WIDTH)),
        ]
        + [whole((SAMPLES, PAIR * EMB))] * REPS,
        out_shape=[
            jax.ShapeDtypeStruct((SAMPLES, 1), F32),
            jax.ShapeDtypeStruct((REPS, OWNERS * 8, WIDTH), BF),
        ]
        + [jax.ShapeDtypeStruct((SAMPLES, PAIR * EMB), BF)] * REPS,
        scratch_shapes=[
            pltpu.VMEM((SAMPLES, WIDTH), F32),
            pltpu.VMEM((3, WIDTH, WIDTH), BF),
            pltpu.VMEM((3, WIDTH, WIDTH), BF),
            pltpu.VMEM((SAMPLES, WIDTH), BF),
            pltpu.VMEM((3, SAMPLES, WIDTH), F32),
            pltpu.VMEM((3, SAMPLES, WIDTH), F32),
            pltpu.VMEM((3, SAMPLES, WIDTH), F32),
            pltpu.VMEM((SAMPLES, WIDTH), F32),
            pltpu.SemaphoreType.DMA((6,)),
            pltpu.VMEM((SAMPLES, WIDTH), BF),
        ],
        compiler_params=pltpu.CompilerParams(vmem_limit_bytes=VMEM),
        name="tower",
    )(rep, got, packed, earlier, labels, gain, cbias, dbias, out_w, cross, deep)


def scatter_kernel(first_ref, trips_ref, word_ref, grads_ref, out_ref, wide, *accs):
    step = pl.program_id(0)

    @pl.when(step == 0)
    def _():
        for acc in accs:
            acc[...] = jnp.zeros_like(acc)

    group = grads_ref.shape[0]
    for g in range(group):
        for r in range(REPS):
            block = grads_ref[g, r]
            base = (g * REPS + r) * PAIR * SAMPLES
            for f in range(PAIR):
                wide[base + f * SAMPLES : base + (f + 1) * SAMPLES, :] = block[
                    :, f * EMB : (f + 1) * EMB
                ].astype(F32)

    def device(k, _):
        listed = step * group * REPS + k
        first = first_ref[listed]

        def some(i, _):
            at = first + i * ACCS
            words = [word_ref[at + j] for j in range(ACCS)]
            rows = [wide[pl.ds(word & (SOURCES - 1), 1), :] for word in words]
            olds = [accs[j][pl.ds(words[j] >> SHIFT, 1), :] for j in range(ACCS)]
            for j in range(ACCS):
                accs[j][pl.ds(words[j] >> SHIFT, 1), :] = olds[j] + rows[j]
            return 0

        lax.fori_loop(0, trips_ref[listed], some, 0)
        return 0

    lax.fori_loop(0, group * REPS, device, 0)

    @pl.when(step == pl.num_programs(0) - 1)
    def _():
        total = accs[0][: PAIR * VOC, :]
        for acc in accs[1:]:
            total = total + acc[: PAIR * VOC, :]
        out_ref[...] = total.astype(out_ref.dtype)


def scatter_call(words, first, trips, grads, group=GROUP):
    rows = PAIR * VOC
    return pl.pallas_call(
        scatter_kernel,
        out_shape=jax.ShapeDtypeStruct((rows, EMB), BF),
        grid_spec=pltpu.PrefetchScalarGridSpec(
            num_scalar_prefetch=2,
            grid=(OWNERS // group,),
            in_specs=[
                pl.BlockSpec(
                    (group * REPS * LISTED,), lambda i, *_: (i,), memory_space=pltpu.SMEM
                ),
                pl.BlockSpec(
                    (group, REPS, SAMPLES, PAIR * EMB), lambda i, *_: (i, 0, 0, 0)
                ),
            ],
            out_specs=pl.BlockSpec((rows, EMB), lambda i, *_: (0, 0)),
            scratch_shapes=[pltpu.VMEM((group * REPS * PAIR * SAMPLES, EMB), F32)]
            + [pltpu.VMEM((rows + 8, EMB), F32) for _ in range(ACCS)],
        ),
        compiler_params=pltpu.CompilerParams(vmem_limit_bytes=VMEM),
        name="scatter",
    )(first, trips, words, grads)


def finish_kernel(count, place_ref, *refs):
    blocks, (out, wide, sems) = refs[:count], refs[-3:]
    copies = []
    n = 0
    for block in blocks:
        for f in range(block.shape[0]):
            wide[n] = block[f].astype(F32)
            to = pl.multiple_of(place_ref[n] * VOC, VOC)
            copies.append(
                pltpu.make_async_copy(wide.at[n], out.at[pl.ds(to, VOC), :], sems.at[n])
            )
            copies[-1].start()
            n += 1
    for copy in copies:
        copy.wait()


def finish_call(places, blocks, earlier=None):
    more = [] if earlier is None else [earlier]
    total = sum(block.shape[0] for block in blocks)
    return pl.pallas_call(
        functools.partial(finish_kernel, len(blocks)),
        out_shape=jax.ShapeDtypeStruct((ROWS, EMB), F32),
        in_specs=[pl.BlockSpec(memory_space=pltpu.SMEM)]
        + [pl.BlockSpec(memory_space=pltpu.VMEM) for _ in blocks]
        + [pl.BlockSpec(memory_space=pl.ANY) for _ in more],
        out_specs=pl.BlockSpec(memory_space=pl.ANY),
        scratch_shapes=[
            pltpu.VMEM((total, VOC, EMB), F32),
            pltpu.SemaphoreType.DMA((total,)),
        ],
        input_output_aliases={1 + len(blocks): 0} if more else {},
        compiler_params=pltpu.CompilerParams(vmem_limit_bytes=16 * 1024 * 1024),
        name="finish",
    )(places, *blocks, *more)


def from_before(x, axis, k):
    if k == 0:
        return x
    n = lax.axis_size(axis)
    return lax.ppermute(x, axis, [(i, (i + k) % n) for i in range(n)])


def in_order(x, axis, me):
    n = lax.axis_size(axis)
    back = [from_before(x, axis, k) for k in range(n)]
    twice = jnp.concatenate([back[(n - 1 - i) % n] for i in range(2 * n - 1)])
    return lax.dynamic_slice_in_dim(twice, (n - 1 - me) * x.shape[0], n * x.shape[0])


def summed(x):
    return jnp.sum(x.astype(F32), axis=0).astype(BF)


def body(
    embed_table,
    row_ids,
    row_owner,
    lengths,
    feature_slot,
    labels,
    norm_gain,
    cross_weight,
    cross_bias,
    deep_weight,
    deep_bias,
    out_weight,
):
    packed, sent = index_call(
        row_ids,
        row_owner.reshape(1, IDS),
        lengths,
        feature_slot.T,
    )
    asked = lax.all_to_all(sent, "shard", split_axis=0, concat_axis=0, tiled=True)
    rows = ((asked >> 10) & (ROWS - 1)).reshape(-1)

    def exchange(x, axis):
        return lax.all_to_all(x, axis, split_axis=0, concat_axis=0, tiled=True)

    picked_early = gather_call(rows, embed_table, 0, EARLY)
    picked_early, lists = lax.optimization_barrier((picked_early, asked))
    got_early = exchange(picked_early, "shard")
    picked_late, lists = lax.optimization_barrier(
        (gather_call(rows, embed_table, EARLY, CAP - EARLY), lists)
    )
    got_late = exchange(picked_late, "shard")

    rep = lax.axis_index("rep")
    everyone = jnp.stack(
        [
            from_before(lists, "rep", k).reshape(OWNERS // GROUP, GROUP, CAP)
            for k in range(REPS)
        ],
        axis=2,
    )
    feature = everyone & (FEATS - 1)
    valid = everyone > 0
    within = feature - rep * PAIR
    ours = valid & (within >= 0) & (within < PAIR)
    target = jnp.where(ours, within * VOC + ((everyone >> 10) & (VOC - 1)), PAIR * VOC)
    group = lax.broadcasted_iota(I32, everyone.shape, 1)
    back = lax.broadcasted_iota(I32, everyone.shape, 2)
    source = (group * REPS + back) * (PAIR * SAMPLES) + jnp.where(
        ours, within * SAMPLES + ((everyone >> 3) & (SAMPLES - 1)), 0
    )
    words = jnp.pad(
        (target << SHIFT) | source,
        ((0, 0), (0, 0), (0, 0), (0, LISTED - CAP)),
        constant_values=(PAIR * VOC) << SHIFT,
    ).reshape(-1)
    below = jnp.sum((valid & (within < 0)).astype(I32), axis=3)
    upto = jnp.sum((valid & (within < PAIR)).astype(I32), axis=3)
    places = lax.broadcasted_iota(I32, below.shape, 1) * REPS + lax.broadcasted_iota(
        I32, below.shape, 2
    )
    first_word = (places * LISTED + below).reshape(-1)
    trips = ((upto - below + ACCS - 1) >> (ACCS.bit_length() - 1)).reshape(-1)
    sums_early = pool_call(got_early, packed, 0)
    slots = feature_slot[lax.axis_index("shard")]
    holder = (rep - jnp.array([0, 1, 3, 2], I32)) % REPS
    features = holder[:, None] * PAIR + jnp.arange(PAIR, dtype=I32)[None, :]
    places = slots[features.reshape(-1)]
    got_late, sums_early, words, first_word, trips, places = lax.optimization_barrier(
        (got_late, sums_early, words, first_word, trips, places)
    )

    logits, first_local, *grads = tower_call(
        rep.reshape(1),
        got_late,
        packed,
        sums_early,
        labels.reshape(SAMPLES, 1),
        norm_gain.reshape(1, WIDTH),
        cross_weight,
        cross_bias,
        deep_weight,
        deep_bias,
        out_weight.reshape(1, WIDTH),
    )
    mine = jnp.stack([from_before(grads[k], "rep", k) for k in range(REPS)])
    mine, first_local = lax.optimization_barrier((mine, first_local))
    all_grads = lax.all_gather(mine, "shard", axis=0)
    quarter = summed(exchange(first_local, "rep"))
    eight = summed(exchange(quarter.reshape(OWNERS, 8, WIDTH), "shard"))
    first_grad = lax.all_gather(
        in_order(eight, "rep", rep), "shard", axis=0, tiled=True
    ).astype(F32)

    part = scatter_call(words, first_word, trips, all_grads).reshape(PAIR, VOC, EMB)
    before = from_before(part, "rep", 1)
    after = from_before(part, "rep", REPS - 1)
    before, after, first_grad = lax.optimization_barrier((before, after, first_grad))
    across = [
        from_before(before[:1], "rep", 1),
        from_before(after[1:], "rep", REPS - 1),
    ]
    near, far = places[: 3 * PAIR], places[3 * PAIR :]
    row_grad = finish_call(near, [part, before, after])
    row_grad = finish_call(far, across, row_grad)
    return (row_grad, first_grad, logits.reshape(SAMPLES))


def solution(mesh):
    both = ("rep", "shard")
    in_specs = (
        P("shard", None),
        P(both, None),
        P(both, None, None),
        P(both, None),
        P(),
        P(both),
        P(),
        P(),
        P(),
        P(),
        P(),
        P(),
    )
    out_specs = (P("shard", None), P(), P(both))
    return jax.shard_map(body, mesh=mesh, in_specs=in_specs, out_specs=out_specs, check_vma=False)
```

```python
import functools

import jax
import jax.numpy as jnp
import numpy as np
from jax import lax
from jax.experimental import pallas as pl
from jax.experimental.pallas import tpu as pltpu
from jax.sharding import PartitionSpec as P

BF = jnp.bfloat16
F32 = jnp.float32
I32 = jnp.int32
OWNERS = 32
FEATS = 8
KEYS = OWNERS * FEATS
CAP = 512
VOC = 1024
ROWS = FEATS * VOC
EMB = 128
BAGS = 1024
SAMPLES = 128
WIDTH = FEATS * EMB
IDS = 8192
REPS = 4
CORES = 2
CHIPS = OWNERS // CORES
PAIR = FEATS // REPS
LANES = 256
IDROWS = IDS // LANES
ACCS = 16
POOLED = 16
GROUP = 4
LISTED = CAP + 64
LISTS = 16
SOURCES = GROUP * REPS * PAIR * SAMPLES
SHIFT = 13
EARLY = 128
VMEM = 62 * 1024 * 1024

NT = (((1,), (1,)), ((), ()))
TN = (((0,), (0,)), ((), ()))


def dot(a, b, dims=(((1,), (0,)), ((), ()))):
    return lax.dot_general(a, b, dims, preferred_element_type=F32)


def iota(shape, dim):
    return lax.broadcasted_iota(I32, shape, dim)


def onehot(cond):
    return jnp.where(cond, 1.0, 0.0).astype(BF)


def index_kernel(
    ids_in, owner_in, len_in, slot_ref, out_ref, send_ref, ids_ref, owner_ref, len_ref, bag_ref, key_ref
):
    for r in range(IDROWS):
        ids_ref[r : r + 1, :] = ids_in[:, r * LANES : (r + 1) * LANES]
        owner_ref[r : r + 1, :] = owner_in[:, r * LANES : (r + 1) * LANES]
    for r in range(BAGS // 128):
        len_ref[r : r + 1, :] = len_in[:, r * 128 : (r + 1) * 128]
    lens = len_ref[...].astype(F32).astype(BF)
    incl128 = onehot(iota((128, 128), 0) <= iota((128, 128), 1))
    within = dot(lens, incl128)
    total = jnp.broadcast_to(within[:, 127:128], (8, 128))
    high = jnp.floor(total * (1.0 / 256.0))
    low = total - high * 256.0
    below8 = onehot(iota((8, 8), 1) < iota((8, 8), 0))
    before = dot(below8, high.astype(BF)) * 256.0 + dot(below8, low.astype(BF))
    start = (within + before).astype(I32) - len_ref[...]
    start_hi = start >> 8
    start_lo = start & 255
    marks = jnp.zeros((IDROWS, LANES), F32)
    for r in range(8):
        a = onehot(iota((IDROWS, 128), 0) == start_hi[r : r + 1, :])
        b = onehot(iota((LANES, 128), 0) == start_lo[r : r + 1, :])
        marks = marks + dot(a, b, NT)
    marks = marks.astype(BF)
    incl = onehot(iota((LANES, LANES), 0) <= iota((LANES, LANES), 1))
    strict = onehot(iota((LANES, LANES), 0) < iota((LANES, LANES), 1))
    row_counts = dot(marks, jnp.ones((LANES, LANES), BF))
    below = onehot(iota((IDROWS, IDROWS), 1) < iota((IDROWS, IDROWS), 0))
    bag = (dot(marks, incl) + dot(below, row_counts.astype(BF))).astype(I32) - 1
    bag_ref[...] = bag
    key_ref[...] = owner_ref[...] * FEATS + (bag & (FEATS - 1))

    key_iota = iota((KEYS, LANES), 0)

    def count(r, acc):
        return acc + jnp.where(key_iota == key_ref[pl.ds(r, 1), :], 1.0, 0.0)

    counts = lax.fori_loop(0, IDROWS, count, jnp.zeros((KEYS, LANES), F32), unroll=4)
    totals = dot(counts.astype(BF), jnp.ones((LANES, LANES), BF))
    high = jnp.floor(totals * (1.0 / 256.0))
    low = totals - high * 256.0
    ki, kj = iota((KEYS, KEYS), 0), iota((KEYS, KEYS), 1)
    earlier = onehot((ki // FEATS == kj // FEATS) & (kj < ki))
    carry0 = dot(earlier, high.astype(BF)) * 256.0 + dot(earlier, low.astype(BF))

    rank_iota = iota((CAP // 2, LANES), 0)
    owner_iota = iota((OWNERS, LANES), 0)

    of_owner = onehot(iota((KEYS, OWNERS), 0) // FEATS == iota((KEYS, OWNERS), 1))
    by_owner = dot(of_owner, slot_ref[...].astype(F32).astype(BF), NT)
    is_feature = (iota((KEYS, FEATS), 0) & (FEATS - 1)) == iota((KEYS, FEATS), 1)
    slots = jnp.sum(jnp.where(is_feature, by_owner, 0.0), axis=1, keepdims=True)
    carry0 = carry0 + jnp.broadcast_to(slots, (KEYS, LANES)) * VOC

    def place(r, state):
        carry, acc = state
        same = key_iota == key_ref[pl.ds(r, 1), :]
        hot = jnp.where(same, 1.0, 0.0)
        prefix = dot(hot.astype(BF), strict)
        found = jnp.sum(jnp.where(same, prefix + carry, 0.0), axis=0, keepdims=True)
        found = found.astype(I32)
        rank = found & (VOC - 1)
        row = (found - rank) + ids_ref[pl.ds(r, 1), :]
        value = (1 << 23) + (row << 10) + bag_ref[pl.ds(r, 1), :]
        mine = owner_iota == owner_ref[pl.ds(r, 1), :]
        pieces = [
            jnp.where(mine, jnp.broadcast_to(p.astype(F32), (OWNERS, LANES)), 0.0)
            for p in (value & 255, (value >> 8) & 255, value >> 16)
        ]
        left = jnp.concatenate(pieces, axis=0).astype(BF)
        upper = rank >= CAP // 2
        left = jnp.concatenate([left * onehot(~upper), left * onehot(upper)], axis=0)
        right = onehot(rank_iota == (rank & (CAP // 2 - 1)))
        acc = acc + dot(left, right, NT)
        carry = carry + (prefix + hot)[:, LANES - 1 : LANES]
        return carry, acc

    _, acc = lax.fori_loop(
        0, IDROWS, place, (carry0, jnp.zeros((6 * OWNERS, CAP // 2), F32)), unroll=IDROWS
    )
    acc = jnp.concatenate([acc[: 3 * OWNERS], acc[3 * OWNERS :]], axis=1).astype(I32)
    packed = acc[:OWNERS] + (acc[OWNERS : 2 * OWNERS] << 8) + (acc[2 * OWNERS :] << 16)
    out_ref[...] = packed
    for c in range(CAP // 128):
        send_ref[:, c, :] = packed[:, c * 128 : (c + 1) * 128]


def index_call(ids, owners, lengths, slots):
    return pl.pallas_call(
        index_kernel,
        out_shape=[
            jax.ShapeDtypeStruct((OWNERS, CAP), I32),
            jax.ShapeDtypeStruct((OWNERS, CAP // 128, 128), I32),
        ],
        scratch_shapes=[
            pltpu.VMEM((IDROWS, LANES), I32),
            pltpu.VMEM((IDROWS, LANES), I32),
            pltpu.VMEM((BAGS // 128, 128), I32),
            pltpu.VMEM((IDROWS, LANES), I32),
            pltpu.VMEM((IDROWS, LANES), I32),
        ],
        compiler_params=pltpu.CompilerParams(vmem_limit_bytes=VMEM),
        name="index",
    )(ids, owners, lengths, slots)


def gather_kernel(offset, row_ref, table_ref, out_ref, wide, picked):
    step = pl.program_id(0)
    depth = out_ref.shape[1]

    @pl.when(step == 0)
    def _():
        wide[...] = table_ref[...].astype(F32)

    for part in range(LISTS):
        base = part * CAP + offset

        def some(i, _):
            at = i * 32
            rows = [wide[pl.ds(row_ref[base + at + j], 1), :] for j in range(32)]
            for j in range(32):
                picked[pl.ds(part * depth + at + j, 1), :] = rows[j]
            return 0

        lax.fori_loop(0, depth // 32, some, 0)
        out_ref[part] = picked[part * depth : (part + 1) * depth, :].astype(BF)


def gather_call(rows, table, offset, depth):
    return pl.pallas_call(
        functools.partial(gather_kernel, offset),
        out_shape=jax.ShapeDtypeStruct((OWNERS, depth, EMB), BF),
        grid=(OWNERS // LISTS,),
        in_specs=[
            pl.BlockSpec((LISTS * CAP,), lambda i: (i,), memory_space=pltpu.SMEM),
            pl.BlockSpec((ROWS, EMB), lambda i: (0, 0)),
        ],
        out_specs=pl.BlockSpec((LISTS, depth, EMB), lambda i: (i, 0, 0)),
        scratch_shapes=[pltpu.VMEM((ROWS, EMB), F32), pltpu.VMEM((LISTS * depth, EMB), F32)],
        compiler_params=pltpu.CompilerParams(vmem_limit_bytes=VMEM),
        name="gather",
    )(rows, table)


def sums_of(packed_ref, got_ref, step, at):
    rows, masked = [], []
    depth = got_ref.shape[1]
    group = packed_ref[pl.ds(pl.multiple_of(step * POOLED, POOLED), POOLED), at : at + depth]
    for i in range(POOLED):
        packed = group[i : i + 1, :]
        bag = packed & (BAGS - 1)
        sample = jnp.where(packed > 0, bag >> 3, -1)
        rows.append(onehot(iota((SAMPLES, depth), 0) == sample))
        feature = jnp.broadcast_to((bag & (FEATS - 1)).astype(F32), (EMB, depth)).T.astype(BF)
        own = got_ref[i]
        masked.append(
            jnp.concatenate(
                [jnp.where(feature == f, own, jnp.zeros((), BF)) for f in range(FEATS)], axis=1
            )
        )
    return dot(jnp.concatenate(rows, axis=1), jnp.concatenate(masked, axis=0))


def pool_kernel(at, got_ref, packed_ref, out_ref):
    step = pl.program_id(0)
    sums = sums_of(packed_ref, got_ref, step, at)

    @pl.when(step == 0)
    def _():
        out_ref[...] = sums

    @pl.when(step > 0)
    def _():
        out_ref[...] += sums


def pool_call(got, packed, at):
    depth = got.shape[1]
    return pl.pallas_call(
        functools.partial(pool_kernel, at),
        out_shape=jax.ShapeDtypeStruct((SAMPLES, WIDTH), F32),
        grid=(OWNERS // POOLED,),
        in_specs=[
            pl.BlockSpec((POOLED, depth, EMB), lambda i: (i, 0, 0)),
            pl.BlockSpec((OWNERS, CAP), lambda i: (0, 0)),
        ],
        out_specs=pl.BlockSpec((SAMPLES, WIDTH), lambda i: (0, 0)),
        compiler_params=pltpu.CompilerParams(vmem_limit_bytes=VMEM),
        name="pool",
    )(got, packed)


def sigmoid(x):
    return 1.0 / (1.0 + jnp.exp(-x))


def tower_kernel(
    at,
    me_ref,
    got_ref,
    packed_ref,
    earlier_ref,
    labels_ref,
    gain_ref,
    cbias_ref,
    dbias_ref,
    out_w_ref,
    cross_hbm,
    deep_hbm,
    logits_ref,
    kept_ref,
    given_ref,
    *refs,
):
    grad_refs = refs[:REPS]
    pooled_ref, cross_w, deep_w, start_ref, cross_t, deep_t, deep_s, gx_ref, sems, result_ref = refs[
        REPS:
    ]
    step = pl.program_id(0)

    def cross_copy(layer):
        return pltpu.make_async_copy(cross_hbm.at[layer], cross_w.at[layer], sems.at[layer])

    def deep_copy(layer):
        return pltpu.make_async_copy(deep_hbm.at[layer], deep_w.at[layer], sems.at[3 + layer])

    @pl.when(step == 0)
    def _():
        for layer in range(3):
            cross_copy(layer).start()
        for layer in range(3):
            deep_copy(layer).start()
        pooled_ref[...] = earlier_ref[...]

    pooled_ref[...] += sums_of(packed_ref, got_ref, step, at)

    @pl.when(step == OWNERS // POOLED - 1)
    def _():
        gain = gain_ref[...]
        pooled = pooled_ref[...]
        inverse = lax.rsqrt(jnp.mean(pooled * pooled, axis=1, keepdims=True) + 1e-06)
        start = (pooled * inverse * gain).astype(BF)
        start_ref[...] = start
        current = start
        for layer in range(3):
            cross_copy(layer).wait()
            product = dot(current, cross_w[layer]) + cbias_ref[layer : layer + 1, :]
            cross_t[layer] = product
            current = (start_ref[...].astype(F32) * product + current.astype(F32)).astype(BF)
        for layer in range(3):
            deep_copy(layer).wait()
            product = dot(current, deep_w[layer]) + dbias_ref[layer : layer + 1, :]
            deep_t[layer] = product
            sig = sigmoid(product)
            deep_s[layer] = sig
            current = (product * sig).astype(BF)
        out_w = out_w_ref[...]
        logits = jnp.sum(current.astype(F32) * out_w, axis=1, keepdims=True)
        logits_ref[...] = logits
        error = sigmoid(logits) - labels_ref[...].astype(F32)
        grad = error * out_w
        for layer in (2, 1, 0):
            product = deep_t[layer]
            sig = deep_s[layer]
            masked = (grad * sig * (1.0 + product * (1.0 - sig))).astype(BF)
            grad = dot(masked, deep_w[layer], NT)
        gx_ref[...] = jnp.zeros_like(gx_ref)
        for layer in (2, 1, 0):
            crossed = (grad * start_ref[...].astype(F32)).astype(BF)
            gx_ref[...] += grad * cross_t[layer]
            grad = grad + dot(crossed, cross_w[layer], NT)
            if layer == 0:
                outer = dot(start_ref[...], crossed, TN).reshape(CHIPS, CORES, REPS, 8, WIDTH)
                for core in range(CORES):

                    @pl.when(me_ref[1] == core)
                    def _():
                        for r in range(REPS):
                            kept_ref[r] = outer[:, core, r].reshape(CHIPS * 8, WIDTH).astype(BF)
                            given_ref[r] = (
                                outer[:, 1 - core, r].reshape(CHIPS * 8, WIDTH).astype(BF)
                            )
        scaled = (gx_ref[...] + grad) * gain
        pooled = pooled_ref[...]
        inverse = lax.rsqrt(jnp.mean(pooled * pooled, axis=1, keepdims=True) + 1e-06)
        mean = jnp.mean(scaled * pooled, axis=1, keepdims=True)
        result = (inverse * scaled - pooled * (inverse * inverse * inverse) * mean).astype(BF)
        result_ref[...] = result
        for k in range(REPS):
            block = (me_ref[0] + k) & (REPS - 1)
            columns = pl.ds(pl.multiple_of(block * (PAIR * EMB), PAIR * EMB), PAIR * EMB)
            grad_refs[k][...] = result_ref[:, columns]


def tower_call(me, got, packed, earlier, labels, gain, cross, cbias, deep, dbias, out_w):
    def whole(shape):
        return pl.BlockSpec(shape, lambda i: (0,) * len(shape))

    return pl.pallas_call(
        functools.partial(tower_kernel, CAP - got.shape[1]),
        grid=(OWNERS // POOLED,),
        in_specs=[
            pl.BlockSpec(memory_space=pltpu.SMEM),
            pl.BlockSpec((POOLED, got.shape[1], EMB), lambda i: (i, 0, 0)),
            whole((OWNERS, CAP)),
            whole((SAMPLES, WIDTH)),
            whole((SAMPLES, 1)),
            whole((1, WIDTH)),
            whole((3, WIDTH)),
            whole((3, WIDTH)),
            whole((1, WIDTH)),
            pl.BlockSpec(memory_space=pl.ANY),
            pl.BlockSpec(memory_space=pl.ANY),
        ],
        out_specs=[
            whole((SAMPLES, 1)),
            whole((REPS, CHIPS * 8, WIDTH)),
            whole((REPS, CHIPS * 8, WIDTH)),
        ]
        + [whole((SAMPLES, PAIR * EMB))] * REPS,
        out_shape=[
            jax.ShapeDtypeStruct((SAMPLES, 1), F32),
            jax.ShapeDtypeStruct((REPS, CHIPS * 8, WIDTH), BF),
            jax.ShapeDtypeStruct((REPS, CHIPS * 8, WIDTH), BF),
        ]
        + [jax.ShapeDtypeStruct((SAMPLES, PAIR * EMB), BF)] * REPS,
        scratch_shapes=[
            pltpu.VMEM((SAMPLES, WIDTH), F32),
            pltpu.VMEM((3, WIDTH, WIDTH), BF),
            pltpu.VMEM((3, WIDTH, WIDTH), BF),
            pltpu.VMEM((SAMPLES, WIDTH), BF),
            pltpu.VMEM((3, SAMPLES, WIDTH), F32),
            pltpu.VMEM((3, SAMPLES, WIDTH), F32),
            pltpu.VMEM((3, SAMPLES, WIDTH), F32),
            pltpu.VMEM((SAMPLES, WIDTH), F32),
            pltpu.SemaphoreType.DMA((6,)),
            pltpu.VMEM((SAMPLES, WIDTH), BF),
        ],
        compiler_params=pltpu.CompilerParams(vmem_limit_bytes=VMEM),
        name="tower",
    )(me, got, packed, earlier, labels, gain, cbias, dbias, out_w, cross, deep)


def scatter_kernel(first_ref, trips_ref, word_ref, grads_ref, out_ref, wide, *accs):
    step = pl.program_id(0)

    @pl.when(step == 0)
    def _():
        for acc in accs:
            acc[...] = jnp.zeros_like(acc)

    group = grads_ref.shape[0]
    for g in range(group):
        for r in range(REPS):
            block = grads_ref[g, r]
            base = (g * REPS + r) * PAIR * SAMPLES
            for f in range(PAIR):
                wide[base + f * SAMPLES : base + (f + 1) * SAMPLES, :] = block[
                    :, f * EMB : (f + 1) * EMB
                ].astype(F32)

    def device(k, _):
        listed = step * group * REPS + k
        first = first_ref[listed]

        def some(i, _):
            at = first + i * ACCS
            words = [word_ref[at + j] for j in range(ACCS)]
            rows = [wide[pl.ds(word & (SOURCES - 1), 1), :] for word in words]
            olds = [accs[j][pl.ds(words[j] >> SHIFT, 1), :] for j in range(ACCS)]
            for j in range(ACCS):
                accs[j][pl.ds(words[j] >> SHIFT, 1), :] = olds[j] + rows[j]
            return 0

        lax.fori_loop(0, trips_ref[listed], some, 0)
        return 0

    lax.fori_loop(0, group * REPS, device, 0)

    @pl.when(step == pl.num_programs(0) - 1)
    def _():
        total = accs[0][: PAIR * VOC, :]
        for acc in accs[1:]:
            total = total + acc[: PAIR * VOC, :]
        out_ref[...] = total.astype(out_ref.dtype)


def scatter_call(words, first, trips, grads, group=GROUP):
    rows = PAIR * VOC
    return pl.pallas_call(
        scatter_kernel,
        out_shape=jax.ShapeDtypeStruct((rows, EMB), BF),
        grid_spec=pltpu.PrefetchScalarGridSpec(
            num_scalar_prefetch=2,
            grid=(OWNERS // group,),
            in_specs=[
                pl.BlockSpec(
                    (group * REPS * LISTED,), lambda i, *_: (i,), memory_space=pltpu.SMEM
                ),
                pl.BlockSpec(
                    (group, REPS, SAMPLES, PAIR * EMB), lambda i, *_: (i, 0, 0, 0)
                ),
            ],
            out_specs=pl.BlockSpec((rows, EMB), lambda i, *_: (0, 0)),
            scratch_shapes=[pltpu.VMEM((group * REPS * PAIR * SAMPLES, EMB), F32)]
            + [pltpu.VMEM((rows + 8, EMB), F32) for _ in range(ACCS)],
        ),
        compiler_params=pltpu.CompilerParams(vmem_limit_bytes=VMEM),
        name="scatter",
    )(first, trips, words, grads)


def finish_kernel(count, place_ref, *refs):
    blocks, (out, wide, sems) = refs[:count], refs[-3:]
    copies = []
    n = 0
    for block in blocks:
        for f in range(block.shape[0]):
            wide[n] = block[f].astype(F32)
            to = pl.multiple_of(place_ref[n] * VOC, VOC)
            copies.append(
                pltpu.make_async_copy(wide.at[n], out.at[pl.ds(to, VOC), :], sems.at[n])
            )
            copies[-1].start()
            n += 1
    for copy in copies:
        copy.wait()


def finish_call(places, blocks, earlier=None):
    more = [] if earlier is None else [earlier]
    total = sum(block.shape[0] for block in blocks)
    return pl.pallas_call(
        functools.partial(finish_kernel, len(blocks)),
        out_shape=jax.ShapeDtypeStruct((ROWS, EMB), F32),
        in_specs=[pl.BlockSpec(memory_space=pltpu.SMEM)]
        + [pl.BlockSpec(memory_space=pltpu.VMEM) for _ in blocks]
        + [pl.BlockSpec(memory_space=pl.ANY) for _ in more],
        out_specs=pl.BlockSpec(memory_space=pl.ANY),
        scratch_shapes=[
            pltpu.VMEM((total, VOC, EMB), F32),
            pltpu.SemaphoreType.DMA((total,)),
        ],
        input_output_aliases={1 + len(blocks): 0} if more else {},
        compiler_params=pltpu.CompilerParams(vmem_limit_bytes=16 * 1024 * 1024),
        name="finish",
    )(places, *blocks, *more)


def from_before(x, axis, k):
    if k == 0:
        return x
    n = lax.axis_size(axis)
    return lax.ppermute(x, axis, [(i, (i + k) % n) for i in range(n)])


def in_order(x, axis, me):
    n = lax.axis_size(axis)
    back = [from_before(x, axis, k) for k in range(n)]
    twice = jnp.concatenate([back[(n - 1 - i) % n] for i in range(2 * n - 1)])
    return lax.dynamic_slice_in_dim(twice, (n - 1 - me) * x.shape[0], n * x.shape[0])


def summed(x):
    return jnp.sum(x.astype(F32), axis=0).astype(BF)


def body(
    embed_table,
    row_ids,
    row_owner,
    lengths,
    feature_slot,
    labels,
    norm_gain,
    cross_weight,
    cross_bias,
    deep_weight,
    deep_bias,
    out_weight,
):
    packed, sent = index_call(
        row_ids,
        row_owner.reshape(1, IDS),
        lengths,
        feature_slot.T,
    )
    asked = lax.all_to_all(sent, "shard", split_axis=0, concat_axis=0, tiled=True)
    rows = ((asked >> 10) & (ROWS - 1)).reshape(-1)

    def exchange(x, axis):
        return lax.all_to_all(x, axis, split_axis=0, concat_axis=0, tiled=True)

    picked_early = gather_call(rows, embed_table, 0, EARLY)
    picked_early, lists = lax.optimization_barrier((picked_early, asked))
    got_early = exchange(picked_early, "shard")
    picked_late, lists = lax.optimization_barrier(
        (gather_call(rows, embed_table, EARLY, CAP - EARLY), lists)
    )
    got_late = exchange(picked_late, "shard")

    rep = lax.axis_index("rep")
    everyone = jnp.stack(
        [
            from_before(lists, "rep", k).reshape(OWNERS // GROUP, GROUP, CAP)
            for k in range(REPS)
        ],
        axis=2,
    )
    feature = everyone & (FEATS - 1)
    valid = everyone > 0
    within = feature - rep * PAIR
    ours = valid & (within >= 0) & (within < PAIR)
    target = jnp.where(ours, within * VOC + ((everyone >> 10) & (VOC - 1)), PAIR * VOC)
    group = lax.broadcasted_iota(I32, everyone.shape, 1)
    back = lax.broadcasted_iota(I32, everyone.shape, 2)
    source = (group * REPS + back) * (PAIR * SAMPLES) + jnp.where(
        ours, within * SAMPLES + ((everyone >> 3) & (SAMPLES - 1)), 0
    )
    words = jnp.pad(
        (target << SHIFT) | source,
        ((0, 0), (0, 0), (0, 0), (0, LISTED - CAP)),
        constant_values=(PAIR * VOC) << SHIFT,
    ).reshape(-1)
    below = jnp.sum((valid & (within < 0)).astype(I32), axis=3)
    upto = jnp.sum((valid & (within < PAIR)).astype(I32), axis=3)
    places = lax.broadcasted_iota(I32, below.shape, 1) * REPS + lax.broadcasted_iota(
        I32, below.shape, 2
    )
    first_word = (places * LISTED + below).reshape(-1)
    trips = ((upto - below + ACCS - 1) >> (ACCS.bit_length() - 1)).reshape(-1)
    sums_early = pool_call(got_early, packed, 0)
    slots = feature_slot[lax.axis_index("shard")]
    holder = (rep - jnp.array([0, 1, 3, 2], I32)) % REPS
    features = holder[:, None] * PAIR + jnp.arange(PAIR, dtype=I32)[None, :]
    places = slots[features.reshape(-1)]
    got_late, sums_early, words, first_word, trips, places = lax.optimization_barrier(
        (got_late, sums_early, words, first_word, trips, places)
    )

    logits, kept, given, *grads = tower_call(
        jnp.stack([rep, lax.axis_index("shard") % CORES]).astype(I32),
        got_late,
        packed,
        sums_early,
        labels.reshape(SAMPLES, 1),
        norm_gain.reshape(1, WIDTH),
        cross_weight,
        cross_bias,
        deep_weight,
        deep_bias,
        out_weight.reshape(1, WIDTH),
    )
    mine = jnp.stack([from_before(grads[k], "rep", k) for k in range(REPS)])
    mine, kept, given = lax.optimization_barrier((mine, kept, given))
    all_grads = lax.all_gather(mine, "shard", axis=0)
    other = lax.ppermute(given, "shard", [(i, i ^ 1) for i in range(OWNERS)])
    half = (kept.astype(F32) + other.astype(F32)).astype(BF)
    quarter = summed(exchange(half, "rep"))
    eight = summed(
        lax.all_to_all(
            quarter.reshape(CHIPS, 8, WIDTH),
            "shard",
            split_axis=0,
            concat_axis=0,
            axis_index_groups=[list(range(c, OWNERS, CORES)) for c in range(CORES)],
            tiled=True,
        )
    )
    first_grad = lax.all_gather(
        in_order(eight, "rep", rep), "shard", axis=0, tiled=True
    ).astype(F32)

    part = scatter_call(words, first_word, trips, all_grads).reshape(PAIR, VOC, EMB)
    before = from_before(part, "rep", 1)
    after = from_before(part, "rep", REPS - 1)
    across = [
        from_before(before[:1], "rep", 1),
        from_before(after[1:], "rep", REPS - 1),
    ]
    near, far = places[: 3 * PAIR], places[3 * PAIR :]
    row_grad = finish_call(near, [part, before, after])
    row_grad = finish_call(far, across, row_grad)
    return (row_grad, first_grad, logits.reshape(SAMPLES))


def solution(mesh):
    both = ("rep", "shard")
    in_specs = (
        P("shard", None),
        P(both, None),
        P(both, None, None),
        P(both, None),
        P(),
        P(both),
        P(),
        P(),
        P(),
        P(),
        P(),
        P(),
    )
    out_specs = (P("shard", None), P(), P(both))
    return jax.shard_map(body, mesh=mesh, in_specs=in_specs, out_specs=out_specs, check_vma=False)
```

```python
import functools

import jax
import jax.numpy as jnp
import numpy as np
from jax import lax
from jax.experimental import pallas as pl
from jax.experimental.pallas import tpu as pltpu
from jax.sharding import PartitionSpec as P

BF = jnp.bfloat16
F32 = jnp.float32
I32 = jnp.int32
OWNERS = 32
FEATS = 8
KEYS = OWNERS * FEATS
CAP = 512
VOC = 1024
ROWS = FEATS * VOC
EMB = 128
BAGS = 1024
SAMPLES = 128
WIDTH = FEATS * EMB
IDS = 8192
REPS = 4
CORES = 2
CHIPS = OWNERS // CORES
PAIR = FEATS // REPS
LANES = 256
IDROWS = IDS // LANES
ACCS = 16
POOLED = 16
GROUP = 4
LISTED = CAP + 64
LISTS = 16
SOURCES = GROUP * REPS * PAIR * SAMPLES
SHIFT = 13
EARLY = 128
VMEM = 62 * 1024 * 1024

NT = (((1,), (1,)), ((), ()))
TN = (((0,), (0,)), ((), ()))


def dot(a, b, dims=(((1,), (0,)), ((), ()))):
    return lax.dot_general(a, b, dims, preferred_element_type=F32)


def iota(shape, dim):
    return lax.broadcasted_iota(I32, shape, dim)


def onehot(cond):
    return jnp.where(cond, 1.0, 0.0).astype(BF)


def index_kernel(
    ids_in, owner_in, len_in, slot_ref, out_ref, send_ref, ids_ref, owner_ref, len_ref, bag_ref, key_ref
):
    for r in range(IDROWS):
        ids_ref[r : r + 1, :] = ids_in[:, r * LANES : (r + 1) * LANES]
        owner_ref[r : r + 1, :] = owner_in[:, r * LANES : (r + 1) * LANES]
    for r in range(BAGS // 128):
        len_ref[r : r + 1, :] = len_in[:, r * 128 : (r + 1) * 128]
    lens = len_ref[...].astype(F32).astype(BF)
    incl128 = onehot(iota((128, 128), 0) <= iota((128, 128), 1))
    within = dot(lens, incl128)
    total = jnp.broadcast_to(within[:, 127:128], (8, 128))
    high = jnp.floor(total * (1.0 / 256.0))
    low = total - high * 256.0
    below8 = onehot(iota((8, 8), 1) < iota((8, 8), 0))
    before = dot(below8, high.astype(BF)) * 256.0 + dot(below8, low.astype(BF))
    start = (within + before).astype(I32) - len_ref[...]
    start_hi = start >> 8
    start_lo = start & 255
    marks = jnp.zeros((IDROWS, LANES), F32)
    for r in range(8):
        a = onehot(iota((IDROWS, 128), 0) == start_hi[r : r + 1, :])
        b = onehot(iota((LANES, 128), 0) == start_lo[r : r + 1, :])
        marks = marks + dot(a, b, NT)
    marks = marks.astype(BF)
    incl = onehot(iota((LANES, LANES), 0) <= iota((LANES, LANES), 1))
    strict = onehot(iota((LANES, LANES), 0) < iota((LANES, LANES), 1))
    row_counts = dot(marks, jnp.ones((LANES, LANES), BF))
    below = onehot(iota((IDROWS, IDROWS), 1) < iota((IDROWS, IDROWS), 0))
    bag = (dot(marks, incl) + dot(below, row_counts.astype(BF))).astype(I32) - 1
    bag_ref[...] = bag
    key_ref[...] = owner_ref[...] * FEATS + (bag & (FEATS - 1))

    key_iota = iota((KEYS, LANES), 0)

    def count(r, acc):
        return acc + jnp.where(key_iota == key_ref[pl.ds(r, 1), :], 1.0, 0.0)

    counts = lax.fori_loop(0, IDROWS, count, jnp.zeros((KEYS, LANES), F32), unroll=4)
    totals = dot(counts.astype(BF), jnp.ones((LANES, LANES), BF))
    high = jnp.floor(totals * (1.0 / 256.0))
    low = totals - high * 256.0
    ki, kj = iota((KEYS, KEYS), 0), iota((KEYS, KEYS), 1)
    earlier = onehot((ki // FEATS == kj // FEATS) & (kj < ki))
    carry0 = dot(earlier, high.astype(BF)) * 256.0 + dot(earlier, low.astype(BF))

    rank_iota = iota((CAP // 2, LANES), 0)
    owner_iota = iota((OWNERS, LANES), 0)

    of_owner = onehot(iota((KEYS, OWNERS), 0) // FEATS == iota((KEYS, OWNERS), 1))
    by_owner = dot(of_owner, slot_ref[...].astype(F32).astype(BF), NT)
    is_feature = (iota((KEYS, FEATS), 0) & (FEATS - 1)) == iota((KEYS, FEATS), 1)
    slots = jnp.sum(jnp.where(is_feature, by_owner, 0.0), axis=1, keepdims=True)
    carry0 = carry0 + jnp.broadcast_to(slots, (KEYS, LANES)) * VOC

    def place(r, state):
        carry, acc = state
        same = key_iota == key_ref[pl.ds(r, 1), :]
        hot = jnp.where(same, 1.0, 0.0)
        prefix = dot(hot.astype(BF), strict)
        found = jnp.sum(jnp.where(same, prefix + carry, 0.0), axis=0, keepdims=True)
        found = found.astype(I32)
        rank = found & (VOC - 1)
        row = (found - rank) + ids_ref[pl.ds(r, 1), :]
        value = (1 << 23) + (row << 10) + bag_ref[pl.ds(r, 1), :]
        mine = owner_iota == owner_ref[pl.ds(r, 1), :]
        pieces = [
            jnp.where(mine, jnp.broadcast_to(p.astype(F32), (OWNERS, LANES)), 0.0)
            for p in (value & 255, (value >> 8) & 255, value >> 16)
        ]
        left = jnp.concatenate(pieces, axis=0).astype(BF)
        upper = rank >= CAP // 2
        left = jnp.concatenate([left * onehot(~upper), left * onehot(upper)], axis=0)
        right = onehot(rank_iota == (rank & (CAP // 2 - 1)))
        acc = acc + dot(left, right, NT)
        carry = carry + (prefix + hot)[:, LANES - 1 : LANES]
        return carry, acc

    _, acc = lax.fori_loop(
        0, IDROWS, place, (carry0, jnp.zeros((6 * OWNERS, CAP // 2), F32)), unroll=IDROWS
    )
    acc = jnp.concatenate([acc[: 3 * OWNERS], acc[3 * OWNERS :]], axis=1).astype(I32)
    packed = acc[:OWNERS] + (acc[OWNERS : 2 * OWNERS] << 8) + (acc[2 * OWNERS :] << 16)
    out_ref[...] = packed
    for c in range(CAP // 128):
        send_ref[:, c, :] = packed[:, c * 128 : (c + 1) * 128]


def index_call(ids, owners, lengths, slots):
    return pl.pallas_call(
        index_kernel,
        out_shape=[
            jax.ShapeDtypeStruct((OWNERS, CAP), I32),
            jax.ShapeDtypeStruct((OWNERS, CAP // 128, 128), I32),
        ],
        scratch_shapes=[
            pltpu.VMEM((IDROWS, LANES), I32),
            pltpu.VMEM((IDROWS, LANES), I32),
            pltpu.VMEM((BAGS // 128, 128), I32),
            pltpu.VMEM((IDROWS, LANES), I32),
            pltpu.VMEM((IDROWS, LANES), I32),
        ],
        compiler_params=pltpu.CompilerParams(vmem_limit_bytes=VMEM),
        name="index",
    )(ids, owners, lengths, slots)


def gather_kernel(offset, row_ref, table_ref, out_ref, wide, picked):
    step = pl.program_id(0)
    depth = out_ref.shape[1]

    @pl.when(step == 0)
    def _():
        wide[...] = table_ref[...].astype(F32)

    for part in range(LISTS):
        base = part * CAP + offset

        def some(i, _):
            at = i * 32
            rows = [wide[pl.ds(row_ref[base + at + j], 1), :] for j in range(32)]
            for j in range(32):
                picked[pl.ds(part * depth + at + j, 1), :] = rows[j]
            return 0

        lax.fori_loop(0, depth // 32, some, 0)
        out_ref[part] = picked[part * depth : (part + 1) * depth, :].astype(BF)


def gather_call(rows, table, offset, depth):
    return pl.pallas_call(
        functools.partial(gather_kernel, offset),
        out_shape=jax.ShapeDtypeStruct((OWNERS, depth, EMB), BF),
        grid=(OWNERS // LISTS,),
        in_specs=[
            pl.BlockSpec((LISTS * CAP,), lambda i: (i,), memory_space=pltpu.SMEM),
            pl.BlockSpec((ROWS, EMB), lambda i: (0, 0)),
        ],
        out_specs=pl.BlockSpec((LISTS, depth, EMB), lambda i: (i, 0, 0)),
        scratch_shapes=[pltpu.VMEM((ROWS, EMB), F32), pltpu.VMEM((LISTS * depth, EMB), F32)],
        compiler_params=pltpu.CompilerParams(vmem_limit_bytes=VMEM),
        name="gather",
    )(rows, table)


def sums_of(packed_ref, got_ref, step, at):
    rows, masked = [], []
    depth = got_ref.shape[1]
    group = packed_ref[pl.ds(pl.multiple_of(step * POOLED, POOLED), POOLED), at : at + depth]
    for i in range(POOLED):
        packed = group[i : i + 1, :]
        bag = packed & (BAGS - 1)
        sample = jnp.where(packed > 0, bag >> 3, -1)
        rows.append(onehot(iota((SAMPLES, depth), 0) == sample))
        feature = jnp.broadcast_to((bag & (FEATS - 1)).astype(F32), (EMB, depth)).T.astype(BF)
        own = got_ref[i]
        masked.append(
            jnp.concatenate(
                [jnp.where(feature == f, own, jnp.zeros((), BF)) for f in range(FEATS)], axis=1
            )
        )
    return dot(jnp.concatenate(rows, axis=1), jnp.concatenate(masked, axis=0))


def pool_kernel(at, got_ref, packed_ref, out_ref):
    step = pl.program_id(0)
    sums = sums_of(packed_ref, got_ref, step, at)

    @pl.when(step == 0)
    def _():
        out_ref[...] = sums

    @pl.when(step > 0)
    def _():
        out_ref[...] += sums


def pool_call(got, packed, at):
    depth = got.shape[1]
    return pl.pallas_call(
        functools.partial(pool_kernel, at),
        out_shape=jax.ShapeDtypeStruct((SAMPLES, WIDTH), F32),
        grid=(OWNERS // POOLED,),
        in_specs=[
            pl.BlockSpec((POOLED, depth, EMB), lambda i: (i, 0, 0)),
            pl.BlockSpec((OWNERS, CAP), lambda i: (0, 0)),
        ],
        out_specs=pl.BlockSpec((SAMPLES, WIDTH), lambda i: (0, 0)),
        compiler_params=pltpu.CompilerParams(vmem_limit_bytes=VMEM),
        name="pool",
    )(got, packed)


def sigmoid(x):
    return 1.0 / (1.0 + jnp.exp(-x))


def tower_kernel(
    at,
    me_ref,
    got_ref,
    packed_ref,
    earlier_ref,
    labels_ref,
    gain_ref,
    cbias_ref,
    dbias_ref,
    out_w_ref,
    cross_hbm,
    deep_hbm,
    logits_ref,
    kept_ref,
    given_ref,
    *refs,
):
    grad_refs = refs[:REPS]
    pooled_ref, cross_w, deep_w, start_ref, cross_t, deep_t, deep_s, gx_ref, sems, result_ref = refs[
        REPS:
    ]
    step = pl.program_id(0)

    def cross_copy(layer):
        return pltpu.make_async_copy(cross_hbm.at[layer], cross_w.at[layer], sems.at[layer])

    def deep_copy(layer):
        return pltpu.make_async_copy(deep_hbm.at[layer], deep_w.at[layer], sems.at[3 + layer])

    @pl.when(step == 0)
    def _():
        for layer in range(3):
            cross_copy(layer).start()
        for layer in range(3):
            deep_copy(layer).start()
        pooled_ref[...] = earlier_ref[...]

    pooled_ref[...] += sums_of(packed_ref, got_ref, step, at)

    @pl.when(step == OWNERS // POOLED - 1)
    def _():
        gain = gain_ref[...]
        pooled = pooled_ref[...]
        inverse = lax.rsqrt(jnp.mean(pooled * pooled, axis=1, keepdims=True) + 1e-06)
        start = (pooled * inverse * gain).astype(BF)
        start_ref[...] = start
        current = start
        for layer in range(3):
            cross_copy(layer).wait()
            product = dot(current, cross_w[layer]) + cbias_ref[layer : layer + 1, :]
            cross_t[layer] = product
            current = (start_ref[...].astype(F32) * product + current.astype(F32)).astype(BF)
        for layer in range(3):
            deep_copy(layer).wait()
            product = dot(current, deep_w[layer]) + dbias_ref[layer : layer + 1, :]
            deep_t[layer] = product
            sig = sigmoid(product)
            deep_s[layer] = sig
            current = (product * sig).astype(BF)
        out_w = out_w_ref[...]
        logits = jnp.sum(current.astype(F32) * out_w, axis=1, keepdims=True)
        logits_ref[...] = logits
        error = sigmoid(logits) - labels_ref[...].astype(F32)
        grad = error * out_w
        for layer in (2, 1, 0):
            product = deep_t[layer]
            sig = deep_s[layer]
            masked = (grad * sig * (1.0 + product * (1.0 - sig))).astype(BF)
            grad = dot(masked, deep_w[layer], NT)
        gx_ref[...] = jnp.zeros_like(gx_ref)
        for layer in (2, 1, 0):
            crossed = (grad * start_ref[...].astype(F32)).astype(BF)
            gx_ref[...] += grad * cross_t[layer]
            grad = grad + dot(crossed, cross_w[layer], NT)
            if layer == 0:
                outer = dot(start_ref[...], crossed, TN).reshape(CHIPS, CORES, REPS, 8, WIDTH)
                for core in range(CORES):

                    @pl.when(me_ref[1] == core)
                    def _():
                        for r in range(REPS):
                            kept_ref[r] = outer[:, core, r].reshape(CHIPS * 8, WIDTH).astype(BF)
                            given_ref[r] = (
                                outer[:, 1 - core, r].reshape(CHIPS * 8, WIDTH).astype(BF)
                            )
        scaled = (gx_ref[...] + grad) * gain
        pooled = pooled_ref[...]
        inverse = lax.rsqrt(jnp.mean(pooled * pooled, axis=1, keepdims=True) + 1e-06)
        mean = jnp.mean(scaled * pooled, axis=1, keepdims=True)
        result = (inverse * scaled - pooled * (inverse * inverse * inverse) * mean).astype(BF)
        result_ref[...] = result
        for k in range(REPS):
            block = (me_ref[0] + k) & (REPS - 1)
            columns = pl.ds(pl.multiple_of(block * (PAIR * EMB), PAIR * EMB), PAIR * EMB)
            grad_refs[k][...] = result_ref[:, columns]


def tower_call(me, got, packed, earlier, labels, gain, cross, cbias, deep, dbias, out_w):
    def whole(shape):
        return pl.BlockSpec(shape, lambda i: (0,) * len(shape))

    return pl.pallas_call(
        functools.partial(tower_kernel, CAP - got.shape[1]),
        grid=(OWNERS // POOLED,),
        in_specs=[
            pl.BlockSpec(memory_space=pltpu.SMEM),
            pl.BlockSpec((POOLED, got.shape[1], EMB), lambda i: (i, 0, 0)),
            whole((OWNERS, CAP)),
            whole((SAMPLES, WIDTH)),
            whole((SAMPLES, 1)),
            whole((1, WIDTH)),
            whole((3, WIDTH)),
            whole((3, WIDTH)),
            whole((1, WIDTH)),
            pl.BlockSpec(memory_space=pl.ANY),
            pl.BlockSpec(memory_space=pl.ANY),
        ],
        out_specs=[
            whole((SAMPLES, 1)),
            whole((REPS, CHIPS * 8, WIDTH)),
            whole((REPS, CHIPS * 8, WIDTH)),
        ]
        + [whole((SAMPLES, PAIR * EMB))] * REPS,
        out_shape=[
            jax.ShapeDtypeStruct((SAMPLES, 1), F32),
            jax.ShapeDtypeStruct((REPS, CHIPS * 8, WIDTH), BF),
            jax.ShapeDtypeStruct((REPS, CHIPS * 8, WIDTH), BF),
        ]
        + [jax.ShapeDtypeStruct((SAMPLES, PAIR * EMB), BF)] * REPS,
        scratch_shapes=[
            pltpu.VMEM((SAMPLES, WIDTH), F32),
            pltpu.VMEM((3, WIDTH, WIDTH), BF),
            pltpu.VMEM((3, WIDTH, WIDTH), BF),
            pltpu.VMEM((SAMPLES, WIDTH), BF),
            pltpu.VMEM((3, SAMPLES, WIDTH), F32),
            pltpu.VMEM((3, SAMPLES, WIDTH), F32),
            pltpu.VMEM((3, SAMPLES, WIDTH), F32),
            pltpu.VMEM((SAMPLES, WIDTH), F32),
            pltpu.SemaphoreType.DMA((6,)),
            pltpu.VMEM((SAMPLES, WIDTH), BF),
        ],
        compiler_params=pltpu.CompilerParams(vmem_limit_bytes=VMEM),
        name="tower",
    )(me, got, packed, earlier, labels, gain, cbias, dbias, out_w, cross, deep)


def scatter_kernel(first_ref, trips_ref, word_ref, grads_ref, out_ref, wide, *accs):
    step = pl.program_id(0)

    @pl.when(step == 0)
    def _():
        for acc in accs:
            acc[...] = jnp.zeros_like(acc)

    group = grads_ref.shape[0]
    for g in range(group):
        for r in range(REPS):
            block = grads_ref[g, r]
            base = (g * REPS + r) * PAIR * SAMPLES
            for f in range(PAIR):
                wide[base + f * SAMPLES : base + (f + 1) * SAMPLES, :] = block[
                    :, f * EMB : (f + 1) * EMB
                ].astype(F32)

    def device(k, _):
        listed = step * group * REPS + k
        first = first_ref[listed]

        def some(i, _):
            at = first + i * ACCS
            words = [word_ref[at + j] for j in range(ACCS)]
            rows = [wide[pl.ds(word & (SOURCES - 1), 1), :] for word in words]
            olds = [accs[j][pl.ds(words[j] >> SHIFT, 1), :] for j in range(ACCS)]
            for j in range(ACCS):
                accs[j][pl.ds(words[j] >> SHIFT, 1), :] = olds[j] + rows[j]
            return 0

        lax.fori_loop(0, trips_ref[listed], some, 0)
        return 0

    lax.fori_loop(0, group * REPS, device, 0)

    @pl.when(step == pl.num_programs(0) - 1)
    def _():
        total = accs[0][: PAIR * VOC, :]
        for acc in accs[1:]:
            total = total + acc[: PAIR * VOC, :]
        out_ref[...] = total.astype(out_ref.dtype)


def scatter_call(words, first, trips, grads, group=GROUP):
    rows = PAIR * VOC
    return pl.pallas_call(
        scatter_kernel,
        out_shape=jax.ShapeDtypeStruct((rows, EMB), BF),
        grid_spec=pltpu.PrefetchScalarGridSpec(
            num_scalar_prefetch=2,
            grid=(OWNERS // group,),
            in_specs=[
                pl.BlockSpec(
                    (group * REPS * LISTED,), lambda i, *_: (i,), memory_space=pltpu.SMEM
                ),
                pl.BlockSpec(
                    (group, REPS, SAMPLES, PAIR * EMB), lambda i, *_: (i, 0, 0, 0)
                ),
            ],
            out_specs=pl.BlockSpec((rows, EMB), lambda i, *_: (0, 0)),
            scratch_shapes=[pltpu.VMEM((group * REPS * PAIR * SAMPLES, EMB), F32)]
            + [pltpu.VMEM((rows + 8, EMB), F32) for _ in range(ACCS)],
        ),
        compiler_params=pltpu.CompilerParams(vmem_limit_bytes=VMEM),
        name="scatter",
    )(first, trips, words, grads)


def finish_kernel(count, place_ref, *refs):
    blocks, (out, wide, sems) = refs[:count], refs[-3:]
    copies = []
    n = 0
    for block in blocks:
        for f in range(block.shape[0]):
            wide[n] = block[f].astype(F32)
            to = pl.multiple_of(place_ref[n] * VOC, VOC)
            copies.append(
                pltpu.make_async_copy(wide.at[n], out.at[pl.ds(to, VOC), :], sems.at[n])
            )
            copies[-1].start()
            n += 1
    for copy in copies:
        copy.wait()


def finish_call(places, blocks, earlier=None):
    more = [] if earlier is None else [earlier]
    total = sum(block.shape[0] for block in blocks)
    return pl.pallas_call(
        functools.partial(finish_kernel, len(blocks)),
        out_shape=jax.ShapeDtypeStruct((ROWS, EMB), F32),
        in_specs=[pl.BlockSpec(memory_space=pltpu.SMEM)]
        + [pl.BlockSpec(memory_space=pltpu.VMEM) for _ in blocks]
        + [pl.BlockSpec(memory_space=pl.ANY) for _ in more],
        out_specs=pl.BlockSpec(memory_space=pl.ANY),
        scratch_shapes=[
            pltpu.VMEM((total, VOC, EMB), F32),
            pltpu.SemaphoreType.DMA((total,)),
        ],
        input_output_aliases={1 + len(blocks): 0} if more else {},
        compiler_params=pltpu.CompilerParams(vmem_limit_bytes=16 * 1024 * 1024),
        name="finish",
    )(places, *blocks, *more)


def join_kernel(*refs):
    blocks, (out, sems) = refs[:-2], refs[-2:]
    copies = [
        pltpu.make_async_copy(block, out.at[k], sems.at[k]) for k, block in enumerate(blocks)
    ]
    for copy in copies:
        copy.start()
    for copy in copies:
        copy.wait()


def join_call(blocks):
    return pl.pallas_call(
        join_kernel,
        out_shape=jax.ShapeDtypeStruct((len(blocks),) + blocks[0].shape, blocks[0].dtype),
        in_specs=[pl.BlockSpec(memory_space=pl.ANY) for _ in blocks],
        out_specs=pl.BlockSpec(memory_space=pl.ANY),
        scratch_shapes=[pltpu.SemaphoreType.DMA((len(blocks),))],
        compiler_params=pltpu.CompilerParams(vmem_limit_bytes=VMEM),
        name="join",
    )(*blocks)


def from_before(x, axis, k):
    if k == 0:
        return x
    n = lax.axis_size(axis)
    return lax.ppermute(x, axis, [(i, (i + k) % n) for i in range(n)])


def in_order(x, axis, me):
    n = lax.axis_size(axis)
    back = [from_before(x, axis, k) for k in range(n)]
    twice = jnp.concatenate([back[(n - 1 - i) % n] for i in range(2 * n - 1)])
    return lax.dynamic_slice_in_dim(twice, (n - 1 - me) * x.shape[0], n * x.shape[0])


def summed(x):
    return jnp.sum(x.astype(F32), axis=0).astype(BF)


def body(
    embed_table,
    row_ids,
    row_owner,
    lengths,
    feature_slot,
    labels,
    norm_gain,
    cross_weight,
    cross_bias,
    deep_weight,
    deep_bias,
    out_weight,
):
    packed, sent = index_call(
        row_ids,
        row_owner.reshape(1, IDS),
        lengths,
        feature_slot.T,
    )
    asked = lax.all_to_all(sent, "shard", split_axis=0, concat_axis=0, tiled=True)
    rows = ((asked >> 10) & (ROWS - 1)).reshape(-1)

    def exchange(x, axis):
        return lax.all_to_all(x, axis, split_axis=0, concat_axis=0, tiled=True)

    picked_early = gather_call(rows, embed_table, 0, EARLY)
    picked_early, lists = lax.optimization_barrier((picked_early, asked))
    got_early = exchange(picked_early, "shard")
    picked_late, lists = lax.optimization_barrier(
        (gather_call(rows, embed_table, EARLY, CAP - EARLY), lists)
    )
    got_late = exchange(picked_late, "shard")

    rep = lax.axis_index("rep")
    everyone = jnp.stack(
        [
            from_before(lists, "rep", k).reshape(OWNERS // GROUP, GROUP, CAP)
            for k in range(REPS)
        ],
        axis=2,
    )
    feature = everyone & (FEATS - 1)
    valid = everyone > 0
    within = feature - rep * PAIR
    ours = valid & (within >= 0) & (within < PAIR)
    target = jnp.where(ours, within * VOC + ((everyone >> 10) & (VOC - 1)), PAIR * VOC)
    group = lax.broadcasted_iota(I32, everyone.shape, 1)
    back = lax.broadcasted_iota(I32, everyone.shape, 2)
    source = (group * REPS + back) * (PAIR * SAMPLES) + jnp.where(
        ours, within * SAMPLES + ((everyone >> 3) & (SAMPLES - 1)), 0
    )
    words = jnp.pad(
        (target << SHIFT) | source,
        ((0, 0), (0, 0), (0, 0), (0, LISTED - CAP)),
        constant_values=(PAIR * VOC) << SHIFT,
    ).reshape(-1)
    below = jnp.sum((valid & (within < 0)).astype(I32), axis=3)
    upto = jnp.sum((valid & (within < PAIR)).astype(I32), axis=3)
    places = lax.broadcasted_iota(I32, below.shape, 1) * REPS + lax.broadcasted_iota(
        I32, below.shape, 2
    )
    first_word = (places * LISTED + below).reshape(-1)
    trips = ((upto - below + ACCS - 1) >> (ACCS.bit_length() - 1)).reshape(-1)
    sums_early = pool_call(got_early, packed, 0)
    slots = feature_slot[lax.axis_index("shard")]
    holder = (rep - jnp.array([0, 1, 3, 2], I32)) % REPS
    features = holder[:, None] * PAIR + jnp.arange(PAIR, dtype=I32)[None, :]
    places = slots[features.reshape(-1)]
    got_late, sums_early, words, first_word, trips, places = lax.optimization_barrier(
        (got_late, sums_early, words, first_word, trips, places)
    )

    logits, kept, given, *grads = tower_call(
        jnp.stack([rep, lax.axis_index("shard") % CORES]).astype(I32),
        got_late,
        packed,
        sums_early,
        labels.reshape(SAMPLES, 1),
        norm_gain.reshape(1, WIDTH),
        cross_weight,
        cross_bias,
        deep_weight,
        deep_bias,
        out_weight.reshape(1, WIDTH),
    )
    mine = join_call([from_before(grads[k], "rep", k) for k in range(REPS)])
    mine, kept, given = lax.optimization_barrier((mine, kept, given))
    all_grads = lax.all_gather(mine, "shard", axis=0)
    all_grads, logits = lax.optimization_barrier((all_grads, logits.reshape(SAMPLES)))
    other = lax.ppermute(given, "shard", [(i, i ^ 1) for i in range(OWNERS)])
    half = (kept.astype(F32) + other.astype(F32)).astype(BF)
    quarter = summed(exchange(half, "rep"))
    eight = summed(
        lax.all_to_all(
            quarter.reshape(CHIPS, 8, WIDTH),
            "shard",
            split_axis=0,
            concat_axis=0,
            axis_index_groups=[list(range(c, OWNERS, CORES)) for c in range(CORES)],
            tiled=True,
        )
    )
    first_grad = lax.all_gather(
        in_order(eight, "rep", rep), "shard", axis=0, tiled=True
    ).astype(F32)

    part = scatter_call(words, first_word, trips, all_grads).reshape(PAIR, VOC, EMB)
    before = from_before(part, "rep", 1)
    after = from_before(part, "rep", REPS - 1)
    across = [
        from_before(before[:1], "rep", 1),
        from_before(after[1:], "rep", REPS - 1),
    ]
    near, far = places[: 3 * PAIR], places[3 * PAIR :]
    row_grad = finish_call(near, [part, before, after])
    row_grad = finish_call(far, across, row_grad)
    return (row_grad, first_grad, logits)


def solution(mesh):
    both = ("rep", "shard")
    in_specs = (
        P("shard", None),
        P(both, None),
        P(both, None, None),
        P(both, None),
        P(),
        P(both),
        P(),
        P(),
        P(),
        P(),
        P(),
        P(),
    )
    out_specs = (P("shard", None), P(), P(both))
    return jax.shard_map(body, mesh=mesh, in_specs=in_specs, out_specs=out_specs, check_vma=False)
```
